128 devices in a mesh: layer: 4 (over y), strip: 32 (over x, z, core).
Axes of the slice: x: 4, y: 4, z: 4, core: 2. Of those that a mesh axis runs over, the one named last changes fastest.
Arguments:
- launch: bfloat16 [2, 2, 1024, 1024], P(None, None, 'strip'), may hold values from -6 to 6
- screens: float32 [4, 1024, 1024], P('layer', 'strip'), may hold values from -3.140625 to 3.140625
- distance: float32 [4], P('layer'), may hold values from 1024 to 2048
- templates: bfloat16 [1024, 16], replicated, may hold values from -0.1875 to 0.1875
- send_table: int32 [32, 32, 4], P('strip', None, 'layer'), may hold values from 0 to 127, as said below
- send_counts: int32 [32, 32], P('strip'), may hold values from 0 to 4, as said below
Outputs:
- pupil: bfloat16 [2, 2, 1024, 1024], P(None, None, 'strip')
- correlation: float32 [32, 32, 4, 2, 16], P('strip', None, 'layer')
The draws below stay inside these ranges and needn't reach their ends.
Inputs may be any that keep to these rules, and one draw needn't show every extreme that they name: For each source strip s the 32 x 4 entries send_table[s] are distinct subaperture numbers local to that strip (row by row over its 128 subapertures). `send_counts`: some owner receives 4 live slots from every source.
All inputs are finite; a program needn't handle non-finite values.
Results may differ from the reference program's by a relative error of at most 0.03.
Values may be sent and summed in bfloat16 or wider, within the bound.
No kernel may reach another device: no remote copies, remote signals or barrier semaphores. Data moves between devices by JAX's collectives and lax.ppermute only.
A program may use at most 64 MiB of HBM per device.

```python
import math
import jax
import jax.numpy as jnp
from jax import lax

N = 1024
SUB = 16
CHANNELS = 16
FIELDS = 2
CAP = 4
LAYERS = 4
SIDE = 64
SUBS_DEV = 128
PIX = 1024
N_STRIP = 32


def routing_tables(key):
    base = jax.random.fold_in(key, 4177)
    order_key, count_key, owner_key = jax.random.split(base, 3)

    def shuffled(single_key):
        return jax.random.permutation(single_key, SUBS_DEV)
    orders = jax.vmap(shuffled)(jax.random.split(order_key, N_STRIP))
    table = orders[:, :N_STRIP * CAP].reshape(N_STRIP, N_STRIP, CAP).astype(jnp.int32)
    counts = jax.random.randint(count_key, (N_STRIP, N_STRIP), 0, CAP + 1, dtype=jnp.int32)
    busiest = jax.random.randint(owner_key, (), 0, N_STRIP, dtype=jnp.int32)
    counts = jnp.where(jnp.arange(N_STRIP, dtype=jnp.int32)[None, :] == busiest, CAP, counts)
    return (table, counts.astype(jnp.int32))


def draw_send_table(key, part):
    return routing_tables(key)[0]


def draw_send_counts(key, part):
    return routing_tables(key)[1]


def levels(rng, extent, shards, smallest, largest):
    def one(dim, parts):
        draws = jax.random.uniform(jax.random.fold_in(jax.random.fold_in(rng, 6), dim), (parts,), jnp.float32, smallest / len(shards), largest / len(shards))
        return jnp.repeat(jnp.exp(draws), extent[dim] // parts).reshape((-1,) + (1,) * (len(extent) - dim - 1))

    level = one(*shards[0])
    for cut in shards[1:]:
        level = level * one(*cut)
    return level


def bell_draw(rng, shape, spread, reach, shards=(), kind=jnp.bfloat16):
    loudness = levels(rng, shape, shards, -0.22, 0.18) if shards else 1.0
    entries = jax.random.normal(rng, shape, jnp.float32) * spread * loudness
    return jnp.minimum(jnp.maximum(entries, -reach), reach).astype(kind)


def setup_inputs(seed: int = 0) -> dict:
    arg_keys = jax.random.split(jax.random.key(seed), 7)
    return {
        "launch": bell_draw(arg_keys[0], (FIELDS, 2, N, N), 1.0, 6.0, ((2, 32),)),
        "screens": jnp.clip(jax.random.uniform(arg_keys[1], (LAYERS, N, N), jnp.float32, -3.140625, 3.140625), -3.140625, 3.140625),
        "distance": jnp.clip(jnp.exp(math.log(2048.0) - 0.6931472 * jax.random.uniform(arg_keys[2], (LAYERS,), jnp.float32) ** levels(arg_keys[2], (LAYERS,), ((0, 4),), -0.2, 0.2)), 1024.0, 2048.0),
        "templates": bell_draw(arg_keys[3], (PIX, CHANNELS), PIX ** -0.5, 0.1875),
        "send_table": draw_send_table(jax.random.fold_in(arg_keys[6], 71), 0),
        "send_counts": draw_send_counts(jax.random.fold_in(arg_keys[6], 71), 0),
    }


def fourier_tables(length):
    counter = jnp.arange(length, dtype=jnp.int32)
    product = counter[:, None] * counter[None, :] % length
    angles = product.astype(jnp.float32) * (2.0 * math.pi / length)
    factor = 1.0 / math.sqrt(length)
    return ((jnp.cos(angles) * factor).astype(jnp.bfloat16), (jnp.sin(angles) * factor).astype(jnp.bfloat16))

def spectral_factor(distance_value, length):
    counter = jnp.arange(length, dtype=jnp.int32)
    signed = jnp.where(counter < length // 2, counter, counter - length).astype(jnp.float32)
    phases = -distance_value * math.pi * signed * signed / float(length * length)
    return (jnp.cos(phases), jnp.sin(phases))

def spot_table(subsize):
    spotsize = 2 * subsize
    outer = jnp.arange(spotsize, dtype=jnp.int32)
    inner = jnp.arange(subsize, dtype=jnp.int32)
    angles = (inner[:, None] * outer[None, :] % spotsize).astype(jnp.float32) * (2.0 * math.pi / spotsize)
    wave_re = jnp.cos(angles) / math.sqrt(subsize)
    wave_im = -jnp.sin(angles) / math.sqrt(subsize)
    kron_re = wave_re[:, None, :, None] * wave_re[None, :, None, :] - wave_im[:, None, :, None] * wave_im[None, :, None, :]
    kron_im = wave_re[:, None, :, None] * wave_im[None, :, None, :] + wave_im[:, None, :, None] * wave_re[None, :, None, :]
    kron_re = kron_re.reshape(subsize * subsize, spotsize * spotsize)
    kron_im = kron_im.reshape(subsize * subsize, spotsize * spotsize)
    upper = jnp.concatenate([kron_re, kron_im], axis=1)
    lower = jnp.concatenate([-kron_im, kron_re], axis=1)
    return jnp.concatenate([upper, lower], axis=0).astype(jnp.bfloat16)

def rounded(value):
    return lax.optimization_barrier(value.astype(jnp.bfloat16)).astype(jnp.float32)

def layer_pass(field, screen, distance_value, cosine_table, sine_table):
    real_part = field[0].astype(jnp.float32)
    imag_part = field[1].astype(jnp.float32)
    screen_cos = jnp.cos(screen)
    screen_sin = jnp.sin(screen)
    screened = rounded(jnp.stack([real_part * screen_cos - imag_part * screen_sin, real_part * screen_sin + imag_part * screen_cos]))
    factor_re, factor_im = spectral_factor(distance_value, field.shape[2])
    along_cos = jnp.einsum('prj,jk->prk', screened, cosine_table)
    along_sin = jnp.einsum('prj,jk->prk', screened, sine_table)
    freq_re = along_cos[0] + along_sin[1]
    freq_im = along_cos[1] - along_sin[0]
    spectrum = rounded(jnp.stack([freq_re * factor_re[None, :] - freq_im * factor_im[None, :], freq_re * factor_im[None, :] + freq_im * factor_re[None, :]]))
    row_cos = jnp.einsum('pjc,jk->pkc', spectrum, cosine_table)
    row_sin = jnp.einsum('pjc,jk->pkc', spectrum, sine_table)
    wave_re = row_cos[0] + row_sin[1]
    wave_im = row_cos[1] - row_sin[0]
    phased = rounded(jnp.stack([wave_re * factor_re[:, None] - wave_im * factor_im[:, None], wave_re * factor_im[:, None] + wave_im * factor_re[:, None]]))
    back_cos = jnp.einsum('pjc,jk->pkc', phased, cosine_table)
    back_sin = jnp.einsum('pjc,jk->pkc', phased, sine_table)
    returned = rounded(jnp.stack([back_cos[0] - back_sin[1], back_cos[1] + back_sin[0]]))
    final_cos = jnp.einsum('prk,kj->prj', returned, cosine_table)
    final_sin = jnp.einsum('prk,kj->prj', returned, sine_table)
    return jnp.stack([final_cos[0] - final_sin[1], final_cos[1] + final_sin[0]]).astype(jnp.bfloat16)

def correlate_slots(slots, big_table, templates):
    pixels = templates.shape[0]
    fields_count = slots.shape[-1] // big_table.shape[0]
    shaped = slots.reshape(slots.shape[:-1] + (fields_count, big_table.shape[0])).astype(jnp.float32)
    spot_field = jnp.einsum('...i,io->...o', shaped, big_table.astype(jnp.float32))
    intensity = spot_field[..., :pixels] * spot_field[..., :pixels] + spot_field[..., pixels:] * spot_field[..., pixels:]
    intensity = rounded(intensity)
    return jnp.einsum('...i,io->...o', intensity, templates.astype(jnp.float32))

def reference(launch, screens, distance, templates, send_table, send_counts):
    cosine_bf, sine_bf = fourier_tables(N)
    cosine_table = cosine_bf.astype(jnp.float32)
    sine_table = sine_bf.astype(jnp.float32)
    finished = []
    for field_index in range(FIELDS):
        current = launch[field_index]
        for layer_index in range(LAYERS):
            current = layer_pass(current, screens[layer_index], distance[layer_index], cosine_table, sine_table)
        finished.append(current)
    pupil = jnp.stack(finished)
    blocks = pupil.reshape(FIELDS, 2, SIDE, SUB, SIDE, SUB).transpose(2, 4, 0, 1, 3, 5)
    blocks = blocks.reshape(SIDE * SIDE, FIELDS * 2 * SUB * SUB)
    offsets = (jnp.arange(N_STRIP, dtype=jnp.int32) * SUBS_DEV)[:, None, None]
    chosen = (send_table + offsets).astype(jnp.int32).reshape(-1)
    gathered = blocks[chosen].reshape(N_STRIP, N_STRIP, CAP, FIELDS * 2 * SUB * SUB)
    live = jnp.arange(CAP, dtype=jnp.int32)[None, None, :] < send_counts[:, :, None]
    gathered = jnp.where(live[:, :, :, None], gathered, jnp.zeros((), jnp.bfloat16))
    big_table = spot_table(SUB)
    correlation = correlate_slots(gathered, big_table, templates)
    return (pupil, correlation.transpose(1, 0, 2, 3, 4))
```

```python
import math

import jax
import jax.numpy as jnp
import numpy as np
from jax import lax
from jax.experimental import pallas as pl
from jax.experimental.pallas import tpu as pltpu
from jax.sharding import PartitionSpec as P

N = 1024
Q = 256
SUB = 16
SPOT = 2 * SUB
BF = jnp.bfloat16
F32 = jnp.float32


def bf16(table):
    return np.asarray(table, np.float32).astype(jnp.bfloat16)


def angle_tables():
    n = np.arange(Q)
    turn = 2.0 * np.pi * ((n[:, None] * n[None, :]) % Q) / Q
    cos, sin = np.cos(turn) / 16.0, np.sin(turn) / 16.0
    forward = np.block([[cos, -sin], [sin, cos]])
    inverse = np.block([[cos, sin], [-sin, cos]])
    k1 = np.arange(4)
    tw = 2.0 * np.pi * (k1[:, None] * n[None, :]) / N
    twiddle = np.stack([np.cos(tw), np.sin(tw)])
    index = (n[None, :, None] * (4 * n[None, None, :] + k1[:, None, None])) % N
    full = 2.0 * np.pi * index / N
    turned = np.concatenate([np.cos(full), np.sin(full)], axis=2) / 16.0
    order = (np.arange(SUB)[None, :] * SUB + np.arange(SUB)[:, None]).reshape(-1)
    both = np.concatenate([order, Q + order])
    return {
        "forward": bf16(forward),
        "inverse": bf16(inverse),
        "turned": bf16(turned),
        "twiddle": twiddle.astype(np.float32),
        "inverse_sub": bf16(inverse[:, both]),
        "twiddle_sub": twiddle[:, :, order].astype(np.float32),
    }


def spot_table():
    turn = 2.0 * np.pi * ((np.arange(SPOT)[:, None] * np.arange(SUB)[None, :]) % SPOT) / SPOT
    wave = (np.cos(turn) - 1j * np.sin(turn)) / math.sqrt(SUB)
    kron = wave[:, None, None, :] * wave[None, :, :, None]
    kron = kron.reshape(SPOT * SPOT, SUB * SUB)
    return bf16(np.block([[kron.real, -kron.imag], [kron.imag, kron.real]]))


def sincos(x):
    y = 0.5 * x
    z = y * y
    s = -1.0 / 39916800.0
    for c in (1.0 / 362880.0, -1.0 / 5040.0, 1.0 / 120.0, -1.0 / 6.0, 1.0):
        s = s * z + c
    s = s * y
    c = 1.0 / 479001600.0
    for a in (-1.0 / 3628800.0, 1.0 / 40320.0, -1.0 / 720.0, 1.0 / 24.0, -0.5, 1.0):
        c = c * z + a
    return 1.0 - 2.0 * s * s, 2.0 * s * c


def spectral(shared, layer):
    tail = shared[layer, 32:48, :].astype(F32)
    d = (tail[0:1] + tail[1:2]) + tail[2:3]
    place = lax.broadcasted_iota(jnp.int32, (1, N), 1)
    k = 4 * (place % Q) + place // Q
    m = jnp.where(k < N // 2, k, k - N).astype(F32)
    turns = d * (m * m * (0.5 / (N * N)))
    frac = turns - jnp.floor(turns + 0.5)
    cos, sin = sincos(frac * (2.0 * math.pi))
    return 0.25 * cos, -0.25 * sin


def granules(parts, width):
    parts = list(parts)
    lane = lax.broadcasted_iota(jnp.int32, parts[0].shape, 1) // width
    bit = 1
    while bit < len(parts):
        high = (lane & bit) != 0
        for i in range(len(parts)):
            if i & bit:
                continue
            a, b = parts[i], parts[i | bit]
            parts[i] = jnp.where(high, pltpu.roll(b, width * bit, 1), a)
            parts[i | bit] = jnp.where(high, b, pltpu.roll(a, 128 - width * bit, 1))
        bit *= 2
    return parts


def gathered(block, first, rows):
    columns = []
    for start in range(0, 32, 4):
        parts = [block[start + t, first : first + rows, :].astype(F32) for t in range(4)]
        columns.append(granules(parts, 32))
    return [jnp.concatenate([c[g] for c in columns], axis=1) for g in range(4)]


def quarters(x):
    return [x[:, Q * n : Q * n + Q] for n in range(4)]


def forward(re, im, h, twiddle, table):
    ar, ai = re[0] + re[2], im[0] + im[2]
    br, bi = re[0] - re[2], im[0] - im[2]
    cr, ci = re[1] + re[3], im[1] + im[3]
    dr, di = re[1] - re[3], im[1] - im[3]
    outs = [
        (ar + cr, ai + ci),
        (br + di, bi - dr),
        (ar - cr, ai - ci),
        (br - di, bi + dr),
    ]
    rows = []
    for k1, (r, m) in enumerate(outs):
        if k1:
            c, s = twiddle[0, k1 : k1 + 1, :], twiddle[1, k1 : k1 + 1, :]
            r, m = r * c + m * s, m * c - r * s
        rows.append(jnp.concatenate([r, m], axis=1).astype(BF))
    z = jnp.dot(jnp.concatenate(rows, axis=0), table[...], preferred_element_type=F32)
    spectrum = []
    for k1 in range(4):
        zr, zi = z[64 * k1 : 64 * k1 + 64, :Q], z[64 * k1 : 64 * k1 + 64, Q:]
        hr, hi = h[0][:, Q * k1 : Q * k1 + Q], h[1][:, Q * k1 : Q * k1 + Q]
        spectrum.append(((zr * hr - zi * hi).astype(BF), (zr * hi + zi * hr).astype(BF)))
    return spectrum


def inverse(spectrum, twiddle, table):
    stacked = jnp.concatenate([jnp.concatenate(s, axis=1) for s in spectrum], axis=0)
    y = jnp.dot(stacked, table[...], preferred_element_type=F32)
    outs = []
    for k1 in range(4):
        r, m = y[64 * k1 : 64 * k1 + 64, :Q], y[64 * k1 : 64 * k1 + 64, Q:]
        if k1:
            c, s = twiddle[0, k1 : k1 + 1, :], twiddle[1, k1 : k1 + 1, :]
            r, m = r * c - m * s, m * c + r * s
        outs.append((r, m))
    (r0, i0), (r1, i1), (r2, i2), (r3, i3) = outs
    ar, ai, br, bi = r0 + r2, i0 + i2, r0 - r2, i0 - i2
    cr, ci, dr, di = r1 + r3, i1 + i3, r1 - r3, i1 - i3
    re = [ar + cr, br - di, ar - cr, br + di]
    im = [ai + ci, bi + dr, ai - ci, bi - dr]
    return re, im


def inverse_turned(spectrum, turned, out):
    ys = []
    for k1 in range(4):
        r, m = spectrum[k1]
        rows = jnp.concatenate(
            [jnp.concatenate([r, -m], axis=1), jnp.concatenate([m, r], axis=1)], axis=0
        )
        ys.append(
            lax.dot_general(
                turned[k1], rows, (((1,), (1,)), ((), ())), preferred_element_type=F32
            )
        )
    a, b, c, d = ys[0] + ys[2], ys[0] - ys[2], ys[1] + ys[3], ys[1] - ys[3]
    lane = lax.broadcasted_iota(jnp.int32, d.shape, 1)
    swapped = pltpu.roll(d, 64, 1)
    d = jnp.where(lane < 64, -swapped, swapped)
    for n1, x in enumerate((a + c, b + d, a - c, b - d)):
        out[8 * n1 : 8 * n1 + 8, 0:32, :] = x.astype(BF).reshape(8, 32, 128)


def through_screen(re, im, phase):
    cos, sin = sincos(phase)
    out_re, out_im = [], []
    for n in range(4):
        c, s = cos[:, Q * n : Q * n + Q], sin[:, Q * n : Q * n + Q]
        c, s = jnp.concatenate([c, c], axis=0), jnp.concatenate([s, s], axis=0)
        out_re.append(re[n] * c - im[n] * s)
        out_im.append(re[n] * s + im[n] * c)
    return out_re, out_im


def first_kernel(launch, shared, twiddle, table, turned, out):
    re = quarters(jnp.concatenate([launch[0, 0], launch[1, 0]], axis=0).astype(F32))
    im = quarters(jnp.concatenate([launch[0, 1], launch[1, 1]], axis=0).astype(F32))
    re, im = through_screen(re, im, shared[0, 0:32, :].astype(F32))
    spectrum = forward(re, im, spectral(shared, 0), twiddle, table)
    inverse_turned(spectrum, turned, out)
    both = jnp.concatenate([shared[1, 0:32, :], shared[3, 0:32, :]], axis=0).astype(F32)
    for block in range(8):
        piece = both[:, 128 * block : 128 * block + 128].T.reshape(4, 2, 16, 64)
        out[4 * block : 4 * block + 4, 32:48, :] = jnp.concatenate(
            [piece[:, 0], piece[:, 1]], axis=2
        ).astype(BF)


def halves(groups):
    re = jnp.concatenate([groups[0], groups[1]], axis=0)
    im = jnp.concatenate([groups[2], groups[3]], axis=0)
    return quarters(re), quarters(im)


def column_kernel(layer, came, carried, shared, twiddle, table, back, turned, out):
    groups = gathered(carried, 32, 16)
    which = layer // 2
    phase = jnp.concatenate([groups[which], groups[2 + which]], axis=0)
    re, im = halves(gathered(came, 0, 32))
    spectrum = forward(re, im, spectral(shared, layer), twiddle, table)
    re, im = inverse(spectrum, twiddle, back)
    re, im = through_screen(re, im, phase)
    spectrum = forward(re, im, spectral(shared, layer + 1), twiddle, table)
    inverse_turned(spectrum, turned, out)


def row_kernel(layer, came, shared, twiddle, table, back, turned, out):
    re, im = halves(gathered(came, 0, 32))
    spectrum = forward(re, im, spectral(shared, layer), twiddle, table)
    re, im = inverse(spectrum, twiddle, back)
    re, im = through_screen(re, im, shared[layer + 1, 0:32, :].astype(F32))
    spectrum = forward(re, im, spectral(shared, layer + 1), twiddle, table)
    inverse_turned(spectrum, turned, out)


def last_kernel(
    came, shared, twiddle, table, back, twiddle_sub, back_sub, spots, templates, picks,
    pupil, result, cells,
):
    re, im = halves(gathered(came, 0, 32))
    spectrum = forward(re, im, spectral(shared, 3), twiddle, table)
    re, im = inverse(spectrum, twiddle, back)
    for n in range(4):
        for field in range(2):
            rows = slice(32 * field, 32 * field + 32)
            pupil[field, 0, :, Q * n : Q * n + Q] = re[n][rows].astype(BF)
            pupil[field, 1, :, Q * n : Q * n + Q] = im[n][rows].astype(BF)
    for part, x in enumerate(inverse(spectrum, twiddle_sub, back_sub)):
        for field in range(2):
            for upper in range(2):
                parts = [
                    x[n1][32 * field + 16 * a : 32 * field + 16 * a + 16,
                          128 * upper : 128 * upper + 128]
                    for a in range(2)
                    for n1 in range(4)
                ]
                for k, piece in enumerate(granules(parts, 16)):
                    row = part * 256 + (upper * 8 + k) * 16
                    cells[row : row + 16, 128 * field : 128 * field + 128] = piece.astype(BF)
    total = jnp.zeros((16, 256), F32)
    step = 256
    for start in range(0, 1024, step):
        sre = jnp.dot(spots[start : start + step, :], cells[...], preferred_element_type=F32)
        sim = jnp.dot(
            spots[1024 + start : 1024 + start + step, :], cells[...], preferred_element_type=F32
        )
        intensity = (sre * sre + sim * sim).astype(BF)
        total += jnp.dot(
            templates[:, start : start + step], intensity, preferred_element_type=F32
        )
    lane = lax.broadcasted_iota(jnp.int32, (32, 128), 1)
    chosen = jnp.where(lane == picks[...], 1.0, 0.0).astype(F32)
    for field in range(2):
        result[:, 16 * field : 16 * field + 16] = lax.dot_general(
            chosen,
            total[:, 128 * field : 128 * field + 128],
            (((1,), (1,)), ((), ())),
            precision=lax.Precision.HIGHEST,
            preferred_element_type=F32,
        )


def call(kernel, shapes, *operands, scratch=(), name=None):
    return pl.pallas_call(
        kernel,
        out_shape=shapes,
        scratch_shapes=list(scratch),
        compiler_params=pltpu.CompilerParams(vmem_limit_bytes=48 * 1024 * 1024),
        name=name,
    )(*operands)


def exchanged(block):
    return lax.all_to_all(block, "strip", split_axis=0, concat_axis=0, tiled=True)


def per_device(launch, screens, distance, templates, send_table, send_counts):
    tables = {name: jnp.asarray(value) for name, value in angle_tables().items()}
    twiddle, table = tables["twiddle"], tables["forward"]
    back, turned = tables["inverse"], tables["turned"]

    d = distance.reshape(1, 1)
    high = lax.reduce_precision(d, 8, 7)
    middle = lax.reduce_precision(d - high, 8, 7)
    low = (d - high) - middle
    row = lax.broadcasted_iota(jnp.int32, (16, N), 0)
    tail = jnp.where(row == 0, high, jnp.where(row == 1, middle, jnp.where(row == 2, low, 0.0)))
    mine = jnp.concatenate([screens[0], tail], axis=0).astype(BF)
    shared = lax.all_to_all(
        jnp.broadcast_to(mine[None], (4, 48, N)), "layer", split_axis=0, concat_axis=0, tiled=True
    )

    wide = jax.ShapeDtypeStruct((32, 48, 128), BF)
    plain = jax.ShapeDtypeStruct((32, 32, 128), BF)
    sent = call(first_kernel, wide, launch, shared, twiddle, table, turned, name="rows0")
    carried = exchanged(sent)

    def columns(layer, came, name):
        def kernel(*refs):
            column_kernel(layer, *refs)

        return call(
            kernel, plain, came, carried, shared, twiddle, table, back, turned, name=name
        )

    def rows(layer, came, name):
        def kernel(*refs):
            row_kernel(layer, *refs)

        return call(kernel, plain, came, shared, twiddle, table, back, turned, name=name)

    came = exchanged(columns(0, carried, "columns01"))
    came = exchanged(rows(1, came, "rows12"))
    came = exchanged(columns(2, came, "columns23"))

    slot = lax.axis_index("layer")
    picks = jnp.where(slot < send_counts[0], send_table[0, :, 0], -1).reshape(32, 1)
    pupil, result = call(
        last_kernel,
        (jax.ShapeDtypeStruct(launch.shape, BF), jax.ShapeDtypeStruct((32, 32), F32)),
        came, shared, twiddle, table, back, tables["twiddle_sub"], tables["inverse_sub"],
        jnp.asarray(spot_table()), templates.T, picks,
        scratch=[pltpu.VMEM((512, 256), BF)],
        name="rows3",
    )
    return (pupil, exchanged(result).reshape(1, 32, 1, 2, 16))


def solution(mesh):
    placed = (
        P(None, None, "strip", None),
        P("layer", "strip", None),
        P("layer"),
        P(),
        P("strip", None, "layer"),
        P("strip", None),
    )
    return jax.shard_map(
        per_device,
        mesh=mesh,
        in_specs=placed,
        out_specs=(P(None, None, "strip", None), P("strip", None, "layer", None, None)),
        check_vma=False,
    )
```

```python
import math

import jax
import jax.numpy as jnp
import numpy as np
from jax import lax
from jax.experimental import pallas as pl
from jax.experimental.pallas import tpu as pltpu
from jax.sharding import PartitionSpec as P

N = 1024
Q = 256
SUB = 16
SPOT = 2 * SUB
BF = jnp.bfloat16
F32 = jnp.float32


def bf16(table):
    return np.asarray(table, np.float32).astype(jnp.bfloat16)


def angle_tables():
    n = np.arange(Q)
    turn = 2.0 * np.pi * ((n[:, None] * n[None, :]) % Q) / Q
    cos, sin = np.cos(turn) / 16.0, np.sin(turn) / 16.0
    forward = np.block([[cos, -sin], [sin, cos]])
    inverse = np.block([[cos, sin], [-sin, cos]])
    k1 = np.arange(4)
    index = (n[None, :, None] * (4 * n[None, None, :] + k1[:, None, None])) % N
    full = 2.0 * np.pi * index / N
    turned = np.concatenate([np.cos(full), np.sin(full)], axis=2) / 16.0
    order = (np.arange(SUB)[None, :] * SUB + np.arange(SUB)[:, None]).reshape(-1)
    both = np.concatenate([order, Q + order])
    return {
        "forward": bf16(forward),
        "inverse": bf16(inverse),
        "turned": bf16(turned),
        "inverse_sub": bf16(inverse[:, both]),
    }


def spot_table():
    turn = 2.0 * np.pi * ((np.arange(SPOT)[:, None] * np.arange(SUB)[None, :]) % SPOT) / SPOT
    wave = (np.cos(turn) - 1j * np.sin(turn)) / math.sqrt(SUB)
    kron = wave[:, None, None, :] * wave[None, :, :, None]
    kron = kron.reshape(SPOT * SPOT, SUB * SUB)
    return bf16(np.block([[kron.real, -kron.imag], [kron.imag, kron.real]]))


def sincos(x):
    y = 0.5 * x
    z = y * y
    s = -1.0 / 39916800.0
    for c in (1.0 / 362880.0, -1.0 / 5040.0, 1.0 / 120.0, -1.0 / 6.0, 1.0):
        s = s * z + c
    s = s * y
    c = 1.0 / 479001600.0
    for a in (-1.0 / 3628800.0, 1.0 / 40320.0, -1.0 / 720.0, 1.0 / 24.0, -0.5, 1.0):
        c = c * z + a
    return 1.0 - 2.0 * s * s, 2.0 * s * c


def twiddles(sub=False):
    k1 = lax.broadcasted_iota(jnp.int32, (4, Q), 0)
    n2 = lax.broadcasted_iota(jnp.int32, (4, Q), 1)
    if sub:
        n2 = (n2 % SUB) * SUB + n2 // SUB
    turns = (k1 * n2).astype(F32) * (1.0 / N)
    turns = jnp.where(turns > 0.5, turns - 1.0, turns)
    return sincos(turns * (2.0 * math.pi))


def spectral(shared, layer):
    tail = shared[layer, 32:48, :].astype(F32)
    d = (tail[0:1] + tail[1:2]) + tail[2:3]
    place = lax.broadcasted_iota(jnp.int32, (1, N), 1)
    k = 4 * (place % Q) + place // Q
    m = jnp.where(k < N // 2, k, k - N).astype(F32)
    turns = d * (m * m * (0.5 / (N * N)))
    frac = turns - jnp.floor(turns + 0.5)
    cos, sin = sincos(frac * (2.0 * math.pi))
    return 0.25 * cos, -0.25 * sin


def granules(parts, width):
    parts = list(parts)
    lane = lax.broadcasted_iota(jnp.int32, parts[0].shape, 1) // width
    bit = 1
    while bit < len(parts):
        high = (lane & bit) != 0
        for i in range(len(parts)):
            if i & bit:
                continue
            a, b = parts[i], parts[i | bit]
            parts[i] = jnp.where(high, pltpu.roll(b, width * bit, 1), a)
            parts[i | bit] = jnp.where(high, b, pltpu.roll(a, 128 - width * bit, 1))
        bit *= 2
    return parts


def gathered(block, first, rows):
    columns = []
    for start in range(0, 32, 4):
        parts = [block[start + t, first : first + rows, :].astype(F32) for t in range(4)]
        columns.append(granules(parts, 32))
    return [jnp.concatenate([c[g] for c in columns], axis=1) for g in range(4)]


def quarters(x):
    return [x[:, Q * n : Q * n + Q] for n in range(4)]


def forward(re, im, h, twiddle, table):
    ar, ai = re[0] + re[2], im[0] + im[2]
    br, bi = re[0] - re[2], im[0] - im[2]
    cr, ci = re[1] + re[3], im[1] + im[3]
    dr, di = re[1] - re[3], im[1] - im[3]
    outs = [
        (ar + cr, ai + ci),
        (br + di, bi - dr),
        (ar - cr, ai - ci),
        (br - di, bi + dr),
    ]
    rows = []
    for k1, (r, m) in enumerate(outs):
        if k1:
            c, s = twiddle[0][k1 : k1 + 1, :], twiddle[1][k1 : k1 + 1, :]
            r, m = r * c + m * s, m * c - r * s
        rows.append(jnp.concatenate([r, m], axis=1).astype(BF))
    z = jnp.dot(jnp.concatenate(rows, axis=0), table[...], preferred_element_type=F32)
    spectrum = []
    for k1 in range(4):
        zr, zi = z[64 * k1 : 64 * k1 + 64, :Q], z[64 * k1 : 64 * k1 + 64, Q:]
        hr, hi = h[0][:, Q * k1 : Q * k1 + Q], h[1][:, Q * k1 : Q * k1 + Q]
        spectrum.append(((zr * hr - zi * hi).astype(BF), (zr * hi + zi * hr).astype(BF)))
    return spectrum


def inverse(spectrum, twiddle, table):
    stacked = jnp.concatenate([jnp.concatenate(s, axis=1) for s in spectrum], axis=0)
    y = jnp.dot(stacked, table[...], preferred_element_type=F32)
    outs = []
    for k1 in range(4):
        r, m = y[64 * k1 : 64 * k1 + 64, :Q], y[64 * k1 : 64 * k1 + 64, Q:]
        if k1:
            c, s = twiddle[0][k1 : k1 + 1, :], twiddle[1][k1 : k1 + 1, :]
            r, m = r * c - m * s, m * c + r * s
        outs.append((r, m))
    (r0, i0), (r1, i1), (r2, i2), (r3, i3) = outs
    ar, ai, br, bi = r0 + r2, i0 + i2, r0 - r2, i0 - i2
    cr, ci, dr, di = r1 + r3, i1 + i3, r1 - r3, i1 - i3
    re = [ar + cr, br - di, ar - cr, br + di]
    im = [ai + ci, bi + dr, ai - ci, bi - dr]
    return re, im


def inverse_turned(spectrum, turned, out):
    ys = []
    for k1 in range(4):
        r, m = spectrum[k1]
        rows = jnp.concatenate(
            [jnp.concatenate([r, -m], axis=1), jnp.concatenate([m, r], axis=1)], axis=0
        )
        ys.append(
            lax.dot_general(
                turned[k1], rows, (((1,), (1,)), ((), ())), preferred_element_type=F32
            )
        )
    a, b, c, d = ys[0] + ys[2], ys[0] - ys[2], ys[1] + ys[3], ys[1] - ys[3]
    lane = lax.broadcasted_iota(jnp.int32, d.shape, 1)
    swapped = pltpu.roll(d, 64, 1)
    d = jnp.where(lane < 64, -swapped, swapped)
    for n1, x in enumerate((a + c, b + d, a - c, b - d)):
        out[8 * n1 : 8 * n1 + 8, 0:32, :] = x.astype(BF).reshape(8, 32, 128)


def through_screen(re, im, phase):
    cos, sin = sincos(phase)
    out_re, out_im = [], []
    for n in range(4):
        c, s = cos[:, Q * n : Q * n + Q], sin[:, Q * n : Q * n + Q]
        c, s = jnp.concatenate([c, c], axis=0), jnp.concatenate([s, s], axis=0)
        out_re.append(re[n] * c - im[n] * s)
        out_im.append(re[n] * s + im[n] * c)
    return out_re, out_im


def payload_kernel(
    distance, far_screens, launch, far_targets, far_counts, far_table, far_turned, far_back,
    shared, held, picks, table, turned, back,
    screens, targets, counts, sems,
):
    copies = [
        pltpu.make_async_copy(source, target, sems.at[i])
        for i, (source, target) in enumerate([
            (far_screens, screens), (far_targets, targets), (far_counts, counts),
            (launch, held), (far_table, table), (far_turned, turned), (far_back, back),
        ])
    ]
    for copy in copies:
        copy.start()
    for copy in copies[:3]:
        copy.wait()
    phase = screens[0].astype(BF)
    d = jnp.full((16, N), distance[0], F32)
    high = d.astype(BF).astype(F32)
    middle = (d - high).astype(BF).astype(F32)
    low = (d - high) - middle
    row = lax.broadcasted_iota(jnp.int32, (16, N), 0)
    tail = jnp.where(row == 0, high, jnp.where(row == 1, middle, jnp.where(row == 2, low, 0.0)))
    tail = tail.astype(BF)
    for group in range(4):
        shared[group, 0:32, :] = phase
        shared[group, 32:48, :] = tail
    picks[...] = jnp.where(lax.axis_index("layer") < counts[...], targets[...], -1)
    for copy in copies[3:]:
        copy.wait()


def first_kernel(launch, shared, table, turned, out):
    twiddle = twiddles()
    re = quarters(jnp.concatenate([launch[0, 0], launch[1, 0]], axis=0).astype(F32))
    im = quarters(jnp.concatenate([launch[0, 1], launch[1, 1]], axis=0).astype(F32))
    re, im = through_screen(re, im, shared[0, 0:32, :].astype(F32))
    spectrum = forward(re, im, spectral(shared, 0), twiddle, table)
    inverse_turned(spectrum, turned, out)
    both = jnp.concatenate([shared[1, 0:32, :], shared[3, 0:32, :]], axis=0).astype(F32)
    for block in range(8):
        piece = both[:, 128 * block : 128 * block + 128].T.reshape(4, 2, 16, 64)
        out[4 * block : 4 * block + 4, 32:48, :] = jnp.concatenate(
            [piece[:, 0], piece[:, 1]], axis=2
        ).astype(BF)


def halves(groups):
    re = jnp.concatenate([groups[0], groups[1]], axis=0)
    im = jnp.concatenate([groups[2], groups[3]], axis=0)
    return quarters(re), quarters(im)


def column_kernel(layer, came, carried, shared, table, back, turned, out):
    twiddle = twiddles()
    groups = gathered(carried, 32, 16)
    which = layer // 2
    phase = jnp.concatenate([groups[which], groups[2 + which]], axis=0)
    re, im = halves(gathered(came, 0, 32))
    spectrum = forward(re, im, spectral(shared, layer), twiddle, table)
    re, im = inverse(spectrum, twiddle, back)
    re, im = through_screen(re, im, phase)
    spectrum = forward(re, im, spectral(shared, layer + 1), twiddle, table)
    inverse_turned(spectrum, turned, out)


def row_kernel(layer, came, shared, table, back, turned, out):
    twiddle = twiddles()
    re, im = halves(gathered(came, 0, 32))
    spectrum = forward(re, im, spectral(shared, layer), twiddle, table)
    re, im = inverse(spectrum, twiddle, back)
    re, im = through_screen(re, im, shared[layer + 1, 0:32, :].astype(F32))
    spectrum = forward(re, im, spectral(shared, layer + 1), twiddle, table)
    inverse_turned(spectrum, turned, out)


def last_kernel(
    came, shared, table, back, back_sub, spots, templates, picks,
    far_pupil, result,
    cells, pupil, sem,
):
    re, im = halves(gathered(came, 0, 32))
    twiddle = twiddles()
    spectrum = forward(re, im, spectral(shared, 3), twiddle, table)
    re, im = inverse(spectrum, twiddle, back)
    for n in range(4):
        for field in range(2):
            rows = slice(32 * field, 32 * field + 32)
            pupil[field, 0, :, Q * n : Q * n + Q] = re[n][rows].astype(BF)
            pupil[field, 1, :, Q * n : Q * n + Q] = im[n][rows].astype(BF)
    written = pltpu.make_async_copy(pupil, far_pupil, sem)
    written.start()
    for part, x in enumerate(inverse(spectrum, twiddles(True), back_sub)):
        for field in range(2):
            for upper in range(2):
                parts = [
                    x[n1][32 * field + 16 * a : 32 * field + 16 * a + 16,
                          128 * upper : 128 * upper + 128]
                    for a in range(2)
                    for n1 in range(4)
                ]
                for k, piece in enumerate(granules(parts, 16)):
                    row = part * 256 + (upper * 8 + k) * 16
                    cells[row : row + 16, 128 * field : 128 * field + 128] = piece.astype(BF)
    total = jnp.zeros((16, 256), F32)
    step = 256
    for start in range(0, 1024, step):
        sre = jnp.dot(spots[start : start + step, :], cells[...], preferred_element_type=F32)
        sim = jnp.dot(
            spots[1024 + start : 1024 + start + step, :], cells[...], preferred_element_type=F32
        )
        intensity = (sre * sre + sim * sim).astype(BF)
        total += jnp.dot(
            templates[:, start : start + step], intensity, preferred_element_type=F32
        )
    chosen = jnp.where(lax.broadcasted_iota(jnp.int32, (128, 32), 0) == picks[...], 1.0, 0.0)
    for field in range(2):
        result[:, 16 * field : 16 * field + 16] = lax.dot_general(
            chosen.astype(F32),
            total[:, 128 * field : 128 * field + 128],
            (((0,), (1,)), ((), ())),
            precision=lax.Precision.HIGHEST,
            preferred_element_type=F32,
        )
    written.wait()


VMEM = pl.BlockSpec(memory_space=pltpu.VMEM)
SMEM = pl.BlockSpec(memory_space=pltpu.SMEM)
FAR = pl.BlockSpec(memory_space=pltpu.HBM)


def call(kernel, shapes, *operands, name=None, **specs):
    return pl.pallas_call(
        kernel,
        out_shape=shapes,
        compiler_params=pltpu.CompilerParams(vmem_limit_bytes=24 * 1024 * 1024),
        name=name,
        **specs,
    )(*operands)


def exchanged(block, axis="strip"):
    return lax.all_to_all(block, axis, split_axis=0, concat_axis=0, tiled=True)


def per_device(launch, screens, distance, templates, send_table, send_counts):
    tables = {name: jnp.asarray(value) for name, value in angle_tables().items()}
    table, back, turned = tables["forward"], tables["inverse"], tables["turned"]

    payload, held, picks, table, turned, back = call(
        payload_kernel,
        (
            jax.ShapeDtypeStruct((4, 48, N), BF),
            jax.ShapeDtypeStruct(launch.shape, BF),
            jax.ShapeDtypeStruct((1, 32), jnp.int32),
            jax.ShapeDtypeStruct(table.shape, BF),
            jax.ShapeDtypeStruct(turned.shape, BF),
            jax.ShapeDtypeStruct(back.shape, BF),
        ),
        distance,
        *[
            pltpu.with_memory_space_constraint(x, pltpu.HBM)
            for x in (
                screens, launch, send_table.reshape(1, 32), send_counts, table, turned, back
            )
        ],
        in_specs=[SMEM] + [FAR] * 7,
        out_specs=(VMEM,) * 6,
        scratch_shapes=[
            pltpu.VMEM(screens.shape, F32),
            pltpu.VMEM((1, 32), jnp.int32),
            pltpu.VMEM((1, 32), jnp.int32),
            pltpu.SemaphoreType.DMA((7,)),
        ],
        name="payload",
    )
    shared = exchanged(payload, "layer")

    wide = jax.ShapeDtypeStruct((32, 48, 128), BF)
    plain = jax.ShapeDtypeStruct((32, 32, 128), BF)
    sent = call(first_kernel, wide, held, shared, table, turned, name="rows0")
    carried = exchanged(sent)

    def columns(layer, came, name):
        def kernel(*refs):
            column_kernel(layer, *refs)

        return call(kernel, plain, came, carried, shared, table, back, turned, name=name)

    def rows(layer, came, name):
        def kernel(*refs):
            row_kernel(layer, *refs)

        return call(kernel, plain, came, shared, table, back, turned, name=name)

    came = exchanged(columns(0, carried, "columns01"))
    came = exchanged(rows(1, came, "rows12"))
    came = exchanged(columns(2, came, "columns23"))

    spots = jnp.asarray(spot_table())
    pupil, result = call(
        last_kernel,
        (jax.ShapeDtypeStruct(launch.shape, BF), jax.ShapeDtypeStruct((32, 32), F32)),
        came, shared, table, back, tables["inverse_sub"], spots, templates.T, picks,
        in_specs=[VMEM] * 8,
        out_specs=(FAR, VMEM),
        scratch_shapes=[
            pltpu.VMEM((512, 256), BF),
            pltpu.VMEM(launch.shape, BF),
            pltpu.SemaphoreType.DMA,
        ],
        name="rows3",
    )
    return (pupil, exchanged(result).reshape(1, 32, 1, 2, 16))


def solution(mesh):
    placed = (
        P(None, None, "strip", None),
        P("layer", "strip", None),
        P("layer"),
        P(),
        P("strip", None, "layer"),
        P("strip", None),
    )
    return jax.shard_map(
        per_device,
        mesh=mesh,
        in_specs=placed,
        out_specs=(P(None, None, "strip", None), P("strip", None, "layer", None, None)),
        check_vma=False,
    )
```

```python
import math

import jax
import jax.numpy as jnp
import numpy as np
from jax import lax
from jax.experimental import pallas as pl
from jax.experimental.pallas import tpu as pltpu
from jax.sharding import PartitionSpec as P

N = 1024
Q = 256
SUB = 16
SPOT = 2 * SUB
BF = jnp.bfloat16
F32 = jnp.float32


def bf16(table):
    return np.asarray(table, np.float32).astype(jnp.bfloat16)


def angle_tables():
    n = np.arange(Q)
    turn = 2.0 * np.pi * ((n[:, None] * n[None, :]) % Q) / Q
    cos, sin = np.cos(turn) / 16.0, np.sin(turn) / 16.0
    forward = np.block([[cos, -sin], [sin, cos]])
    inverse = np.block([[cos, sin], [-sin, cos]])
    k1 = np.arange(4)
    index = (n[None, :, None] * (4 * n[None, None, :] + k1[:, None, None])) % N
    full = 2.0 * np.pi * index / N
    turned = np.concatenate([np.cos(full), np.sin(full)], axis=2) / 16.0
    order = (np.arange(SUB)[None, :] * SUB + np.arange(SUB)[:, None]).reshape(-1)
    both = np.concatenate([order, Q + order])
    return {
        "forward": bf16(forward),
        "inverse": bf16(inverse),
        "turned": bf16(turned),
        "inverse_sub": bf16(inverse[:, both]),
    }


def spot_table():
    turn = 2.0 * np.pi * ((np.arange(SPOT)[:, None] * np.arange(SUB)[None, :]) % SPOT) / SPOT
    wave = (np.cos(turn) - 1j * np.sin(turn)) / math.sqrt(SUB)
    kron = wave[:, None, None, :] * wave[None, :, :, None]
    kron = kron.reshape(SPOT * SPOT, SUB * SUB)
    return bf16(np.block([[kron.real, -kron.imag], [kron.imag, kron.real]]))


def sincos(x):
    y = 0.5 * x
    z = y * y
    s = -1.0 / 39916800.0
    for c in (1.0 / 362880.0, -1.0 / 5040.0, 1.0 / 120.0, -1.0 / 6.0, 1.0):
        s = s * z + c
    s = s * y
    c = 1.0 / 479001600.0
    for a in (-1.0 / 3628800.0, 1.0 / 40320.0, -1.0 / 720.0, 1.0 / 24.0, -0.5, 1.0):
        c = c * z + a
    return 1.0 - 2.0 * s * s, 2.0 * s * c


def twiddles(sub=False):
    k1 = lax.broadcasted_iota(jnp.int32, (4, Q), 0)
    n2 = lax.broadcasted_iota(jnp.int32, (4, Q), 1)
    if sub:
        n2 = (n2 % SUB) * SUB + n2 // SUB
    turns = (k1 * n2).astype(F32) * (1.0 / N)
    turns = jnp.where(turns > 0.5, turns - 1.0, turns)
    return sincos(turns * (2.0 * math.pi))


def spectral(shared, layer):
    tail = shared[layer, 0:16, N : N + 128].astype(F32)
    d = jnp.concatenate([(tail[0:1] + tail[1:2]) + tail[2:3]] * (N // 128), axis=1)
    place = lax.broadcasted_iota(jnp.int32, (1, N), 1)
    k = 4 * (place % Q) + place // Q
    m = jnp.where(k < N // 2, k, k - N).astype(F32)
    turns = d * (m * m * (0.5 / (N * N)))
    frac = turns - jnp.floor(turns + 0.5)
    cos, sin = sincos(frac * (2.0 * math.pi))
    return 0.25 * cos, -0.25 * sin


def granules(parts, width):
    parts = list(parts)
    lane = lax.broadcasted_iota(jnp.int32, parts[0].shape, 1) // width
    bit = 1
    while bit < len(parts):
        high = (lane & bit) != 0
        for i in range(len(parts)):
            if i & bit:
                continue
            a, b = parts[i], parts[i | bit]
            parts[i] = jnp.where(high, pltpu.roll(b, width * bit, 1), a)
            parts[i | bit] = jnp.where(high, b, pltpu.roll(a, 128 - width * bit, 1))
        bit *= 2
    return parts


def gathered(block, base, first):
    columns = []
    for start in range(base, base + 32, 4):
        parts = [block[start + t, first : first + 16, :].astype(F32) for t in range(4)]
        columns.append(granules(parts, 32))
    return [jnp.concatenate([c[g] for c in columns], axis=1) for g in range(4)]


def field_of(block, base=0):
    groups = gathered(block, base, 0)
    return (
        jnp.concatenate([groups[0], groups[2]], axis=0),
        jnp.concatenate([groups[1], groups[3]], axis=0),
    )


def quarters(x):
    return [x[:, Q * n : Q * n + Q] for n in range(4)]


def forward(re, im, h, twiddle, table):
    ar, ai = re[0] + re[2], im[0] + im[2]
    br, bi = re[0] - re[2], im[0] - im[2]
    cr, ci = re[1] + re[3], im[1] + im[3]
    dr, di = re[1] - re[3], im[1] - im[3]
    outs = [
        (ar + cr, ai + ci),
        (br + di, bi - dr),
        (ar - cr, ai - ci),
        (br - di, bi + dr),
    ]
    rows = []
    for k1, (r, m) in enumerate(outs):
        if k1:
            c, s = twiddle[0][k1 : k1 + 1, :], twiddle[1][k1 : k1 + 1, :]
            r, m = r * c + m * s, m * c - r * s
        rows.append(jnp.concatenate([r, m], axis=1).astype(BF))
    z = jnp.dot(jnp.concatenate(rows, axis=0), table[...], preferred_element_type=F32)
    spectrum = []
    size = re[0].shape[0]
    for k1 in range(4):
        zr, zi = z[size * k1 : size * k1 + size, :Q], z[size * k1 : size * k1 + size, Q:]
        hr, hi = h[0][:, Q * k1 : Q * k1 + Q], h[1][:, Q * k1 : Q * k1 + Q]
        spectrum.append(((zr * hr - zi * hi).astype(BF), (zr * hi + zi * hr).astype(BF)))
    return spectrum


def inverse(spectrum, twiddle, table):
    stacked = jnp.concatenate([jnp.concatenate(s, axis=1) for s in spectrum], axis=0)
    y = jnp.dot(stacked, table[...], preferred_element_type=F32)
    outs = []
    size = spectrum[0][0].shape[0]
    for k1 in range(4):
        r, m = y[size * k1 : size * k1 + size, :Q], y[size * k1 : size * k1 + size, Q:]
        if k1:
            c, s = twiddle[0][k1 : k1 + 1, :], twiddle[1][k1 : k1 + 1, :]
            r, m = r * c - m * s, m * c + r * s
        outs.append((r, m))
    (r0, i0), (r1, i1), (r2, i2), (r3, i3) = outs
    ar, ai, br, bi = r0 + r2, i0 + i2, r0 - r2, i0 - i2
    cr, ci, dr, di = r1 + r3, i1 + i3, r1 - r3, i1 - i3
    re = [ar + cr, br - di, ar - cr, br + di]
    im = [ai + ci, bi + dr, ai - ci, bi - dr]
    return re, im


def inverse_turned(spectrum, turned, out):
    ys = []
    for k1 in range(4):
        r, m = spectrum[k1]
        pair = [jnp.concatenate([r, -m], axis=1), jnp.concatenate([m, r], axis=1)]
        ys.append(
            lax.dot_general(
                turned[k1],
                jnp.concatenate(pair + pair, axis=0),
                (((1,), (1,)), ((), ())),
                preferred_element_type=F32,
            )
        )
    a, b, c, d = ys[0] + ys[2], ys[0] - ys[2], ys[1] + ys[3], ys[1] - ys[3]
    lane = lax.broadcasted_iota(jnp.int32, d.shape, 1)
    swapped = pltpu.roll(d, 32, 1)
    d = jnp.where((lane // 32) % 2 == 0, -swapped, swapped)
    low = lax.broadcasted_iota(jnp.int32, (8, 16, 128), 2) < 64
    for n1, x in enumerate((a + c, b + d, a - c, b - d)):
        x = x.reshape(8, 2, 16, 128)
        x = jnp.where(low, x[:, 0], x[:, 1]).astype(BF)
        for base in range(0, out.shape[0], 32):
            out[base + 8 * n1 : base + 8 * n1 + 8, 0:16, :] = x


def through_screen(re, im, phase):
    cos, sin = sincos(phase)
    out_re, out_im = [], []
    for r, m, c, s in zip(re, im, quarters(cos), quarters(sin)):
        out_re.append(r * c - m * s)
        out_im.append(r * s + m * c)
    return out_re, out_im


def payload_kernel(
    distance, far_screens, launch, far_targets, far_counts, far_table, far_turned, far_back,
    shared, held, picks, table, turned, back,
    screens, targets, counts, sems,
):
    group = lax.axis_index("layer")
    copies = [
        pltpu.make_async_copy(source, target, sems.at[i])
        for i, (source, target) in enumerate([
            (far_screens, screens), (far_targets, targets), (far_counts, counts),
            (launch.at[group % 2], held), (far_table, table), (far_turned, turned),
            (far_back, back),
        ])
    ]
    for copy in copies:
        copy.start()
    d = jnp.full((32, 128), distance[0], F32)
    high = d.astype(BF).astype(F32)
    middle = (d - high).astype(BF).astype(F32)
    low = (d - high) - middle
    row = lax.broadcasted_iota(jnp.int32, (32, 128), 0)
    tail = jnp.where(row == 0, high, jnp.where(row == 1, middle, jnp.where(row == 2, low, 0.0)))
    tail = tail.astype(BF)
    for copy in copies[:3]:
        copy.wait()
    phase = screens[0].astype(BF)
    for other in range(4):
        shared[other, :, 0:N] = phase
        shared[other, :, N : N + 128] = tail
    picks[...] = jnp.where(group < counts[...], targets[...], -1)
    for copy in copies[3:]:
        copy.wait()


def first_kernel(held, shared, table, turned, out):
    twiddle = twiddles()
    re, im = quarters(held[0].astype(F32)), quarters(held[1].astype(F32))
    re, im = through_screen(re, im, shared[0, :, 0:N].astype(F32))
    spectrum = forward(re, im, spectral(shared, 0), twiddle, table)
    inverse_turned(spectrum, turned, out)
    both = jnp.concatenate([shared[1, :, 0:N], shared[3, :, 0:N]], axis=0).astype(F32)
    for block in range(8):
        piece = both[:, 128 * block : 128 * block + 128].T.reshape(4, 2, 16, 64)
        out[4 * block : 4 * block + 4, 16:32, :] = jnp.concatenate(
            [piece[:, 0], piece[:, 1]], axis=2
        ).astype(BF)


def middle(layer, came, phase, shared, table, back, turned, out):
    twiddle = twiddles()
    re, im = field_of(came)
    spectrum = forward(
        quarters(re), quarters(im), spectral(shared, layer), twiddle, table
    )
    re, im = inverse(spectrum, twiddle, back)
    re, im = through_screen(re, im, phase)
    spectrum = forward(re, im, spectral(shared, layer + 1), twiddle, table)
    inverse_turned(spectrum, turned, out)


def column_kernel(layer, came, carried, shared, *rest):
    groups = gathered(carried, 0, 16)
    which = layer // 2
    phase = jnp.concatenate([groups[which], groups[2 + which]], axis=0)
    middle(layer, came, phase, shared, *rest)


def row_kernel(layer, came, shared, *rest):
    middle(layer, came, shared[layer + 1, :, 0:N].astype(F32), shared, *rest)


def last_kernel(
    came, shared, table, back, back_sub, spots, templates, picks,
    far_pupil, result,
    cells, pupil, sem,
):
    fields = [field_of(came, 0), field_of(came, 32)]
    re, im = [quarters(jnp.concatenate(x, axis=0)) for x in zip(*fields)]
    twiddle = twiddles()
    spectrum = forward(re, im, spectral(shared, 3), twiddle, table)
    re, im = inverse(spectrum, twiddle, back)
    for n in range(4):
        for field in range(2):
            rows = slice(32 * field, 32 * field + 32)
            pupil[field, 0, :, Q * n : Q * n + Q] = re[n][rows].astype(BF)
            pupil[field, 1, :, Q * n : Q * n + Q] = im[n][rows].astype(BF)
    written = pltpu.make_async_copy(pupil, far_pupil, sem)
    written.start()
    for part, x in enumerate(inverse(spectrum, twiddles(True), back_sub)):
        for field in range(2):
            for upper in range(2):
                parts = [
                    x[n1][32 * field + 16 * a : 32 * field + 16 * a + 16,
                          128 * upper : 128 * upper + 128]
                    for a in range(2)
                    for n1 in range(4)
                ]
                for k, piece in enumerate(granules(parts, 16)):
                    row = part * 256 + (upper * 8 + k) * 16
                    cells[row : row + 16, 128 * field : 128 * field + 128] = piece.astype(BF)
    total = jnp.zeros((16, 256), F32)
    step = 256
    for start in range(0, 1024, step):
        sre = jnp.dot(spots[start : start + step, :], cells[...], preferred_element_type=F32)
        sim = jnp.dot(
            spots[1024 + start : 1024 + start + step, :], cells[...], preferred_element_type=F32
        )
        intensity = (sre * sre + sim * sim).astype(BF)
        total += jnp.dot(
            templates[:, start : start + step], intensity, preferred_element_type=F32
        )
    chosen = jnp.where(lax.broadcasted_iota(jnp.int32, (128, 32), 0) == picks[...], 1.0, 0.0)
    for field in range(2):
        result[:, 16 * field : 16 * field + 16] = lax.dot_general(
            chosen.astype(F32),
            total[:, 128 * field : 128 * field + 128],
            (((0,), (1,)), ((), ())),
            precision=lax.Precision.HIGHEST,
            preferred_element_type=F32,
        )
    written.wait()


VMEM = pl.BlockSpec(memory_space=pltpu.VMEM)
SMEM = pl.BlockSpec(memory_space=pltpu.SMEM)
FAR = pl.BlockSpec(memory_space=pltpu.HBM)


def call(kernel, shapes, *operands, name=None, **specs):
    return pl.pallas_call(
        kernel,
        out_shape=shapes,
        compiler_params=pltpu.CompilerParams(vmem_limit_bytes=24 * 1024 * 1024),
        name=name,
        **specs,
    )(*operands)


def exchanged(block, axis="strip", groups=None):
    return lax.all_to_all(
        block, axis, split_axis=0, concat_axis=0, tiled=True, axis_index_groups=groups
    )


def per_device(launch, screens, distance, templates, send_table, send_counts):
    tables = {name: jnp.asarray(value) for name, value in angle_tables().items()}
    table, back, turned = tables["forward"], tables["inverse"], tables["turned"]

    payload, held, picks, table, turned, back = call(
        payload_kernel,
        (
            jax.ShapeDtypeStruct((4, 32, N + 128), BF),
            jax.ShapeDtypeStruct(launch.shape[1:], BF),
            jax.ShapeDtypeStruct((1, 32), jnp.int32),
            jax.ShapeDtypeStruct(table.shape, BF),
            jax.ShapeDtypeStruct(turned.shape, BF),
            jax.ShapeDtypeStruct(back.shape, BF),
        ),
        distance,
        *[
            pltpu.with_memory_space_constraint(x, pltpu.HBM)
            for x in (
                screens, launch, send_table.reshape(1, 32), send_counts, table, turned, back
            )
        ],
        in_specs=[SMEM] + [FAR] * 7,
        out_specs=(VMEM,) * 6,
        scratch_shapes=[
            pltpu.VMEM(screens.shape, F32),
            pltpu.VMEM((1, 32), jnp.int32),
            pltpu.VMEM((1, 32), jnp.int32),
            pltpu.SemaphoreType.DMA((7,)),
        ],
        name="payload",
    )
    shared = exchanged(payload, "layer")

    wide = jax.ShapeDtypeStruct((32, 32, 128), BF)
    plain = jax.ShapeDtypeStruct((32, 16, 128), BF)
    twice = jax.ShapeDtypeStruct((64, 16, 128), BF)
    pairs = [[32 * group + strip for group in pair for strip in range(32)] for pair in ((0, 1), (2, 3))]
    sent = call(first_kernel, wide, held, shared, table, turned, name="rows0")
    carried = exchanged(sent)

    def columns(layer, came, shape, name):
        def kernel(*refs):
            column_kernel(layer, *refs)

        return call(kernel, shape, came, carried, shared, table, back, turned, name=name)

    def rows(layer, came, name):
        def kernel(*refs):
            row_kernel(layer, *refs)

        return call(kernel, plain, came, shared, table, back, turned, name=name)

    came = exchanged(columns(0, carried, plain, "columns01"))
    came = exchanged(rows(1, came, "rows12"))
    came = exchanged(columns(2, came, twice, "columns23"), ("layer", "strip"), pairs)

    spots = jnp.asarray(spot_table())
    pupil, result = call(
        last_kernel,
        (jax.ShapeDtypeStruct(launch.shape, BF), jax.ShapeDtypeStruct((32, 32), F32)),
        came, shared, table, back, tables["inverse_sub"], spots, templates.T, picks,
        in_specs=[VMEM] * 8,
        out_specs=(FAR, VMEM),
        scratch_shapes=[
            pltpu.VMEM((512, 256), BF),
            pltpu.VMEM(launch.shape, BF),
            pltpu.SemaphoreType.DMA,
        ],
        name="rows3",
    )
    return (pupil, exchanged(result).reshape(1, 32, 1, 2, 16))


def solution(mesh):
    placed = (
        P(None, None, "strip", None),
        P("layer", "strip", None),
        P("layer"),
        P(),
        P("strip", None, "layer"),
        P("strip", None),
    )
    return jax.shard_map(
        per_device,
        mesh=mesh,
        in_specs=placed,
        out_specs=(P(None, None, "strip", None), P("strip", None, "layer", None, None)),
        check_vma=False,
    )
```

```python
import math

import jax
import jax.numpy as jnp
import numpy as np
from jax import lax
from jax.experimental import pallas as pl
from jax.experimental.pallas import tpu as pltpu
from jax.sharding import PartitionSpec as P

N = 1024
Q = 256
SUB = 16
SPOT = 2 * SUB
BF = jnp.bfloat16
F32 = jnp.float32


def bf16(table):
    return np.asarray(table, np.float32).astype(jnp.bfloat16)


ORDERS = {
    "plain": lambda at: at,
    "send": lambda at: (at % 128) // 16 * 32 + at // 128 * 16 + at % 16,
    "sub": lambda at: at % SUB * SUB + at // SUB,
}


def angle_tables():
    n = np.arange(Q)
    turn = 2.0 * np.pi * ((n[:, None] * n[None, :]) % Q) / Q
    cos, sin = np.cos(turn) / 16.0, np.sin(turn) / 16.0
    forward = np.block([[cos, -sin], [sin, cos]])
    inverse = np.block([[cos, sin], [-sin, cos]])
    tables = {"forward": bf16(forward)}
    for name, order in ORDERS.items():
        tables[name] = bf16(inverse[:, np.concatenate([order(n), Q + order(n)])])
    return tables


def spot_table():
    turn = 2.0 * np.pi * ((np.arange(SPOT)[:, None] * np.arange(SUB)[None, :]) % SPOT) / SPOT
    wave = (np.cos(turn) - 1j * np.sin(turn)) / math.sqrt(SUB)
    kron = wave[:, None, None, :] * wave[None, :, :, None]
    kron = kron.reshape(SPOT * SPOT, SUB * SUB)
    return bf16(np.block([[kron.real, -kron.imag], [kron.imag, kron.real]]))


def sincos(x):
    y = 0.5 * x
    z = y * y
    s = -1.0 / 39916800.0
    for c in (1.0 / 362880.0, -1.0 / 5040.0, 1.0 / 120.0, -1.0 / 6.0, 1.0):
        s = s * z + c
    s = s * y
    c = 1.0 / 479001600.0
    for a in (-1.0 / 3628800.0, 1.0 / 40320.0, -1.0 / 720.0, 1.0 / 24.0, -0.5, 1.0):
        c = c * z + a
    return 1.0 - 2.0 * s * s, 2.0 * s * c


def twiddles(out):
    k1 = lax.broadcasted_iota(jnp.int32, (4, Q), 0)
    at = lax.broadcasted_iota(jnp.int32, (4, Q), 1)
    for i, order in enumerate(ORDERS.values()):
        turns = (k1 * order(at)).astype(F32) * (1.0 / N)
        turns = jnp.where(turns > 0.5, turns - 1.0, turns)
        out[8 * i : 8 * i + 4, :], out[8 * i + 4 : 8 * i + 8, :] = sincos(turns * (2.0 * math.pi))


def spectra(shared, out):
    d = []
    for layer in range(4):
        tail = shared[layer, 0:16, N : N + 128].astype(F32)
        d.append((tail[0:1] + tail[1:2]) + tail[2:3])
    d = jnp.concatenate([jnp.concatenate(d, axis=0)] * (N // 128), axis=1)
    place = lax.broadcasted_iota(jnp.int32, (4, N), 1)
    k = 4 * (place % Q) + place // Q
    m = jnp.where(k < N // 2, k, k - N).astype(F32)
    turns = d * (m * m * (0.5 / (N * N)))
    frac = turns - jnp.floor(turns + 0.5)
    cos, sin = sincos(frac * (2.0 * math.pi))
    out[0:4, :], out[4:8, :] = 0.25 * cos, -0.25 * sin


def twisted(twiddle, order, k1):
    row = 8 * list(ORDERS).index(order) + k1
    return twiddle[row : row + 1, :], twiddle[row + 4 : row + 5, :]


def granules(parts, width):
    parts = list(parts)
    lane = lax.broadcasted_iota(jnp.int32, parts[0].shape, 1) // width
    bit = 1
    while bit < len(parts):
        high = (lane & bit) != 0
        for i in range(len(parts)):
            if i & bit:
                continue
            a, b = parts[i], parts[i | bit]
            parts[i] = jnp.where(high, pltpu.roll(b, width * bit, 1), a)
            parts[i | bit] = jnp.where(high, b, pltpu.roll(a, 128 - width * bit, 1))
        bit *= 2
    return parts


def gathered(block, base, first):
    columns = []
    for start in range(base, base + 32, 4):
        parts = [block[start + t, first : first + 16, :].astype(F32) for t in range(4)]
        columns.append(granules(parts, 32))
    return [jnp.concatenate([c[g] for c in columns], axis=1) for g in range(4)]


def field_of(block, base=0):
    groups = gathered(block, base, 0)
    return (
        jnp.concatenate([groups[0], groups[2]], axis=0),
        jnp.concatenate([groups[1], groups[3]], axis=0),
    )


def quarters(x):
    return [x[:, Q * n : Q * n + Q] for n in range(4)]


def forward(re, im, layer, spectrum_rows, twiddle, table):
    ar, ai = re[0] + re[2], im[0] + im[2]
    br, bi = re[0] - re[2], im[0] - im[2]
    cr, ci = re[1] + re[3], im[1] + im[3]
    dr, di = re[1] - re[3], im[1] - im[3]
    outs = [
        (ar + cr, ai + ci),
        (br + di, bi - dr),
        (ar - cr, ai - ci),
        (br - di, bi + dr),
    ]
    rows = []
    for k1, (r, m) in enumerate(outs):
        if k1:
            c, s = twisted(twiddle, "plain", k1)
            r, m = r * c + m * s, m * c - r * s
        rows.append(jnp.concatenate([r, m], axis=1).astype(BF))
    z = jnp.dot(jnp.concatenate(rows, axis=0), table[...], preferred_element_type=F32)
    spectrum = []
    size = re[0].shape[0]
    for k1 in range(4):
        zr, zi = z[size * k1 : size * k1 + size, :Q], z[size * k1 : size * k1 + size, Q:]
        hr = spectrum_rows[layer : layer + 1, Q * k1 : Q * k1 + Q]
        hi = spectrum_rows[layer + 4 : layer + 5, Q * k1 : Q * k1 + Q]
        spectrum.append(((zr * hr - zi * hi).astype(BF), (zr * hi + zi * hr).astype(BF)))
    return spectrum


def inverse(spectrum, order, twiddle, table):
    stacked = jnp.concatenate([jnp.concatenate(s, axis=1) for s in spectrum], axis=0)
    y = jnp.dot(stacked, table[...], preferred_element_type=F32)
    outs = []
    size = spectrum[0][0].shape[0]
    for k1 in range(4):
        r, m = y[size * k1 : size * k1 + size, :Q], y[size * k1 : size * k1 + size, Q:]
        if k1:
            c, s = twisted(twiddle, order, k1)
            r, m = r * c - m * s, m * c + r * s
        outs.append((r, m))
    (r0, i0), (r1, i1), (r2, i2), (r3, i3) = outs
    ar, ai, br, bi = r0 + r2, i0 + i2, r0 - r2, i0 - i2
    cr, ci, dr, di = r1 + r3, i1 + i3, r1 - r3, i1 - i3
    re = [ar + cr, br - di, ar - cr, br + di]
    im = [ai + ci, bi + dr, ai - ci, bi - dr]
    return re, im


def sent(spectrum, twiddle, table, out):
    for n1, (r, m) in enumerate(zip(*inverse(spectrum, "send", twiddle, table))):
        x = jnp.concatenate([r[:, :128], m[:, :128], r[:, 128:], m[:, 128:]], axis=0)
        x = x.T.astype(BF).reshape(8, 16, 128)
        for base in range(0, out.shape[0], 32):
            out[base + 8 * n1 : base + 8 * n1 + 8, 0:16, :] = x


def through_screen(re, im, phase):
    cos, sin = sincos(phase)
    out_re, out_im = [], []
    for r, m, c, s in zip(re, im, quarters(cos), quarters(sin)):
        out_re.append(r * c - m * s)
        out_im.append(r * s + m * c)
    return out_re, out_im


def payload_kernel(
    distance, far_screens, launch, far_targets, far_counts, far_table, far_send, far_back,
    shared, held, picks, table, send, back, twiddle,
    screens, targets, counts, sems,
):
    group = lax.axis_index("layer")
    copies = [
        pltpu.make_async_copy(source, target, sems.at[i])
        for i, (source, target) in enumerate([
            (far_screens, screens), (far_targets, targets), (far_counts, counts),
            (launch.at[group % 2], held), (far_table, table), (far_send, send),
            (far_back, back),
        ])
    ]
    for copy in copies:
        copy.start()
    d = jnp.full((32, 128), distance[0], F32)
    high = d.astype(BF).astype(F32)
    middle = (d - high).astype(BF).astype(F32)
    low = (d - high) - middle
    row = lax.broadcasted_iota(jnp.int32, (32, 128), 0)
    tail = jnp.where(row == 0, high, jnp.where(row == 1, middle, jnp.where(row == 2, low, 0.0)))
    tail = tail.astype(BF)
    twiddles(twiddle)
    for copy in copies[:3]:
        copy.wait()
    phase = screens[0].astype(BF)
    for other in range(4):
        shared[other, :, 0:N] = phase
        shared[other, :, N : N + 128] = tail
    picks[...] = jnp.where(group < counts[...], targets[...], -1)
    for copy in copies[3:]:
        copy.wait()


def first_kernel(held, shared, twiddle, table, send, out, h):
    spectra(shared, h)
    re, im = quarters(held[0].astype(F32)), quarters(held[1].astype(F32))
    re, im = through_screen(re, im, shared[0, :, 0:N].astype(F32))
    sent(forward(re, im, 0, h, twiddle, table), twiddle, send, out)
    both = jnp.concatenate([shared[1, :, 0:N], shared[3, :, 0:N]], axis=0).astype(F32)
    for block in range(8):
        piece = both[:, 128 * block : 128 * block + 128].T.reshape(4, 2, 16, 64)
        out[4 * block : 4 * block + 4, 16:32, :] = jnp.concatenate(
            [piece[:, 0], piece[:, 1]], axis=2
        ).astype(BF)


def middle(layer, came, phase, h, twiddle, table, back, send, out):
    re, im = field_of(came)
    spectrum = forward(quarters(re), quarters(im), layer, h, twiddle, table)
    re, im = inverse(spectrum, "plain", twiddle, back)
    re, im = through_screen(re, im, phase)
    sent(forward(re, im, layer + 1, h, twiddle, table), twiddle, send, out)


def column_kernel(layer, came, carried, *rest):
    groups = gathered(carried, 0, 16)
    which = layer // 2
    phase = jnp.concatenate([groups[which], groups[2 + which]], axis=0)
    middle(layer, came, phase, *rest)


def row_kernel(layer, came, shared, *rest):
    middle(layer, came, shared[layer + 1, :, 0:N].astype(F32), *rest)


def last_kernel(
    came, h, twiddle, table, back, back_sub, spots, templates, picks,
    far_pupil, result,
    cells, pupil, sem,
):
    fields = [field_of(came, 0), field_of(came, 32)]
    re, im = [quarters(jnp.concatenate(x, axis=0)) for x in zip(*fields)]
    spectrum = forward(re, im, 3, h, twiddle, table)
    re, im = inverse(spectrum, "plain", twiddle, back)
    for n in range(4):
        for field in range(2):
            rows = slice(32 * field, 32 * field + 32)
            pupil[field, 0, :, Q * n : Q * n + Q] = re[n][rows].astype(BF)
            pupil[field, 1, :, Q * n : Q * n + Q] = im[n][rows].astype(BF)
    written = pltpu.make_async_copy(pupil, far_pupil, sem)
    written.start()
    for part, x in enumerate(inverse(spectrum, "sub", twiddle, back_sub)):
        for field in range(2):
            for upper in range(2):
                parts = [
                    x[n1][32 * field + 16 * a : 32 * field + 16 * a + 16,
                          128 * upper : 128 * upper + 128]
                    for a in range(2)
                    for n1 in range(4)
                ]
                for k, piece in enumerate(granules(parts, 16)):
                    row = part * 256 + (upper * 8 + k) * 16
                    cells[row : row + 16, 128 * field : 128 * field + 128] = piece.astype(BF)
    total = jnp.zeros((16, 256), F32)
    step = 256
    for start in range(0, 1024, step):
        sre = jnp.dot(spots[start : start + step, :], cells[...], preferred_element_type=F32)
        sim = jnp.dot(
            spots[1024 + start : 1024 + start + step, :], cells[...], preferred_element_type=F32
        )
        intensity = (sre * sre + sim * sim).astype(BF)
        total += jnp.dot(
            templates[:, start : start + step], intensity, preferred_element_type=F32
        )
    chosen = jnp.where(lax.broadcasted_iota(jnp.int32, (128, 32), 0) == picks[...], 1.0, 0.0)
    for field in range(2):
        result[:, 16 * field : 16 * field + 16] = lax.dot_general(
            chosen.astype(F32),
            total[:, 128 * field : 128 * field + 128],
            (((0,), (1,)), ((), ())),
            precision=lax.Precision.HIGHEST,
            preferred_element_type=F32,
        )
    written.wait()


VMEM = pl.BlockSpec(memory_space=pltpu.VMEM)
SMEM = pl.BlockSpec(memory_space=pltpu.SMEM)
FAR = pl.BlockSpec(memory_space=pltpu.HBM)


def call(kernel, shapes, *operands, name=None, **specs):
    return pl.pallas_call(
        kernel,
        out_shape=shapes,
        compiler_params=pltpu.CompilerParams(vmem_limit_bytes=24 * 1024 * 1024),
        name=name,
        **specs,
    )(*operands)


def exchanged(block, axis="strip", groups=None):
    return lax.all_to_all(
        block, axis, split_axis=0, concat_axis=0, tiled=True, axis_index_groups=groups
    )


def per_device(launch, screens, distance, templates, send_table, send_counts):
    tables = {name: jnp.asarray(value) for name, value in angle_tables().items()}
    table, back, send = tables["forward"], tables["plain"], tables["send"]

    payload, held, picks, table, send, back, twiddle = call(
        payload_kernel,
        (
            jax.ShapeDtypeStruct((4, 32, N + 128), BF),
            jax.ShapeDtypeStruct(launch.shape[1:], BF),
            jax.ShapeDtypeStruct((1, 32), jnp.int32),
            jax.ShapeDtypeStruct(table.shape, BF),
            jax.ShapeDtypeStruct(send.shape, BF),
            jax.ShapeDtypeStruct(back.shape, BF),
            jax.ShapeDtypeStruct((24, Q), F32),
        ),
        distance,
        *[
            pltpu.with_memory_space_constraint(x, pltpu.HBM)
            for x in (
                screens, launch, send_table.reshape(1, 32), send_counts, table, send, back
            )
        ],
        in_specs=[SMEM] + [FAR] * 7,
        out_specs=(VMEM,) * 7,
        scratch_shapes=[
            pltpu.VMEM(screens.shape, F32),
            pltpu.VMEM((1, 32), jnp.int32),
            pltpu.VMEM((1, 32), jnp.int32),
            pltpu.SemaphoreType.DMA((7,)),
        ],
        name="payload",
    )
    shared = exchanged(payload, "layer")

    wide = jax.ShapeDtypeStruct((32, 32, 128), BF)
    plain = jax.ShapeDtypeStruct((32, 16, 128), BF)
    twice = jax.ShapeDtypeStruct((64, 16, 128), BF)
    pairs = [[32 * group + strip for group in pair for strip in range(32)] for pair in ((0, 1), (2, 3))]
    leaving, h = call(
        first_kernel, (wide, jax.ShapeDtypeStruct((8, N), F32)),
        held, shared, twiddle, table, send, name="rows0",
    )
    carried = exchanged(leaving)

    def columns(layer, came, shape, name):
        def kernel(*refs):
            column_kernel(layer, *refs)

        return call(kernel, shape, came, carried, h, twiddle, table, back, send, name=name)

    def rows(layer, came, name):
        def kernel(*refs):
            row_kernel(layer, *refs)

        return call(kernel, plain, came, shared, h, twiddle, table, back, send, name=name)

    came = exchanged(columns(0, carried, plain, "columns01"))
    came = exchanged(rows(1, came, "rows12"))
    came = exchanged(columns(2, came, twice, "columns23"), ("layer", "strip"), pairs)

    spots = jnp.asarray(spot_table())
    pupil, result = call(
        last_kernel,
        (jax.ShapeDtypeStruct(launch.shape, BF), jax.ShapeDtypeStruct((32, 32), F32)),
        came, h, twiddle, table, back, tables["sub"], spots, templates.T, picks,
        in_specs=[VMEM] * 9,
        out_specs=(FAR, VMEM),
        scratch_shapes=[
            pltpu.VMEM((512, 256), BF),
            pltpu.VMEM(launch.shape, BF),
            pltpu.SemaphoreType.DMA,
        ],
        name="rows3",
    )
    return (pupil, exchanged(result).reshape(1, 32, 1, 2, 16))


def solution(mesh):
    placed = (
        P(None, None, "strip", None),
        P("layer", "strip", None),
        P("layer"),
        P(),
        P("strip", None, "layer"),
        P("strip", None),
    )
    return jax.shard_map(
        per_device,
        mesh=mesh,
        in_specs=placed,
        out_specs=(P(None, None, "strip", None), P("strip", None, "layer", None, None)),
        check_vma=False,
    )
```

```python
import math

import jax
import jax.numpy as jnp
import numpy as np
from jax import lax
from jax.experimental import pallas as pl
from jax.experimental.pallas import tpu as pltpu
from jax.sharding import PartitionSpec as P

N = 1024
Q = 256
SUB = 16
SPOT = 2 * SUB
BF = jnp.bfloat16
F32 = jnp.float32


def bf16(table):
    return np.asarray(table, np.float32).astype(jnp.bfloat16)


ORDERS = {
    "plain": lambda at: at,
    "send": lambda at: (at % 128) // 16 * 32 + at // 128 * 16 + at % 16,
    "sub": lambda at: at % SUB * SUB + at // SUB,
}


def angle_tables():
    n = np.arange(Q)
    turn = 2.0 * np.pi * ((n[:, None] * n[None, :]) % Q) / Q
    cos, sin = np.cos(turn) / 16.0, np.sin(turn) / 16.0
    forward = np.block([[cos, -sin], [sin, cos]])
    inverse = np.block([[cos, sin], [-sin, cos]])
    tables = {"forward": bf16(forward)}
    for name, order in ORDERS.items():
        tables[name] = bf16(inverse[:, np.concatenate([order(n), Q + order(n)])])
    return tables


def spot_table():
    turn = 2.0 * np.pi * ((np.arange(SPOT)[:, None] * np.arange(SUB)[None, :]) % SPOT) / SPOT
    wave = (np.cos(turn) - 1j * np.sin(turn)) / math.sqrt(SUB)
    kron = wave[:, None, None, :] * wave[None, :, :, None]
    kron = kron.reshape(SPOT * SPOT, SUB * SUB)
    return bf16(np.block([[kron.real, -kron.imag], [kron.imag, kron.real]]).T)


def sincos(x):
    y = 0.5 * x
    z = y * y
    s = -1.0 / 39916800.0
    for c in (1.0 / 362880.0, -1.0 / 5040.0, 1.0 / 120.0, -1.0 / 6.0, 1.0):
        s = s * z + c
    s = s * y
    c = 1.0 / 479001600.0
    for a in (-1.0 / 3628800.0, 1.0 / 40320.0, -1.0 / 720.0, 1.0 / 24.0, -0.5, 1.0):
        c = c * z + a
    return 1.0 - 2.0 * s * s, 2.0 * s * c


def twiddles(out):
    k1 = lax.broadcasted_iota(jnp.int32, (4, Q), 0)
    at = lax.broadcasted_iota(jnp.int32, (4, Q), 1)
    for i, order in enumerate(ORDERS.values()):
        turns = (k1 * order(at)).astype(F32) * (1.0 / N)
        turns = jnp.where(turns > 0.5, turns - 1.0, turns)
        out[8 * i : 8 * i + 4, :], out[8 * i + 4 : 8 * i + 8, :] = sincos(turns * (2.0 * math.pi))


def spectra(shared, out):
    d = []
    for layer in range(4):
        tail = shared[layer, 0:16, N : N + 128].astype(F32)
        d.append((tail[0:1] + tail[1:2]) + tail[2:3])
    d = jnp.concatenate([jnp.concatenate(d, axis=0)] * (N // 128), axis=1)
    place = lax.broadcasted_iota(jnp.int32, (4, N), 1)
    k = 4 * (place % Q) + place // Q
    m = jnp.where(k < N // 2, k, k - N).astype(F32)
    turns = d * (m * m * (0.5 / (N * N)))
    frac = turns - jnp.floor(turns + 0.5)
    cos, sin = sincos(frac * (2.0 * math.pi))
    out[0:4, :], out[4:8, :] = 0.25 * cos, -0.25 * sin


def twisted(twiddle, order, k1):
    row = 8 * list(ORDERS).index(order) + k1
    return twiddle[row : row + 1, :], twiddle[row + 4 : row + 5, :]


def granules(parts, width):
    parts = list(parts)
    lane = lax.broadcasted_iota(jnp.int32, parts[0].shape, 1) // width
    bit = 1
    while bit < len(parts):
        high = (lane & bit) != 0
        for i in range(len(parts)):
            if i & bit:
                continue
            a, b = parts[i], parts[i | bit]
            parts[i] = jnp.where(high, pltpu.roll(b, width * bit, 1), a)
            parts[i | bit] = jnp.where(high, b, pltpu.roll(a, 128 - width * bit, 1))
        bit *= 2
    return parts


def gathered(block, base, first):
    columns = []
    for start in range(base, base + 32, 4):
        parts = [block[start + t, first : first + 16, :] for t in range(4)]
        columns.append(granules(parts, 32))
    return [jnp.concatenate([c[g] for c in columns], axis=1).astype(F32) for g in range(4)]


def field_of(block, base=0):
    groups = gathered(block, base, 0)
    return (
        jnp.concatenate([groups[0], groups[2]], axis=0),
        jnp.concatenate([groups[1], groups[3]], axis=0),
    )


def quarters(x):
    return [x[:, Q * n : Q * n + Q] for n in range(4)]


def forward(re, im, layer, spectrum_rows, twiddle, table):
    ar, ai = re[0] + re[2], im[0] + im[2]
    br, bi = re[0] - re[2], im[0] - im[2]
    cr, ci = re[1] + re[3], im[1] + im[3]
    dr, di = re[1] - re[3], im[1] - im[3]
    outs = [
        (ar + cr, ai + ci),
        (br + di, bi - dr),
        (ar - cr, ai - ci),
        (br - di, bi + dr),
    ]
    rows = []
    for k1, (r, m) in enumerate(outs):
        if k1:
            c, s = twisted(twiddle, "plain", k1)
            r, m = r * c + m * s, m * c - r * s
        rows.append(jnp.concatenate([r, m], axis=1).astype(BF))
    z = jnp.dot(jnp.concatenate(rows, axis=0), table[...], preferred_element_type=F32)
    spectrum = []
    size = re[0].shape[0]
    for k1 in range(4):
        zr, zi = z[size * k1 : size * k1 + size, :Q], z[size * k1 : size * k1 + size, Q:]
        hr = spectrum_rows[layer : layer + 1, Q * k1 : Q * k1 + Q]
        hi = spectrum_rows[layer + 4 : layer + 5, Q * k1 : Q * k1 + Q]
        spectrum.append(((zr * hr - zi * hi).astype(BF), (zr * hi + zi * hr).astype(BF)))
    return spectrum


def inverse(spectrum, order, twiddle, table):
    stacked = jnp.concatenate([jnp.concatenate(s, axis=1) for s in spectrum], axis=0)
    y = jnp.dot(stacked, table[...], preferred_element_type=F32)
    outs = []
    size = spectrum[0][0].shape[0]
    for k1 in range(4):
        r, m = y[size * k1 : size * k1 + size, :Q], y[size * k1 : size * k1 + size, Q:]
        if k1:
            c, s = twisted(twiddle, order, k1)
            r, m = r * c - m * s, m * c + r * s
        outs.append((r, m))
    (r0, i0), (r1, i1), (r2, i2), (r3, i3) = outs
    ar, ai, br, bi = r0 + r2, i0 + i2, r0 - r2, i0 - i2
    cr, ci, dr, di = r1 + r3, i1 + i3, r1 - r3, i1 - i3
    re = [ar + cr, br - di, ar - cr, br + di]
    im = [ai + ci, bi + dr, ai - ci, bi - dr]
    return re, im


def sent(spectrum, twiddle, table, out):
    for n1, (r, m) in enumerate(zip(*inverse(spectrum, "send", twiddle, table))):
        x = jnp.concatenate([r[:, :128], m[:, :128], r[:, 128:], m[:, 128:]], axis=0)
        x = x.T.astype(BF).reshape(8, 16, 128)
        for base in range(0, out.shape[0], 32):
            out[base + 8 * n1 : base + 8 * n1 + 8, 0:16, :] = x


def through_screen(re, im, phase):
    cos, sin = sincos(phase)
    out_re, out_im = [], []
    for r, m, c, s in zip(re, im, quarters(cos), quarters(sin)):
        out_re.append(r * c - m * s)
        out_im.append(r * s + m * c)
    return out_re, out_im


def payload_kernel(
    distance, far_screens, launch, far_targets, far_counts, far_table,
    shared, held, picks, table, twiddle,
    screens, targets, counts, sems,
):
    group = lax.axis_index("layer")
    copies = [
        pltpu.make_async_copy(source, target, sems.at[i])
        for i, (source, target) in enumerate([
            (far_screens, screens), (far_targets, targets), (far_counts, counts),
            (launch.at[group % 2], held), (far_table, table),
        ])
    ]
    for copy in copies:
        copy.start()
    d = jnp.full((32, 128), distance[0], F32)
    high = d.astype(BF).astype(F32)
    middle = (d - high).astype(BF).astype(F32)
    low = (d - high) - middle
    row = lax.broadcasted_iota(jnp.int32, (32, 128), 0)
    tail = jnp.where(row == 0, high, jnp.where(row == 1, middle, jnp.where(row == 2, low, 0.0)))
    tail = tail.astype(BF)
    twiddles(twiddle)
    for copy in copies[:3]:
        copy.wait()
    phase = screens[0].astype(BF)
    for other in range(4):
        shared[other, :, 0:N] = phase
        shared[other, :, N : N + 128] = tail
    picks[...] = jnp.where(group < counts[...], targets[...], -1)
    for copy in copies[3:]:
        copy.wait()


def first_kernel(held, shared, twiddle, table, far_send, out, h, send, sem):
    copy = pltpu.make_async_copy(far_send, send, sem)
    copy.start()
    spectra(shared, h)
    re, im = quarters(held[0].astype(F32)), quarters(held[1].astype(F32))
    re, im = through_screen(re, im, shared[0, :, 0:N].astype(F32))
    spectrum = forward(re, im, 0, h, twiddle, table)
    copy.wait()
    sent(spectrum, twiddle, send, out)
    both = jnp.concatenate([shared[1, :, 0:N], shared[3, :, 0:N]], axis=0).astype(F32)
    for block in range(8):
        piece = both[:, 128 * block : 128 * block + 128].T.reshape(4, 2, 16, 64)
        out[4 * block : 4 * block + 4, 16:32, :] = jnp.concatenate(
            [piece[:, 0], piece[:, 1]], axis=2
        ).astype(BF)


def middle(layer, came, phase, h, twiddle, table, back, send, out):
    re, im = field_of(came)
    spectrum = forward(quarters(re), quarters(im), layer, h, twiddle, table)
    re, im = inverse(spectrum, "plain", twiddle, back)
    re, im = through_screen(re, im, phase)
    sent(forward(re, im, layer + 1, h, twiddle, table), twiddle, send, out)


def column_kernel(layer, came, carried, *rest):
    groups = gathered(carried, 0, 16)
    which = layer // 2
    phase = jnp.concatenate([groups[which], groups[2 + which]], axis=0)
    middle(layer, came, phase, *rest)


def row_kernel(layer, came, shared, *rest):
    middle(layer, came, shared[layer + 1, :, 0:N].astype(F32), *rest)


def last_kernel(
    came, h, twiddle, table, back, back_sub, spots, templates, picks,
    far_pupil, result,
    cells, pupil, sem,
):
    fields = [field_of(came, 0), field_of(came, 32)]
    re, im = [quarters(jnp.concatenate(x, axis=0)) for x in zip(*fields)]
    spectrum = forward(re, im, 3, h, twiddle, table)
    for part, x in enumerate(inverse(spectrum, "sub", twiddle, back_sub)):
        for field in range(2):
            for upper in range(2):
                parts = [
                    x[n1][32 * field + 16 * a : 32 * field + 16 * a + 16,
                          128 * upper : 128 * upper + 128].astype(BF)
                    for a in range(2)
                    for n1 in range(4)
                ]
                for k, piece in enumerate(granules(parts, 16)):
                    row = part * 256 + (upper * 8 + k) * 16
                    cells[row : row + 16, 128 * field : 128 * field + 128] = piece
    re, im = inverse(spectrum, "plain", twiddle, back)
    for n in range(4):
        for field in range(2):
            rows = slice(32 * field, 32 * field + 32)
            pupil[field, 0, :, Q * n : Q * n + Q] = re[n][rows].astype(BF)
            pupil[field, 1, :, Q * n : Q * n + Q] = im[n][rows].astype(BF)
    written = pltpu.make_async_copy(pupil, far_pupil, sem)
    written.start()
    place = lax.broadcasted_iota(jnp.int32, (128, 32), 0)
    chosen = jnp.where(place == picks[...], 1.0, 0.0).astype(F32).T.astype(BF)
    slots = [
        lax.dot_general(
            chosen,
            cells[:, 128 * field : 128 * field + 128],
            (((1,), (1,)), ((), ())),
            preferred_element_type=F32,
        ).astype(BF)
        for field in range(2)
    ]
    spot = jnp.dot(jnp.concatenate(slots, axis=0), spots[...], preferred_element_type=F32)
    intensity = (spot[:, :1024] * spot[:, :1024] + spot[:, 1024:] * spot[:, 1024:]).astype(BF)
    total = lax.dot_general(
        intensity, templates[...], (((1,), (1,)), ((), ())), preferred_element_type=F32
    )
    for field in range(2):
        result[:, 16 * field : 16 * field + 16] = total[32 * field : 32 * field + 32]
    written.wait()


VMEM = pl.BlockSpec(memory_space=pltpu.VMEM)
SMEM = pl.BlockSpec(memory_space=pltpu.SMEM)
FAR = pl.BlockSpec(memory_space=pltpu.HBM)


def call(kernel, shapes, *operands, name=None, **specs):
    return pl.pallas_call(
        kernel,
        out_shape=shapes,
        compiler_params=pltpu.CompilerParams(vmem_limit_bytes=24 * 1024 * 1024),
        name=name,
        **specs,
    )(*operands)


def exchanged(block, axis="strip", groups=None):
    return lax.all_to_all(
        block, axis, split_axis=0, concat_axis=0, tiled=True, axis_index_groups=groups
    )


def per_device(launch, screens, distance, templates, send_table, send_counts):
    tables = {name: jnp.asarray(value) for name, value in angle_tables().items()}
    table, back, send = tables["forward"], tables["plain"], tables["send"]

    payload, held, picks, table, twiddle = call(
        payload_kernel,
        (
            jax.ShapeDtypeStruct((4, 32, N + 128), BF),
            jax.ShapeDtypeStruct(launch.shape[1:], BF),
            jax.ShapeDtypeStruct((1, 32), jnp.int32),
            jax.ShapeDtypeStruct(table.shape, BF),
            jax.ShapeDtypeStruct((24, Q), F32),
        ),
        distance,
        *[
            pltpu.with_memory_space_constraint(x, pltpu.HBM)
            for x in (
                screens, launch, send_table.reshape(1, 32), send_counts, table
            )
        ],
        in_specs=[SMEM] + [FAR] * 5,
        out_specs=(VMEM,) * 5,
        scratch_shapes=[
            pltpu.VMEM(screens.shape, F32),
            pltpu.VMEM((1, 32), jnp.int32),
            pltpu.VMEM((1, 32), jnp.int32),
            pltpu.SemaphoreType.DMA((5,)),
        ],
        name="payload",
    )
    shared = exchanged(payload, "layer")

    wide = jax.ShapeDtypeStruct((32, 32, 128), BF)
    plain = jax.ShapeDtypeStruct((32, 16, 128), BF)
    twice = jax.ShapeDtypeStruct((64, 16, 128), BF)
    pairs = [[32 * group + strip for group in pair for strip in range(32)] for pair in ((0, 1), (2, 3))]
    leaving, h, send = call(
        first_kernel,
        (wide, jax.ShapeDtypeStruct((8, N), F32), jax.ShapeDtypeStruct(send.shape, BF)),
        held, shared, twiddle, table, pltpu.with_memory_space_constraint(send, pltpu.HBM),
        in_specs=[VMEM] * 4 + [FAR],
        out_specs=(VMEM,) * 3,
        scratch_shapes=[pltpu.SemaphoreType.DMA],
        name="rows0",
    )
    carried = exchanged(leaving)

    def columns(layer, came, shape, name):
        def kernel(*refs):
            column_kernel(layer, *refs)

        return call(kernel, shape, came, carried, h, twiddle, table, back, send, name=name)

    def rows(layer, came, name):
        def kernel(*refs):
            row_kernel(layer, *refs)

        return call(kernel, plain, came, shared, h, twiddle, table, back, send, name=name)

    came = exchanged(columns(0, carried, plain, "columns01"))
    came = exchanged(rows(1, came, "rows12"))
    came = exchanged(columns(2, came, twice, "columns23"), ("layer", "strip"), pairs)

    spots = jnp.asarray(spot_table())
    pupil, result = call(
        last_kernel,
        (jax.ShapeDtypeStruct(launch.shape, BF), jax.ShapeDtypeStruct((32, 32), F32)),
        came, h, twiddle, table, back, tables["sub"], spots, templates.T, picks,
        in_specs=[VMEM] * 9,
        out_specs=(FAR, VMEM),
        scratch_shapes=[
            pltpu.VMEM((512, 256), BF),
            pltpu.VMEM(launch.shape, BF),
            pltpu.SemaphoreType.DMA,
        ],
        name="rows3",
    )
    return (pupil, exchanged(result).reshape(1, 32, 1, 2, 16))


def solution(mesh):
    placed = (
        P(None, None, "strip", None),
        P("layer", "strip", None),
        P("layer"),
        P(),
        P("strip", None, "layer"),
        P("strip", None),
    )
    return jax.shard_map(
        per_device,
        mesh=mesh,
        in_specs=placed,
        out_specs=(P(None, None, "strip", None), P("strip", None, "layer", None, None)),
        check_vma=False,
    )
```

```python
import math

import jax
import jax.numpy as jnp
import numpy as np
from jax import lax
from jax.experimental import pallas as pl
from jax.experimental.pallas import tpu as pltpu
from jax.sharding import PartitionSpec as P

N = 1024
Q = 256
SUB = 16
SPOT = 2 * SUB
BF = jnp.bfloat16
F32 = jnp.float32


def bf16(table):
    return np.asarray(table, np.float32).astype(jnp.bfloat16)


ORDERS = {
    "plain": lambda at: at,
    "send": lambda at: (at % 128) // 16 * 32 + at // 128 * 16 + at % 16,
    "sub": lambda at: at % SUB * SUB + at // SUB,
}


def angle_tables():
    n = np.arange(Q)
    turn = 2.0 * np.pi * ((n[:, None] * n[None, :]) % Q) / Q
    cos, sin = np.cos(turn) / 16.0, np.sin(turn) / 16.0
    forward = np.block([[cos, -sin], [sin, cos]])
    inverse = np.block([[cos, sin], [-sin, cos]])
    tables = {"forward": bf16(forward)}
    for name, order in ORDERS.items():
        tables[name] = bf16(inverse[:, np.concatenate([order(n), Q + order(n)])])
    return tables


def spot_table():
    turn = 2.0 * np.pi * ((np.arange(SPOT)[:, None] * np.arange(SUB)[None, :]) % SPOT) / SPOT
    wave = (np.cos(turn) - 1j * np.sin(turn)) / math.sqrt(SUB)
    kron = wave[:, None, None, :] * wave[None, :, :, None]
    kron = kron.reshape(SPOT * SPOT, SUB * SUB)
    return bf16(np.block([[kron.real, -kron.imag], [kron.imag, kron.real]]).T)


def sincos(x):
    y = 0.5 * x
    z = y * y
    s = 2.6048728614114225e-06
    for a in (-0.0001980891975108534, 0.008333048783242702, -0.16666658222675323, 1.0):
        s = s * z + a
    s = s * y
    c = 2.3149976186687127e-05
    for a in (-0.0013853529235348105, 0.04166356101632118, -0.4999990463256836, 0.9999999403953552):
        c = c * z + a
    t = s + s
    return 1.0 - t * s, t * c


def twiddles(out):
    k1 = lax.broadcasted_iota(jnp.int32, (4, Q), 0)
    at = lax.broadcasted_iota(jnp.int32, (4, Q), 1)
    for i, order in enumerate(ORDERS.values()):
        turns = (k1 * order(at)).astype(F32) * (1.0 / N)
        turns = jnp.where(turns > 0.5, turns - 1.0, turns)
        out[8 * i : 8 * i + 4, :], out[8 * i + 4 : 8 * i + 8, :] = sincos(turns * (2.0 * math.pi))


def spectra(shared, out):
    d = []
    for layer in range(4):
        tail = shared[layer, 0:16, N : N + 128].astype(F32)
        d.append((tail[0:1] + tail[1:2]) + tail[2:3])
    d = jnp.concatenate([jnp.concatenate(d, axis=0)] * (N // 128), axis=1)
    place = lax.broadcasted_iota(jnp.int32, (4, N), 1)
    k = 4 * (place % Q) + place // Q
    m = jnp.where(k < N // 2, k, k - N).astype(F32)
    turns = d * (m * m * (0.5 / (N * N)))
    frac = turns - jnp.floor(turns + 0.5)
    cos, sin = sincos(frac * (2.0 * math.pi))
    out[0:4, :], out[4:8, :] = 0.25 * cos, -0.25 * sin


def twisted(twiddle, order, k1):
    row = 8 * list(ORDERS).index(order) + k1
    return twiddle[row : row + 1, :], twiddle[row + 4 : row + 5, :]


def granules(parts, width):
    parts = list(parts)
    lane = lax.broadcasted_iota(jnp.int32, parts[0].shape, 1) // width
    bit = 1
    while bit < len(parts):
        high = (lane & bit) != 0
        for i in range(len(parts)):
            if i & bit:
                continue
            a, b = parts[i], parts[i | bit]
            parts[i] = jnp.where(high, pltpu.roll(b, width * bit, 1), a)
            parts[i | bit] = jnp.where(high, b, pltpu.roll(a, 128 - width * bit, 1))
        bit *= 2
    return parts


def gathered(block, base, first):
    columns = []
    for start in range(base, base + 32, 4):
        parts = [block[start + t, first : first + 16, :] for t in range(4)]
        columns.append(granules(parts, 32))
    return [jnp.concatenate([c[g] for c in columns], axis=1).astype(F32) for g in range(4)]


def field_of(block, base=0):
    groups = gathered(block, base, 0)
    return (
        jnp.concatenate([groups[0], groups[2]], axis=0),
        jnp.concatenate([groups[1], groups[3]], axis=0),
    )


def quarters(x):
    return [x[:, Q * n : Q * n + Q] for n in range(4)]


def forward(re, im, layer, spectrum_rows, twiddle, table):
    ar, ai = re[0] + re[2], im[0] + im[2]
    br, bi = re[0] - re[2], im[0] - im[2]
    cr, ci = re[1] + re[3], im[1] + im[3]
    dr, di = re[1] - re[3], im[1] - im[3]
    outs = [
        (ar + cr, ai + ci),
        (br + di, bi - dr),
        (ar - cr, ai - ci),
        (br - di, bi + dr),
    ]
    rows = []
    for k1, (r, m) in enumerate(outs):
        if k1:
            c, s = twisted(twiddle, "plain", k1)
            r, m = r * c + m * s, m * c - r * s
        rows.append(jnp.concatenate([r, m], axis=1).astype(BF))
    z = jnp.dot(jnp.concatenate(rows, axis=0), table[...], preferred_element_type=F32)
    spectrum = []
    size = re[0].shape[0]
    for k1 in range(4):
        zr, zi = z[size * k1 : size * k1 + size, :Q], z[size * k1 : size * k1 + size, Q:]
        hr = spectrum_rows[layer : layer + 1, Q * k1 : Q * k1 + Q]
        hi = spectrum_rows[layer + 4 : layer + 5, Q * k1 : Q * k1 + Q]
        spectrum.append(((zr * hr - zi * hi).astype(BF), (zr * hi + zi * hr).astype(BF)))
    return spectrum


def inverse(spectrum, order, twiddle, table):
    stacked = jnp.concatenate([jnp.concatenate(s, axis=1) for s in spectrum], axis=0)
    y = jnp.dot(stacked, table[...], preferred_element_type=F32)
    outs = []
    size = spectrum[0][0].shape[0]
    for k1 in range(4):
        r, m = y[size * k1 : size * k1 + size, :Q], y[size * k1 : size * k1 + size, Q:]
        if k1:
            c, s = twisted(twiddle, order, k1)
            r, m = r * c - m * s, m * c + r * s
        outs.append((r, m))
    (r0, i0), (r1, i1), (r2, i2), (r3, i3) = outs
    ar, ai, br, bi = r0 + r2, i0 + i2, r0 - r2, i0 - i2
    cr, ci, dr, di = r1 + r3, i1 + i3, r1 - r3, i1 - i3
    re = [ar + cr, br - di, ar - cr, br + di]
    im = [ai + ci, bi + dr, ai - ci, bi - dr]
    return re, im


def sent(spectrum, twiddle, table, out, turned=F32):
    for n1, (r, m) in enumerate(zip(*inverse(spectrum, "send", twiddle, table))):
        x = jnp.concatenate([r[:, :128], m[:, :128], r[:, 128:], m[:, 128:]], axis=0)
        x = x.astype(turned).T.astype(BF).reshape(8, 16, 128)
        for base in range(0, out.shape[0], 32):
            out[base + 8 * n1 : base + 8 * n1 + 8, 0:16, :] = x


def through_screen(re, im, phase):
    cos, sin = sincos(phase)
    out_re, out_im = [], []
    for r, m, c, s in zip(re, im, quarters(cos), quarters(sin)):
        out_re.append(r * c - m * s)
        out_im.append(r * s + m * c)
    return out_re, out_im


def payload_kernel(
    distance, far_screens, launch, far_targets, far_counts, far_table, far_send,
    shared, held, picks, table, send, twiddle,
    screens, targets, counts, sems,
):
    group = lax.axis_index("layer")
    copies = [
        pltpu.make_async_copy(source, target, sems.at[i])
        for i, (source, target) in enumerate([
            (far_screens, screens), (far_targets, targets), (far_counts, counts),
            (launch.at[group % 2], held), (far_table, table), (far_send, send),
        ])
    ]
    for copy in copies:
        copy.start()
    d = jnp.full((32, 128), distance[0], F32)
    high = d.astype(BF).astype(F32)
    middle = (d - high).astype(BF).astype(F32)
    low = (d - high) - middle
    row = lax.broadcasted_iota(jnp.int32, (32, 128), 0)
    tail = jnp.where(row == 0, high, jnp.where(row == 1, middle, jnp.where(row == 2, low, 0.0)))
    tail = tail.astype(BF)
    twiddles(twiddle)
    for copy in copies[:3]:
        copy.wait()
    phase = screens[0].astype(BF)
    for other in range(4):
        shared[other, :, 0:N] = phase
        shared[other, :, N : N + 128] = tail
    picks[...] = jnp.where(group < counts[...], targets[...], -1)
    for copy in copies[3:]:
        copy.wait()


def first_kernel(held, shared, twiddle, table, send, out, h):
    spectra(shared, h)
    re, im = quarters(held[0].astype(F32)), quarters(held[1].astype(F32))
    re, im = through_screen(re, im, shared[0, :, 0:N].astype(F32))
    sent(forward(re, im, 0, h, twiddle, table), twiddle, send, out)
    both = jnp.concatenate([shared[1, :, 0:N], shared[3, :, 0:N]], axis=0).astype(F32)
    for block in range(8):
        piece = both[:, 128 * block : 128 * block + 128].T.reshape(4, 2, 16, 64)
        out[4 * block : 4 * block + 4, 16:32, :] = jnp.concatenate(
            [piece[:, 0], piece[:, 1]], axis=2
        ).astype(BF)


def middle(layer, came, phase, h, twiddle, table, back, send, out):
    re, im = field_of(came)
    spectrum = forward(quarters(re), quarters(im), layer, h, twiddle, table)
    re, im = inverse(spectrum, "plain", twiddle, back)
    re, im = through_screen(re, im, phase)
    sent(forward(re, im, layer + 1, h, twiddle, table), twiddle, send, out, BF)


def column_kernel(layer, came, carried, *rest):
    groups = gathered(carried, 0, 16)
    which = layer // 2
    phase = jnp.concatenate([groups[which], groups[2 + which]], axis=0)
    middle(layer, came, phase, *rest)


def row_kernel(layer, came, shared, *rest):
    middle(layer, came, shared[layer + 1, :, 0:N].astype(F32), *rest)


def last_kernel(
    came, h, twiddle, table, back, back_sub, spots, templates, picks,
    far_pupil, result,
    cells, pupil, sem,
):
    fields = [field_of(came, 0), field_of(came, 32)]
    re, im = [quarters(jnp.concatenate(x, axis=0)) for x in zip(*fields)]
    spectrum = forward(re, im, 3, h, twiddle, table)
    for part, x in enumerate(inverse(spectrum, "sub", twiddle, back_sub)):
        for field in range(2):
            for upper in range(2):
                parts = [
                    x[n1][32 * field + 16 * a : 32 * field + 16 * a + 16,
                          128 * upper : 128 * upper + 128].astype(BF)
                    for a in range(2)
                    for n1 in range(4)
                ]
                for k, piece in enumerate(granules(parts, 16)):
                    row = part * 256 + (upper * 8 + k) * 16
                    cells[row : row + 16, 128 * field : 128 * field + 128] = piece
    re, im = inverse(spectrum, "plain", twiddle, back)
    for n in range(4):
        for field in range(2):
            rows = slice(32 * field, 32 * field + 32)
            pupil[field, 0, :, Q * n : Q * n + Q] = re[n][rows].astype(BF)
            pupil[field, 1, :, Q * n : Q * n + Q] = im[n][rows].astype(BF)
    written = pltpu.make_async_copy(pupil, far_pupil, sem)
    written.start()
    place = lax.broadcasted_iota(jnp.int32, (128, 32), 0)
    chosen = jnp.where(place == picks[...], 1.0, 0.0).astype(F32).T.astype(BF)
    slots = [
        lax.dot_general(
            chosen,
            cells[:, 128 * field : 128 * field + 128],
            (((1,), (1,)), ((), ())),
            preferred_element_type=F32,
        ).astype(BF)
        for field in range(2)
    ]
    spot = jnp.dot(jnp.concatenate(slots, axis=0), spots[...], preferred_element_type=F32)
    intensity = (spot[:, :1024] * spot[:, :1024] + spot[:, 1024:] * spot[:, 1024:]).astype(BF)
    total = lax.dot_general(
        intensity, templates[...], (((1,), (1,)), ((), ())), preferred_element_type=F32
    )
    for field in range(2):
        result[:, 16 * field : 16 * field + 16] = total[32 * field : 32 * field + 32]
    written.wait()


VMEM = pl.BlockSpec(memory_space=pltpu.VMEM)
SMEM = pl.BlockSpec(memory_space=pltpu.SMEM)
FAR = pl.BlockSpec(memory_space=pltpu.HBM)


def call(kernel, shapes, *operands, name=None, **specs):
    return pl.pallas_call(
        kernel,
        out_shape=shapes,
        compiler_params=pltpu.CompilerParams(vmem_limit_bytes=24 * 1024 * 1024),
        name=name,
        **specs,
    )(*operands)


def exchanged(block, axis="strip", groups=None):
    return lax.all_to_all(
        block, axis, split_axis=0, concat_axis=0, tiled=True, axis_index_groups=groups
    )


def per_device(launch, screens, distance, templates, send_table, send_counts):
    tables = {name: jnp.asarray(value) for name, value in angle_tables().items()}
    table, back, send = tables["forward"], tables["plain"], tables["send"]

    payload, held, picks, table, send, twiddle = call(
        payload_kernel,
        (
            jax.ShapeDtypeStruct((4, 32, N + 128), BF),
            jax.ShapeDtypeStruct(launch.shape[1:], BF),
            jax.ShapeDtypeStruct((1, 32), jnp.int32),
            jax.ShapeDtypeStruct(table.shape, BF),
            jax.ShapeDtypeStruct(send.shape, BF),
            jax.ShapeDtypeStruct((24, Q), F32),
        ),
        distance,
        *[
            pltpu.with_memory_space_constraint(x, pltpu.HBM)
            for x in (
                screens, launch, send_table.reshape(1, 32), send_counts, table, send
            )
        ],
        in_specs=[SMEM] + [FAR] * 6,
        out_specs=(VMEM,) * 6,
        scratch_shapes=[
            pltpu.VMEM(screens.shape, F32),
            pltpu.VMEM((1, 32), jnp.int32),
            pltpu.VMEM((1, 32), jnp.int32),
            pltpu.SemaphoreType.DMA((6,)),
        ],
        name="payload",
    )
    shared = exchanged(payload, "layer")

    wide = jax.ShapeDtypeStruct((32, 32, 128), BF)
    plain = jax.ShapeDtypeStruct((32, 16, 128), BF)
    twice = jax.ShapeDtypeStruct((64, 16, 128), BF)
    pairs = [[32 * group + strip for group in pair for strip in range(32)] for pair in ((0, 1), (2, 3))]
    leaving, h = call(
        first_kernel, (wide, jax.ShapeDtypeStruct((8, N), F32)),
        held, shared, twiddle, table, send, name="rows0",
    )
    carried = exchanged(leaving)

    def columns(layer, came, shape, name):
        def kernel(*refs):
            column_kernel(layer, *refs)

        return call(kernel, shape, came, carried, h, twiddle, table, back, send, name=name)

    def rows(layer, came, name):
        def kernel(*refs):
            row_kernel(layer, *refs)

        return call(kernel, plain, came, shared, h, twiddle, table, back, send, name=name)

    came = exchanged(columns(0, carried, plain, "columns01"))
    came = exchanged(rows(1, came, "rows12"))
    came = exchanged(columns(2, came, twice, "columns23"), ("layer", "strip"), pairs)

    spots = jnp.asarray(spot_table())
    pupil, result = call(
        last_kernel,
        (jax.ShapeDtypeStruct(launch.shape, BF), jax.ShapeDtypeStruct((32, 32), F32)),
        came, h, twiddle, table, back, tables["sub"], spots, templates.T, picks,
        in_specs=[VMEM] * 9,
        out_specs=(FAR, VMEM),
        scratch_shapes=[
            pltpu.VMEM((512, 256), BF),
            pltpu.VMEM(launch.shape, BF),
            pltpu.SemaphoreType.DMA,
        ],
        name="rows3",
    )
    return (pupil, exchanged(result).reshape(1, 32, 1, 2, 16))


def solution(mesh):
    placed = (
        P(None, None, "strip", None),
        P("layer", "strip", None),
        P("layer"),
        P(),
        P("strip", None, "layer"),
        P("strip", None),
    )
    return jax.shard_map(
        per_device,
        mesh=mesh,
        in_specs=placed,
        out_specs=(P(None, None, "strip", None), P("strip", None, "layer", None, None)),
        check_vma=False,
    )
```

```python
import math

import jax
import jax.numpy as jnp
import numpy as np
from jax import lax
from jax.experimental import pallas as pl
from jax.experimental.pallas import tpu as pltpu
from jax.sharding import PartitionSpec as P

N = 1024
Q = 256
SUB = 16
SPOT = 2 * SUB
BF = jnp.bfloat16
F32 = jnp.float32


def bf16(table):
    return np.asarray(table, np.float32).astype(jnp.bfloat16)


ORDERS = {
    "plain": lambda at: at,
    "send": lambda at: (at % 128) // 16 * 32 + at // 128 * 16 + at % 16,
    "sub": lambda at: at % SUB * SUB + at // SUB,
}


def angle_tables():
    n = np.arange(Q)
    turn = 2.0 * np.pi * ((n[:, None] * n[None, :]) % Q) / Q
    cos, sin = np.cos(turn) / 16.0, np.sin(turn) / 16.0
    forward = np.block([[cos, -sin], [sin, cos]])
    inverse = np.block([[cos, sin], [-sin, cos]])
    tables = {"forward": bf16(forward)}
    for name, order in ORDERS.items():
        tables[name] = bf16(inverse[:, np.concatenate([order(n), Q + order(n)])])
    return tables


def spot_table():
    turn = 2.0 * np.pi * ((np.arange(SPOT)[:, None] * np.arange(SUB)[None, :]) % SPOT) / SPOT
    wave = (np.cos(turn) - 1j * np.sin(turn)) / math.sqrt(SUB)
    kron = wave[:, None, None, :] * wave[None, :, :, None]
    kron = kron.reshape(SPOT * SPOT, SUB * SUB)
    return bf16(np.block([[kron.real, -kron.imag], [kron.imag, kron.real]]).T)


def sincos(x):
    y = 0.5 * x
    z = y * y
    s = 2.6048728614114225e-06
    for a in (-0.0001980891975108534, 0.008333048783242702, -0.16666658222675323, 1.0):
        s = s * z + a
    s = s * y
    c = 2.3149976186687127e-05
    for a in (-0.0013853529235348105, 0.04166356101632118, -0.4999990463256836, 0.9999999403953552):
        c = c * z + a
    t = s + s
    return 1.0 - t * s, t * c


def twiddles(out):
    k1 = lax.broadcasted_iota(jnp.int32, (4, Q), 0)
    at = lax.broadcasted_iota(jnp.int32, (4, Q), 1)
    for i, order in enumerate(ORDERS.values()):
        turns = (k1 * order(at)).astype(F32) * (1.0 / N)
        turns = jnp.where(turns > 0.5, turns - 1.0, turns)
        out[8 * i : 8 * i + 4, :], out[8 * i + 4 : 8 * i + 8, :] = sincos(turns * (2.0 * math.pi))


def spectra(shared, out):
    d = []
    for layer in range(4):
        tail = shared[layer, 0:16, N : N + 128].astype(F32)
        d.append((tail[0:1] + tail[1:2]) + tail[2:3])
    d = jnp.concatenate([jnp.concatenate(d, axis=0)] * (N // 128), axis=1)
    place = lax.broadcasted_iota(jnp.int32, (4, N), 1)
    k = 4 * (place % Q) + place // Q
    m = jnp.where(k < N // 2, k, k - N).astype(F32)
    turns = d * (m * m * (0.5 / (N * N)))
    frac = turns - jnp.floor(turns + 0.5)
    cos, sin = sincos(frac * (2.0 * math.pi))
    out[0:4, :], out[4:8, :] = 0.25 * cos, -0.25 * sin


def twisted(twiddle, order, k1):
    row = 8 * list(ORDERS).index(order) + k1
    return twiddle[row : row + 1, :], twiddle[row + 4 : row + 5, :]


def granules(parts, width):
    parts = list(parts)
    lane = lax.broadcasted_iota(jnp.int32, parts[0].shape, 1) // width
    bit = 1
    while bit < len(parts):
        high = (lane & bit) != 0
        for i in range(len(parts)):
            if i & bit:
                continue
            a, b = parts[i], parts[i | bit]
            parts[i] = jnp.where(high, pltpu.roll(b, width * bit, 1), a)
            parts[i | bit] = jnp.where(high, b, pltpu.roll(a, 128 - width * bit, 1))
        bit *= 2
    return parts


def gathered(block, base, first):
    columns = []
    for start in range(base, base + 32, 4):
        parts = [block[start + t, first : first + 16, :] for t in range(4)]
        columns.append(granules(parts, 32))
    return [jnp.concatenate([c[g] for c in columns], axis=1).astype(F32) for g in range(4)]


def field_of(block, base=0):
    groups = gathered(block, base, 0)
    return (
        jnp.concatenate([groups[0], groups[2]], axis=0),
        jnp.concatenate([groups[1], groups[3]], axis=0),
    )


def quarters(x):
    return [x[:, Q * n : Q * n + Q] for n in range(4)]


def forward(re, im, layer, spectrum_rows, twiddle, table):
    ar, ai = re[0] + re[2], im[0] + im[2]
    br, bi = re[0] - re[2], im[0] - im[2]
    cr, ci = re[1] + re[3], im[1] + im[3]
    dr, di = re[1] - re[3], im[1] - im[3]
    outs = [
        (ar + cr, ai + ci),
        (br + di, bi - dr),
        (ar - cr, ai - ci),
        (br - di, bi + dr),
    ]
    rows = []
    for k1, (r, m) in enumerate(outs):
        if k1:
            c, s = twisted(twiddle, "plain", k1)
            r, m = r * c + m * s, m * c - r * s
        rows.append(jnp.concatenate([r, m], axis=1).astype(BF))
    z = jnp.dot(jnp.concatenate(rows, axis=0), table[...], preferred_element_type=F32)
    spectrum = []
    size = re[0].shape[0]
    for k1 in range(4):
        zr, zi = z[size * k1 : size * k1 + size, :Q], z[size * k1 : size * k1 + size, Q:]
        hr = spectrum_rows[layer : layer + 1, Q * k1 : Q * k1 + Q]
        hi = spectrum_rows[layer + 4 : layer + 5, Q * k1 : Q * k1 + Q]
        spectrum.append(((zr * hr - zi * hi).astype(BF), (zr * hi + zi * hr).astype(BF)))
    return spectrum


def inverse(spectrum, order, twiddle, table):
    stacked = jnp.concatenate([jnp.concatenate(s, axis=1) for s in spectrum], axis=0)
    y = jnp.dot(stacked, table[...], preferred_element_type=F32)
    outs = []
    size = spectrum[0][0].shape[0]
    for k1 in range(4):
        r, m = y[size * k1 : size * k1 + size, :Q], y[size * k1 : size * k1 + size, Q:]
        if k1:
            c, s = twisted(twiddle, order, k1)
            r, m = r * c - m * s, m * c + r * s
        outs.append((r, m))
    (r0, i0), (r1, i1), (r2, i2), (r3, i3) = outs
    ar, ai, br, bi = r0 + r2, i0 + i2, r0 - r2, i0 - i2
    cr, ci, dr, di = r1 + r3, i1 + i3, r1 - r3, i1 - i3
    re = [ar + cr, br - di, ar - cr, br + di]
    im = [ai + ci, bi + dr, ai - ci, bi - dr]
    return re, im


def sent(spectrum, twiddle, table, out, turned=F32):
    for n1, (r, m) in enumerate(zip(*inverse(spectrum, "send", twiddle, table))):
        x = jnp.concatenate([r[:, :128], m[:, :128], r[:, 128:], m[:, 128:]], axis=0)
        x = x.astype(turned).T.astype(BF).reshape(8, 16, 128)
        for base in range(0, out.shape[0], 32):
            out[base + 8 * n1 : base + 8 * n1 + 8, 0:16, :] = x


def through_screen(re, im, phase):
    cos, sin = sincos(phase)
    out_re, out_im = [], []
    for r, m, c, s in zip(re, im, quarters(cos), quarters(sin)):
        out_re.append(r * c - m * s)
        out_im.append(r * s + m * c)
    return out_re, out_im


def payload_kernel(
    distance, far_screens, launch, far_targets, far_counts, far_table, far_send,
    shared, held, table, send, twiddle,
    screens, targets, counts, sems,
):
    group = lax.axis_index("layer")
    copies = [
        pltpu.make_async_copy(source, target, sems.at[i])
        for i, (source, target) in enumerate([
            (far_screens, screens), (far_targets, targets), (far_counts, counts),
            (launch.at[group % 2], held), (far_table, table), (far_send, send),
        ])
    ]
    for copy in copies:
        copy.start()
    d = jnp.full((32, 128), distance[0], F32)
    high = d.astype(BF).astype(F32)
    middle = (d - high).astype(BF).astype(F32)
    low = (d - high) - middle
    row = lax.broadcasted_iota(jnp.int32, (32, 128), 0)
    twiddles(twiddle)
    for copy in copies[:3]:
        copy.wait()
    picks = jnp.where(group < counts[...], targets[...], -1).astype(F32)
    picks = jnp.concatenate([picks, jnp.full((1, 96), -1.0, F32)], axis=1)
    tail = jnp.zeros((32, 128), F32)
    for i, value in enumerate((high, middle, low, picks)):
        tail = jnp.where(row == i, value, tail)
    tail = tail.astype(BF)
    phase = screens[0].astype(BF)
    for other in range(4):
        shared[other, :, 0:N] = phase
        shared[other, :, N : N + 128] = tail
    for copy in copies[3:]:
        copy.wait()


def first_kernel(held, shared, twiddle, table, send, out, h):
    spectra(shared, h)
    re, im = quarters(held[0].astype(F32)), quarters(held[1].astype(F32))
    re, im = through_screen(re, im, shared[0, :, 0:N].astype(F32))
    sent(forward(re, im, 0, h, twiddle, table), twiddle, send, out)
    both = jnp.concatenate([shared[1, :, 0:N], shared[3, :, 0:N]], axis=0).astype(F32)
    for block in range(8):
        piece = both[:, 128 * block : 128 * block + 128].T.reshape(4, 2, 16, 64)
        out[4 * block : 4 * block + 4, 16:32, :] = jnp.concatenate(
            [piece[:, 0], piece[:, 1]], axis=2
        ).astype(BF)


def middle(layer, came, phase, h, twiddle, table, back, send, out):
    re, im = field_of(came)
    spectrum = forward(quarters(re), quarters(im), layer, h, twiddle, table)
    re, im = inverse(spectrum, "plain", twiddle, back)
    re, im = through_screen(re, im, phase)
    sent(forward(re, im, layer + 1, h, twiddle, table), twiddle, send, out, BF)


def column_kernel(layer, came, carried, *rest):
    groups = gathered(carried, 0, 16)
    which = layer // 2
    phase = jnp.concatenate([groups[which], groups[2 + which]], axis=0)
    middle(layer, came, phase, *rest)


def row_kernel(layer, came, shared, *rest):
    middle(layer, came, shared[layer + 1, :, 0:N].astype(F32), *rest)


def last_kernel(
    came, shared, h, twiddle, table, back, back_sub, spots, templates, mine, result, cells
):
    re, im = field_of(came)
    spectrum = forward(quarters(re), quarters(im), 3, h, twiddle, table)
    for part, x in enumerate(inverse(spectrum, "sub", twiddle, back_sub)):
        for upper in range(2):
            parts = [
                x[n1][16 * a : 16 * a + 16, 128 * upper : 128 * upper + 128].astype(BF)
                for a in range(2)
                for n1 in range(4)
            ]
            for k, piece in enumerate(granules(parts, 16)):
                row = part * 256 + (upper * 8 + k) * 16
                cells[row : row + 16, :] = piece
    for part, x in enumerate(inverse(spectrum, "plain", twiddle, back)):
        for n in range(4):
            mine[part, :, Q * n : Q * n + Q] = x[n].astype(BF)
    first = lax.axis_index("layer") // 2 * 2
    picks = [shared[first + i, 0:16, N : N + 128].astype(F32)[3:4, :32] for i in range(2)]
    picks = jnp.concatenate(picks, axis=1)
    place = lax.broadcasted_iota(jnp.int32, (128, 64), 0).astype(F32)
    chosen = jnp.where(place == picks, 1.0, 0.0).astype(F32).T.astype(BF)
    slots = lax.dot_general(
        chosen, cells[...], (((1,), (1,)), ((), ())), preferred_element_type=F32
    ).astype(BF)
    spot = jnp.dot(slots, spots[...], preferred_element_type=F32)
    intensity = (spot[:, :1024] * spot[:, :1024] + spot[:, 1024:] * spot[:, 1024:]).astype(BF)
    result[...] = lax.dot_general(
        intensity, templates[...], (((1,), (1,)), ((), ())), preferred_element_type=F32
    )


def outputs_kernel(mine, other, result, pupil, correlation, turned, sems):
    own = lax.axis_index("layer") % 2
    copies = [
        pltpu.make_async_copy(mine, pupil.at[own], sems.at[0]),
        pltpu.make_async_copy(other, pupil.at[1 - own], sems.at[1]),
    ]
    for copy in copies:
        copy.start()
    for field in range(2):
        turned[field] = result[32 * field : 32 * field + 32, :].T
    copies.append(pltpu.make_async_copy(turned, correlation, sems.at[2]))
    copies[2].start()
    for copy in copies:
        copy.wait()


VMEM = pl.BlockSpec(memory_space=pltpu.VMEM)
SMEM = pl.BlockSpec(memory_space=pltpu.SMEM)
FAR = pl.BlockSpec(memory_space=pltpu.HBM)


def call(kernel, shapes, *operands, name=None, **specs):
    return pl.pallas_call(
        kernel,
        out_shape=shapes,
        compiler_params=pltpu.CompilerParams(vmem_limit_bytes=24 * 1024 * 1024),
        name=name,
        **specs,
    )(*operands)


def exchanged(block, axis="strip", groups=None):
    return lax.all_to_all(
        block, axis, split_axis=0, concat_axis=0, tiled=True, axis_index_groups=groups
    )


def per_device(launch, screens, distance, templates, send_table, send_counts):
    tables = {name: jnp.asarray(value) for name, value in angle_tables().items()}
    table, back, send = tables["forward"], tables["plain"], tables["send"]

    payload, held, table, send, twiddle = call(
        payload_kernel,
        (
            jax.ShapeDtypeStruct((4, 32, N + 128), BF),
            jax.ShapeDtypeStruct(launch.shape[1:], BF),
            jax.ShapeDtypeStruct(table.shape, BF),
            jax.ShapeDtypeStruct(send.shape, BF),
            jax.ShapeDtypeStruct((24, Q), F32),
        ),
        distance,
        *[
            pltpu.with_memory_space_constraint(x, pltpu.HBM)
            for x in (
                screens, launch, send_table.reshape(1, 32), send_counts, table, send
            )
        ],
        in_specs=[SMEM] + [FAR] * 6,
        out_specs=(VMEM,) * 5,
        scratch_shapes=[
            pltpu.VMEM(screens.shape, F32),
            pltpu.VMEM((1, 32), jnp.int32),
            pltpu.VMEM((1, 32), jnp.int32),
            pltpu.SemaphoreType.DMA((6,)),
        ],
        name="payload",
    )
    shared = exchanged(payload, "layer")

    wide = jax.ShapeDtypeStruct((32, 32, 128), BF)
    plain = jax.ShapeDtypeStruct((32, 16, 128), BF)
    pairs = [[32 * group + strip for group in pair for strip in range(32)] for pair in ((0, 1), (2, 3))]
    leaving, h = call(
        first_kernel, (wide, jax.ShapeDtypeStruct((8, N), F32)),
        held, shared, twiddle, table, send, name="rows0",
    )
    carried = exchanged(leaving)

    def columns(layer, came, name):
        def kernel(*refs):
            column_kernel(layer, *refs)

        return call(kernel, plain, came, carried, h, twiddle, table, back, send, name=name)

    def rows(layer, came, name):
        def kernel(*refs):
            row_kernel(layer, *refs)

        return call(kernel, plain, came, shared, h, twiddle, table, back, send, name=name)

    came = exchanged(columns(0, carried, "columns01"))
    came = exchanged(rows(1, came, "rows12"))
    came = exchanged(columns(2, came, "columns23"))

    spots = jnp.asarray(spot_table())
    mine, result = call(
        last_kernel,
        (jax.ShapeDtypeStruct(launch.shape[1:], BF), jax.ShapeDtypeStruct((64, 16), F32)),
        came, shared, h, twiddle, table, back, tables["sub"], spots, templates.T,
        scratch_shapes=[pltpu.VMEM((512, 128), BF)],
        name="rows3",
    )
    other = lax.ppermute(mine, "layer", [(0, 1), (1, 0), (2, 3), (3, 2)])
    result = exchanged(result, ("layer", "strip"), pairs)
    pupil, correlation = call(
        outputs_kernel,
        (jax.ShapeDtypeStruct(launch.shape, BF), jax.ShapeDtypeStruct((2, 16, 32), F32)),
        mine, other, result,
        in_specs=[VMEM] * 3,
        out_specs=(FAR, FAR),
        scratch_shapes=[pltpu.VMEM((2, 16, 32), F32), pltpu.SemaphoreType.DMA((3,))],
        name="outputs",
    )
    return (pupil, correlation.transpose(2, 0, 1)[None, :, None])


def solution(mesh):
    placed = (
        P(None, None, "strip", None),
        P("layer", "strip", None),
        P("layer"),
        P(),
        P("strip", None, "layer"),
        P("strip", None),
    )
    return jax.shard_map(
        per_device,
        mesh=mesh,
        in_specs=placed,
        out_specs=(P(None, None, "strip", None), P("strip", None, "layer", None, None)),
        check_vma=False,
    )
```

```python
import math

import jax
import jax.numpy as jnp
import numpy as np
from jax import lax
from jax.experimental import pallas as pl
from jax.experimental.pallas import tpu as pltpu
from jax.sharding import PartitionSpec as P

N = 1024
Q = 256
SUB = 16
SPOT = 2 * SUB
BF = jnp.bfloat16
F32 = jnp.float32


def bf16(table):
    return np.asarray(table, np.float32).astype(jnp.bfloat16)


ORDERS = {
    "plain": lambda at: at,
    "send": lambda at: (at % 128) // 16 * 32 + at // 128 * 16 + at % 16,
    "sub": lambda at: at % SUB * SUB + at // SUB,
}


def angle_tables():
    n = np.arange(Q)
    turn = 2.0 * np.pi * ((n[:, None] * n[None, :]) % Q) / Q
    cos, sin = np.cos(turn) / 16.0, np.sin(turn) / 16.0
    forward = np.block([[cos, -sin], [sin, cos]])
    inverse = np.block([[cos, sin], [-sin, cos]])
    tables = {"forward": bf16(forward)}
    for name, order in ORDERS.items():
        tables[name] = bf16(inverse[:, np.concatenate([order(n), Q + order(n)])])
    return tables


def spot_table():
    turn = 2.0 * np.pi * ((np.arange(SPOT)[:, None] * np.arange(SUB)[None, :]) % SPOT) / SPOT
    wave = (np.cos(turn) - 1j * np.sin(turn)) / math.sqrt(SUB)
    kron = wave[:, None, None, :] * wave[None, :, :, None]
    kron = kron.reshape(SPOT * SPOT, SUB * SUB)
    return bf16(np.block([[kron.real, -kron.imag], [kron.imag, kron.real]]).T)


def sincos(x):
    y = 0.5 * x
    z = y * y
    s = 2.6048728614114225e-06
    for a in (-0.0001980891975108534, 0.008333048783242702, -0.16666658222675323, 1.0):
        s = s * z + a
    s = s * y
    c = 2.3149976186687127e-05
    for a in (-0.0013853529235348105, 0.04166356101632118, -0.4999990463256836, 0.9999999403953552):
        c = c * z + a
    t = s + s
    return 1.0 - t * s, t * c


def twiddles(out):
    k1 = lax.broadcasted_iota(jnp.int32, (4, Q), 0)
    at = lax.broadcasted_iota(jnp.int32, (4, Q), 1)
    for i, order in enumerate(ORDERS.values()):
        turns = (k1 * order(at)).astype(F32) * (1.0 / N)
        turns = jnp.where(turns > 0.5, turns - 1.0, turns)
        out[8 * i : 8 * i + 4, :], out[8 * i + 4 : 8 * i + 8, :] = sincos(turns * (2.0 * math.pi))


def spectra(shared, out):
    d = []
    for layer in range(4):
        tail = shared[layer, 0:16, N : N + 128].astype(F32)
        d.append((tail[0:1] + tail[1:2]) + tail[2:3])
    d = jnp.concatenate([jnp.concatenate(d, axis=0)] * (N // 128), axis=1)
    place = lax.broadcasted_iota(jnp.int32, (4, N), 1)
    k = 4 * (place % Q) + place // Q
    m = jnp.where(k < N // 2, k, k - N).astype(F32)
    turns = d * (m * m * (0.5 / (N * N)))
    frac = turns - jnp.floor(turns + 0.5)
    cos, sin = sincos(frac * (2.0 * math.pi))
    out[0:4, :], out[4:8, :] = 0.25 * cos, -0.25 * sin


def twisted(twiddle, order, k1):
    row = 8 * list(ORDERS).index(order) + k1
    return twiddle[row : row + 1, :], twiddle[row + 4 : row + 5, :]


def granules(parts, width):
    parts = list(parts)
    lane = lax.broadcasted_iota(jnp.int32, parts[0].shape, 1) // width
    bit = 1
    while bit < len(parts):
        high = (lane & bit) != 0
        for i in range(len(parts)):
            if i & bit:
                continue
            a, b = parts[i], parts[i | bit]
            parts[i] = jnp.where(high, pltpu.roll(b, width * bit, 1), a)
            parts[i | bit] = jnp.where(high, b, pltpu.roll(a, 128 - width * bit, 1))
        bit *= 2
    return parts


def gathered(block, base, first):
    columns = []
    for start in range(base, base + 32, 4):
        parts = [block[start + t, first : first + 16, :] for t in range(4)]
        columns.append(granules(parts, 32))
    return [jnp.concatenate([c[g] for c in columns], axis=1).astype(F32) for g in range(4)]


def field_of(block, base=0):
    groups = gathered(block, base, 0)
    return (
        jnp.concatenate([groups[0], groups[2]], axis=0),
        jnp.concatenate([groups[1], groups[3]], axis=0),
    )


def quarters(x):
    return [x[:, Q * n : Q * n + Q] for n in range(4)]


def forward(re, im, layer, spectrum_rows, twiddle, table):
    ar, ai = re[0] + re[2], im[0] + im[2]
    br, bi = re[0] - re[2], im[0] - im[2]
    cr, ci = re[1] + re[3], im[1] + im[3]
    dr, di = re[1] - re[3], im[1] - im[3]
    outs = [
        (ar + cr, ai + ci),
        (br + di, bi - dr),
        (ar - cr, ai - ci),
        (br - di, bi + dr),
    ]
    rows = []
    for k1, (r, m) in enumerate(outs):
        if k1:
            c, s = twisted(twiddle, "plain", k1)
            r, m = r * c + m * s, m * c - r * s
        rows.append(jnp.concatenate([r, m], axis=1).astype(BF))
    z = jnp.dot(jnp.concatenate(rows, axis=0), table[...], preferred_element_type=F32)
    spectrum = []
    size = re[0].shape[0]
    for k1 in range(4):
        zr, zi = z[size * k1 : size * k1 + size, :Q], z[size * k1 : size * k1 + size, Q:]
        hr = spectrum_rows[layer : layer + 1, Q * k1 : Q * k1 + Q]
        hi = spectrum_rows[layer + 4 : layer + 5, Q * k1 : Q * k1 + Q]
        spectrum.append(((zr * hr - zi * hi).astype(BF), (zr * hi + zi * hr).astype(BF)))
    return spectrum


def inverse(spectrum, order, twiddle, table):
    stacked = jnp.concatenate([jnp.concatenate(s, axis=1) for s in spectrum], axis=0)
    y = jnp.dot(stacked, table[...], preferred_element_type=F32)
    outs = []
    size = spectrum[0][0].shape[0]
    for k1 in range(4):
        r, m = y[size * k1 : size * k1 + size, :Q], y[size * k1 : size * k1 + size, Q:]
        if k1:
            c, s = twisted(twiddle, order, k1)
            r, m = r * c - m * s, m * c + r * s
        outs.append((r, m))
    (r0, i0), (r1, i1), (r2, i2), (r3, i3) = outs
    ar, ai, br, bi = r0 + r2, i0 + i2, r0 - r2, i0 - i2
    cr, ci, dr, di = r1 + r3, i1 + i3, r1 - r3, i1 - i3
    re = [ar + cr, br - di, ar - cr, br + di]
    im = [ai + ci, bi + dr, ai - ci, bi - dr]
    return re, im


def sent(spectrum, twiddle, table, out, turned=F32):
    for n1, (r, m) in enumerate(zip(*inverse(spectrum, "send", twiddle, table))):
        x = jnp.concatenate([r[:, :128], m[:, :128], r[:, 128:], m[:, 128:]], axis=0)
        x = x.astype(turned).T.astype(BF).reshape(8, 16, 128)
        for base in range(0, out.shape[0], 32):
            out[base + 8 * n1 : base + 8 * n1 + 8, 0:16, :] = x


def through_screen(re, im, phase):
    cos, sin = sincos(phase)
    out_re, out_im = [], []
    for r, m, c, s in zip(re, im, quarters(cos), quarters(sin)):
        out_re.append(r * c - m * s)
        out_im.append(r * s + m * c)
    return out_re, out_im


def payload_kernel(
    distance, far_screens, launch, far_targets, far_counts,
    shared, held, picks, twiddle,
    screens, targets, counts, sems,
):
    group = lax.axis_index("layer")
    copies = [
        pltpu.make_async_copy(source, target, sems.at[i])
        for i, (source, target) in enumerate([
            (far_screens, screens), (far_targets, targets), (far_counts, counts),
            (launch.at[group % 2], held),
        ])
    ]
    for copy in copies:
        copy.start()
    d = jnp.full((32, 128), distance[0], F32)
    high = d.astype(BF).astype(F32)
    middle = (d - high).astype(BF).astype(F32)
    low = (d - high) - middle
    row = lax.broadcasted_iota(jnp.int32, (32, 128), 0)
    tail = jnp.where(row == 0, high, jnp.where(row == 1, middle, jnp.where(row == 2, low, 0.0)))
    tail = tail.astype(BF)
    twiddles(twiddle)
    for copy in copies[:3]:
        copy.wait()
    phase = screens[0].astype(BF)
    for other in range(4):
        shared[other, :, 0:N] = phase
        shared[other, :, N : N + 128] = tail
    picks[...] = jnp.where(group < counts[...], targets[...], -1)
    for copy in copies[3:]:
        copy.wait()


def first_kernel(held, shared, twiddle, table, send, out, h):
    spectra(shared, h)
    re, im = quarters(held[0].astype(F32)), quarters(held[1].astype(F32))
    re, im = through_screen(re, im, shared[0, :, 0:N].astype(F32))
    sent(forward(re, im, 0, h, twiddle, table), twiddle, send, out)
    both = jnp.concatenate([shared[1, :, 0:N], shared[3, :, 0:N]], axis=0).astype(F32)
    for block in range(8):
        piece = both[:, 128 * block : 128 * block + 128].T.reshape(4, 2, 16, 64)
        out[4 * block : 4 * block + 4, 16:32, :] = jnp.concatenate(
            [piece[:, 0], piece[:, 1]], axis=2
        ).astype(BF)


def middle(layer, came, phase, h, twiddle, table, back, send, out):
    re, im = field_of(came)
    spectrum = forward(quarters(re), quarters(im), layer, h, twiddle, table)
    re, im = inverse(spectrum, "plain", twiddle, back)
    re, im = through_screen(re, im, phase)
    sent(forward(re, im, layer + 1, h, twiddle, table), twiddle, send, out, BF)


def column_kernel(layer, came, carried, *rest):
    groups = gathered(carried, 0, 16)
    which = layer // 2
    phase = jnp.concatenate([groups[which], groups[2 + which]], axis=0)
    middle(layer, came, phase, *rest)


def row_kernel(layer, came, shared, *rest):
    middle(layer, came, shared[layer + 1, :, 0:N].astype(F32), *rest)


def last_kernel(
    came, h, twiddle, table, back, back_sub, spots, templates, picks,
    far_pupil, result,
    cells, pupil, sem,
):
    fields = [field_of(came, 0), field_of(came, 32)]
    re, im = [quarters(jnp.concatenate(x, axis=0)) for x in zip(*fields)]
    spectrum = forward(re, im, 3, h, twiddle, table)
    for part, x in enumerate(inverse(spectrum, "sub", twiddle, back_sub)):
        for field in range(2):
            for upper in range(2):
                parts = [
                    x[n1][32 * field + 16 * a : 32 * field + 16 * a + 16,
                          128 * upper : 128 * upper + 128].astype(BF)
                    for a in range(2)
                    for n1 in range(4)
                ]
                for k, piece in enumerate(granules(parts, 16)):
                    row = part * 256 + (upper * 8 + k) * 16
                    cells[row : row + 16, 128 * field : 128 * field + 128] = piece
    re, im = inverse(spectrum, "plain", twiddle, back)
    for n in range(4):
        for field in range(2):
            rows = slice(32 * field, 32 * field + 32)
            pupil[field, 0, :, Q * n : Q * n + Q] = re[n][rows].astype(BF)
            pupil[field, 1, :, Q * n : Q * n + Q] = im[n][rows].astype(BF)
    written = pltpu.make_async_copy(pupil, far_pupil, sem)
    written.start()
    place = lax.broadcasted_iota(jnp.int32, (128, 32), 0)
    chosen = jnp.where(place == picks[...], 1.0, 0.0).astype(F32).T.astype(BF)
    slots = [
        lax.dot_general(
            chosen,
            cells[:, 128 * field : 128 * field + 128],
            (((1,), (1,)), ((), ())),
            preferred_element_type=F32,
        ).astype(BF)
        for field in range(2)
    ]
    spot = jnp.dot(jnp.concatenate(slots, axis=0), spots[...], preferred_element_type=F32)
    intensity = (spot[:, :1024] * spot[:, :1024] + spot[:, 1024:] * spot[:, 1024:]).astype(BF)
    total = lax.dot_general(
        intensity, templates[...], (((1,), (1,)), ((), ())), preferred_element_type=F32
    )
    for field in range(2):
        result[:, 16 * field : 16 * field + 16] = total[32 * field : 32 * field + 32]
    written.wait()


VMEM = pl.BlockSpec(memory_space=pltpu.VMEM)
SMEM = pl.BlockSpec(memory_space=pltpu.SMEM)
FAR = pl.BlockSpec(memory_space=pltpu.HBM)


def call(kernel, shapes, *operands, name=None, **specs):
    return pl.pallas_call(
        kernel,
        out_shape=shapes,
        compiler_params=pltpu.CompilerParams(vmem_limit_bytes=24 * 1024 * 1024),
        name=name,
        **specs,
    )(*operands)


def exchanged(block, axis="strip", groups=None):
    return lax.all_to_all(
        block, axis, split_axis=0, concat_axis=0, tiled=True, axis_index_groups=groups
    )


def per_device(launch, screens, distance, templates, send_table, send_counts):
    tables = {name: jnp.asarray(value) for name, value in angle_tables().items()}
    table, back, send = tables["forward"], tables["plain"], tables["send"]

    payload, held, picks, twiddle = call(
        payload_kernel,
        (
            jax.ShapeDtypeStruct((4, 32, N + 128), BF),
            jax.ShapeDtypeStruct(launch.shape[1:], BF),
            jax.ShapeDtypeStruct((1, 32), jnp.int32),
            jax.ShapeDtypeStruct((24, Q), F32),
        ),
        distance,
        *[
            pltpu.with_memory_space_constraint(x, pltpu.HBM)
            for x in (
                screens, launch, send_table.reshape(1, 32), send_counts
            )
        ],
        in_specs=[SMEM] + [FAR] * 4,
        out_specs=(VMEM,) * 4,
        scratch_shapes=[
            pltpu.VMEM(screens.shape, F32),
            pltpu.VMEM((1, 32), jnp.int32),
            pltpu.VMEM((1, 32), jnp.int32),
            pltpu.SemaphoreType.DMA((4,)),
        ],
        cost_estimate=pl.CostEstimate(flops=1500000000, bytes_accessed=4000000, transcendentals=0),
        name="payload",
    )
    shared = exchanged(payload, "layer")

    wide = jax.ShapeDtypeStruct((32, 32, 128), BF)
    plain = jax.ShapeDtypeStruct((32, 16, 128), BF)
    twice = jax.ShapeDtypeStruct((64, 16, 128), BF)
    pairs = [[32 * group + strip for group in pair for strip in range(32)] for pair in ((0, 1), (2, 3))]
    leaving, h = call(
        first_kernel, (wide, jax.ShapeDtypeStruct((8, N), F32)),
        held, shared, twiddle, table, send, name="rows0",
    )
    carried = exchanged(leaving)

    def columns(layer, came, shape, name):
        def kernel(*refs):
            column_kernel(layer, *refs)

        return call(kernel, shape, came, carried, h, twiddle, table, back, send, name=name)

    def rows(layer, came, name):
        def kernel(*refs):
            row_kernel(layer, *refs)

        return call(kernel, plain, came, shared, h, twiddle, table, back, send, name=name)

    came = exchanged(columns(0, carried, plain, "columns01"))
    came = exchanged(rows(1, came, "rows12"))
    came = exchanged(columns(2, came, twice, "columns23"), ("layer", "strip"), pairs)

    spots = jnp.asarray(spot_table())
    pupil, result = call(
        last_kernel,
        (jax.ShapeDtypeStruct(launch.shape, BF), jax.ShapeDtypeStruct((32, 32), F32)),
        came, h, twiddle, table, back, tables["sub"], spots, templates.T, picks,
        in_specs=[VMEM] * 9,
        out_specs=(FAR, VMEM),
        scratch_shapes=[
            pltpu.VMEM((512, 256), BF),
            pltpu.VMEM(launch.shape, BF),
            pltpu.SemaphoreType.DMA,
        ],
        name="rows3",
    )
    return (pupil, exchanged(result).reshape(1, 32, 1, 2, 16))


def solution(mesh):
    placed = (
        P(None, None, "strip", None),
        P("layer", "strip", None),
        P("layer"),
        P(),
        P("strip", None, "layer"),
        P("strip", None),
    )
    return jax.shard_map(
        per_device,
        mesh=mesh,
        in_specs=placed,
        out_specs=(P(None, None, "strip", None), P("strip", None, "layer", None, None)),
        check_vma=False,
    )
```

```python
import math

import jax
import jax.numpy as jnp
import numpy as np
from jax import lax
from jax.experimental import pallas as pl
from jax.experimental.pallas import tpu as pltpu
from jax.sharding import PartitionSpec as P

N = 1024
Q = 256
SUB = 16
SPOT = 2 * SUB
BF = jnp.bfloat16
F32 = jnp.float32
CODE = 25.0


def bf16(table):
    return np.asarray(table, np.float32).astype(jnp.bfloat16)


ORDERS = {
    "plain": lambda at: at,
    "send": lambda at: (at % 128) // 16 * 32 + at // 128 * 16 + at % 16,
    "sub": lambda at: at % SUB * SUB + at // SUB,
}


def angle_tables():
    n = np.arange(Q)
    turn = 2.0 * np.pi * ((n[:, None] * n[None, :]) % Q) / Q
    cos, sin = np.cos(turn) / 16.0, np.sin(turn) / 16.0
    forward = np.block([[cos, -sin], [sin, cos]])
    inverse = np.block([[cos, sin], [-sin, cos]])
    tables = {"forward": bf16(forward)}
    for name, order in ORDERS.items():
        tables[name] = bf16(inverse[:, np.concatenate([order(n), Q + order(n)])])
    return tables


def spot_table():
    turn = 2.0 * np.pi * ((np.arange(SPOT)[:, None] * np.arange(SUB)[None, :]) % SPOT) / SPOT
    wave = (np.cos(turn) - 1j * np.sin(turn)) / math.sqrt(SUB)
    kron = wave[:, None, None, :] * wave[None, :, :, None]
    kron = kron.reshape(SPOT * SPOT, SUB * SUB)
    return bf16(np.block([[kron.real, -kron.imag], [kron.imag, kron.real]]).T)


def sincos(x):
    y = 0.5 * x
    z = y * y
    s = 2.6048728614114225e-06
    for a in (-0.0001980891975108534, 0.008333048783242702, -0.16666658222675323, 1.0):
        s = s * z + a
    s = s * y
    c = 2.3149976186687127e-05
    for a in (-0.0013853529235348105, 0.04166356101632118, -0.4999990463256836, 0.9999999403953552):
        c = c * z + a
    t = s + s
    return 1.0 - t * s, t * c


def coded(phase):
    return jnp.exp(CODE * phase).astype(BF)


def decoded(code):
    return jnp.log(code.astype(F32)) * (1.0 / CODE)


def twiddles(out):
    k1 = lax.broadcasted_iota(jnp.int32, (4, Q), 0)
    at = lax.broadcasted_iota(jnp.int32, (4, Q), 1)
    for i, order in enumerate(ORDERS.values()):
        turns = (k1 * order(at)).astype(F32) * (1.0 / N)
        turns = jnp.where(turns > 0.5, turns - 1.0, turns)
        out[8 * i : 8 * i + 4, :], out[8 * i + 4 : 8 * i + 8, :] = sincos(turns * (2.0 * math.pi))


def spectra(shared, out):
    d = []
    for layer in range(4):
        tail = shared[layer, 0:16, N : N + 128].astype(F32)
        d.append((tail[0:1] + tail[1:2]) + tail[2:3])
    d = jnp.concatenate([jnp.concatenate(d, axis=0)] * (N // 128), axis=1)
    place = lax.broadcasted_iota(jnp.int32, (4, N), 1)
    k = 4 * (place % Q) + place // Q
    m = jnp.where(k < N // 2, k, k - N).astype(F32)
    turns = d * (m * m * (0.5 / (N * N)))
    frac = turns - jnp.floor(turns + 0.5)
    cos, sin = sincos(frac * (2.0 * math.pi))
    out[0:4, :], out[4:8, :] = 0.25 * cos, -0.25 * sin


def twisted(twiddle, order, k1):
    row = 8 * list(ORDERS).index(order) + k1
    return twiddle[row : row + 1, :], twiddle[row + 4 : row + 5, :]


def granules(parts, width):
    parts = list(parts)
    lane = lax.broadcasted_iota(jnp.int32, parts[0].shape, 1) // width
    bit = 1
    while bit < len(parts):
        high = (lane & bit) != 0
        for i in range(len(parts)):
            if i & bit:
                continue
            a, b = parts[i], parts[i | bit]
            parts[i] = jnp.where(high, pltpu.roll(b, width * bit, 1), a)
            parts[i | bit] = jnp.where(high, b, pltpu.roll(a, 128 - width * bit, 1))
        bit *= 2
    return parts


def gathered(block, base, first):
    columns = []
    for start in range(base, base + 32, 4):
        parts = [block[start + t, first : first + 16, :] for t in range(4)]
        columns.append(granules(parts, 32))
    return [jnp.concatenate([c[g] for c in columns], axis=1).astype(F32) for g in range(4)]


def field_of(block, base=0):
    groups = gathered(block, base, 0)
    return (
        jnp.concatenate([groups[0], groups[2]], axis=0),
        jnp.concatenate([groups[1], groups[3]], axis=0),
    )


def quarters(x):
    return [x[:, Q * n : Q * n + Q] for n in range(4)]


def forward(re, im, layer, spectrum_rows, twiddle, table):
    ar, ai = re[0] + re[2], im[0] + im[2]
    br, bi = re[0] - re[2], im[0] - im[2]
    cr, ci = re[1] + re[3], im[1] + im[3]
    dr, di = re[1] - re[3], im[1] - im[3]
    outs = [
        (ar + cr, ai + ci),
        (br + di, bi - dr),
        (ar - cr, ai - ci),
        (br - di, bi + dr),
    ]
    rows = []
    for k1, (r, m) in enumerate(outs):
        if k1:
            c, s = twisted(twiddle, "plain", k1)
            r, m = r * c + m * s, m * c - r * s
        rows.append(jnp.concatenate([r, m], axis=1).astype(BF))
    z = jnp.dot(jnp.concatenate(rows, axis=0), table[...], preferred_element_type=F32)
    spectrum = []
    size = re[0].shape[0]
    for k1 in range(4):
        zr, zi = z[size * k1 : size * k1 + size, :Q], z[size * k1 : size * k1 + size, Q:]
        hr = spectrum_rows[layer : layer + 1, Q * k1 : Q * k1 + Q]
        hi = spectrum_rows[layer + 4 : layer + 5, Q * k1 : Q * k1 + Q]
        spectrum.append(((zr * hr - zi * hi).astype(BF), (zr * hi + zi * hr).astype(BF)))
    return spectrum


def inverse(spectrum, order, twiddle, table):
    stacked = jnp.concatenate([jnp.concatenate(s, axis=1) for s in spectrum], axis=0)
    y = jnp.dot(stacked, table[...], preferred_element_type=F32)
    outs = []
    size = spectrum[0][0].shape[0]
    for k1 in range(4):
        r, m = y[size * k1 : size * k1 + size, :Q], y[size * k1 : size * k1 + size, Q:]
        if k1:
            c, s = twisted(twiddle, order, k1)
            r, m = r * c - m * s, m * c + r * s
        outs.append((r, m))
    (r0, i0), (r1, i1), (r2, i2), (r3, i3) = outs
    ar, ai, br, bi = r0 + r2, i0 + i2, r0 - r2, i0 - i2
    cr, ci, dr, di = r1 + r3, i1 + i3, r1 - r3, i1 - i3
    re = [ar + cr, br - di, ar - cr, br + di]
    im = [ai + ci, bi + dr, ai - ci, bi - dr]
    return re, im


def sent(spectrum, twiddle, table, out, turned=F32):
    for n1, (r, m) in enumerate(zip(*inverse(spectrum, "send", twiddle, table))):
        x = jnp.concatenate([r[:, :128], m[:, :128], r[:, 128:], m[:, 128:]], axis=0)
        x = x.astype(turned).T.astype(BF).reshape(8, 16, 128)
        for base in range(0, out.shape[0], 32):
            out[base + 8 * n1 : base + 8 * n1 + 8, 0:16, :] = x


def through_screen(re, im, phase):
    cos, sin = sincos(phase)
    out_re, out_im = [], []
    for r, m, c, s in zip(re, im, quarters(cos), quarters(sin)):
        out_re.append(r * c - m * s)
        out_im.append(r * s + m * c)
    return out_re, out_im


def payload_kernel(
    distance, far_screens, launch, far_targets, far_counts,
    shared, held, picks, twiddle,
    screens, targets, counts, sems,
):
    group = lax.axis_index("layer")
    copies = [
        pltpu.make_async_copy(source, target, sems.at[i])
        for i, (source, target) in enumerate([
            (far_screens, screens), (far_targets, targets), (far_counts, counts),
            (launch.at[group % 2], held),
        ])
    ]
    for copy in copies:
        copy.start()
    d = jnp.full((32, 128), distance[0], F32)
    high = d.astype(BF).astype(F32)
    middle = (d - high).astype(BF).astype(F32)
    low = (d - high) - middle
    row = lax.broadcasted_iota(jnp.int32, (32, 128), 0)
    tail = jnp.where(row == 0, high, jnp.where(row == 1, middle, jnp.where(row == 2, low, 0.0)))
    tail = tail.astype(BF)
    twiddles(twiddle)
    for copy in copies[:3]:
        copy.wait()
    phase = coded(screens[0])
    for other in range(4):
        shared[other, :, 0:N] = phase
        shared[other, :, N : N + 128] = tail
    picks[...] = jnp.where(group < counts[...], targets[...], -1)
    for copy in copies[3:]:
        copy.wait()


def first_kernel(held, shared, twiddle, table, send, out, h):
    spectra(shared, h)
    re, im = quarters(held[0].astype(F32)), quarters(held[1].astype(F32))
    re, im = through_screen(re, im, decoded(shared[0, :, 0:N]))
    sent(forward(re, im, 0, h, twiddle, table), twiddle, send, out)
    both = jnp.concatenate([shared[1, :, 0:N], shared[3, :, 0:N]], axis=0).astype(F32)
    for block in range(8):
        piece = both[:, 128 * block : 128 * block + 128].T.reshape(4, 2, 16, 64)
        out[4 * block : 4 * block + 4, 16:32, :] = jnp.concatenate(
            [piece[:, 0], piece[:, 1]], axis=2
        ).astype(BF)


def middle(layer, came, phase, h, twiddle, table, back, send, out):
    re, im = field_of(came)
    spectrum = forward(quarters(re), quarters(im), layer, h, twiddle, table)
    re, im = inverse(spectrum, "plain", twiddle, back)
    re, im = through_screen(re, im, phase)
    sent(forward(re, im, layer + 1, h, twiddle, table), twiddle, send, out, BF)


def column_kernel(layer, came, carried, *rest):
    groups = gathered(carried, 0, 16)
    which = layer // 2
    phase = decoded(jnp.concatenate([groups[which], groups[2 + which]], axis=0))
    middle(layer, came, phase, *rest)


def row_kernel(layer, came, shared, *rest):
    middle(layer, came, decoded(shared[layer + 1, :, 0:N]), *rest)


def last_kernel(
    came, h, twiddle, table, back, back_sub, spots, templates, picks,
    far_pupil, result,
    cells, pupil, sem,
):
    fields = [field_of(came, 0), field_of(came, 32)]
    re, im = [quarters(jnp.concatenate(x, axis=0)) for x in zip(*fields)]
    spectrum = forward(re, im, 3, h, twiddle, table)
    for part, x in enumerate(inverse(spectrum, "sub", twiddle, back_sub)):
        for field in range(2):
            for upper in range(2):
                parts = [
                    x[n1][32 * field + 16 * a : 32 * field + 16 * a + 16,
                          128 * upper : 128 * upper + 128].astype(BF)
                    for a in range(2)
                    for n1 in range(4)
                ]
                for k, piece in enumerate(granules(parts, 16)):
                    row = part * 256 + (upper * 8 + k) * 16
                    cells[row : row + 16, 128 * field : 128 * field + 128] = piece
    re, im = inverse(spectrum, "plain", twiddle, back)
    for n in range(4):
        for field in range(2):
            rows = slice(32 * field, 32 * field + 32)
            pupil[field, 0, :, Q * n : Q * n + Q] = re[n][rows].astype(BF)
            pupil[field, 1, :, Q * n : Q * n + Q] = im[n][rows].astype(BF)
    written = pltpu.make_async_copy(pupil, far_pupil, sem)
    written.start()
    place = lax.broadcasted_iota(jnp.int32, (128, 32), 0)
    chosen = jnp.where(place == picks[...], 1.0, 0.0).astype(F32).T.astype(BF)
    slots = [
        lax.dot_general(
            chosen,
            cells[:, 128 * field : 128 * field + 128],
            (((1,), (1,)), ((), ())),
            preferred_element_type=F32,
        ).astype(BF)
        for field in range(2)
    ]
    spot = jnp.dot(jnp.concatenate(slots, axis=0), spots[...], preferred_element_type=F32)
    intensity = (spot[:, :1024] * spot[:, :1024] + spot[:, 1024:] * spot[:, 1024:]).astype(BF)
    total = lax.dot_general(
        intensity, templates[...], (((1,), (1,)), ((), ())), preferred_element_type=F32
    )
    for field in range(2):
        result[:, 16 * field : 16 * field + 16] = total[32 * field : 32 * field + 32]
    written.wait()


VMEM = pl.BlockSpec(memory_space=pltpu.VMEM)
SMEM = pl.BlockSpec(memory_space=pltpu.SMEM)
FAR = pl.BlockSpec(memory_space=pltpu.HBM)


def call(kernel, shapes, *operands, name=None, **specs):
    return pl.pallas_call(
        kernel,
        out_shape=shapes,
        compiler_params=pltpu.CompilerParams(vmem_limit_bytes=24 * 1024 * 1024),
        name=name,
        **specs,
    )(*operands)


def exchanged(block, axis="strip", groups=None):
    return lax.all_to_all(
        block, axis, split_axis=0, concat_axis=0, tiled=True, axis_index_groups=groups
    )


def per_device(launch, screens, distance, templates, send_table, send_counts):
    tables = {name: jnp.asarray(value) for name, value in angle_tables().items()}
    table, back, send = tables["forward"], tables["plain"], tables["send"]

    payload, held, picks, twiddle = call(
        payload_kernel,
        (
            jax.ShapeDtypeStruct((4, 32, N + 128), BF),
            jax.ShapeDtypeStruct(launch.shape[1:], BF),
            jax.ShapeDtypeStruct((1, 32), jnp.int32),
            jax.ShapeDtypeStruct((24, Q), F32),
        ),
        distance,
        *[
            pltpu.with_memory_space_constraint(x, pltpu.HBM)
            for x in (
                screens, launch, send_table.reshape(1, 32), send_counts
            )
        ],
        in_specs=[SMEM] + [FAR] * 4,
        out_specs=(VMEM,) * 4,
        scratch_shapes=[
            pltpu.VMEM(screens.shape, F32),
            pltpu.VMEM((1, 32), jnp.int32),
            pltpu.VMEM((1, 32), jnp.int32),
            pltpu.SemaphoreType.DMA((4,)),
        ],
        cost_estimate=pl.CostEstimate(flops=1500000000, bytes_accessed=4000000, transcendentals=0),
        name="payload",
    )
    shared = exchanged(payload, "layer")

    wide = jax.ShapeDtypeStruct((32, 32, 128), BF)
    plain = jax.ShapeDtypeStruct((32, 16, 128), BF)
    twice = jax.ShapeDtypeStruct((64, 16, 128), BF)
    pairs = [[32 * group + strip for group in pair for strip in range(32)] for pair in ((0, 1), (2, 3))]
    leaving, h = call(
        first_kernel, (wide, jax.ShapeDtypeStruct((8, N), F32)),
        held, shared, twiddle, table, send, name="rows0",
    )
    carried = exchanged(leaving)

    def columns(layer, came, shape, name):
        def kernel(*refs):
            column_kernel(layer, *refs)

        return call(kernel, shape, came, carried, h, twiddle, table, back, send, name=name)

    def rows(layer, came, name):
        def kernel(*refs):
            row_kernel(layer, *refs)

        return call(kernel, plain, came, shared, h, twiddle, table, back, send, name=name)

    came = exchanged(columns(0, carried, plain, "columns01"))
    came = exchanged(rows(1, came, "rows12"))
    came = exchanged(columns(2, came, twice, "columns23"), ("layer", "strip"), pairs)

    spots = jnp.asarray(spot_table())
    pupil, result = call(
        last_kernel,
        (jax.ShapeDtypeStruct(launch.shape, BF), jax.ShapeDtypeStruct((32, 32), F32)),
        came, h, twiddle, table, back, tables["sub"], spots, templates.T, picks,
        in_specs=[VMEM] * 9,
        out_specs=(FAR, VMEM),
        scratch_shapes=[
            pltpu.VMEM((512, 256), BF),
            pltpu.VMEM(launch.shape, BF),
            pltpu.SemaphoreType.DMA,
        ],
        name="rows3",
    )
    return (pupil, exchanged(result).reshape(1, 32, 1, 2, 16))


def solution(mesh):
    placed = (
        P(None, None, "strip", None),
        P("layer", "strip", None),
        P("layer"),
        P(),
        P("strip", None, "layer"),
        P("strip", None),
    )
    return jax.shard_map(
        per_device,
        mesh=mesh,
        in_specs=placed,
        out_specs=(P(None, None, "strip", None), P("strip", None, "layer", None, None)),
        check_vma=False,
    )
```

```python
import math

import jax
import jax.numpy as jnp
import numpy as np
from jax import lax
from jax.experimental import pallas as pl
from jax.experimental.pallas import tpu as pltpu
from jax.sharding import PartitionSpec as P

N = 1024
Q = 256
SUB = 16
SPOT = 2 * SUB
BF = jnp.bfloat16
F32 = jnp.float32
CODE = 25.0


def bf16(table):
    return np.asarray(table, np.float32).astype(jnp.bfloat16)


ORDERS = {
    "plain": lambda at: at,
    "send": lambda at: (at % 128) // 16 * 32 + at // 128 * 16 + at % 16,
    "sub": lambda at: at % SUB * SUB + at // SUB,
}


def angle_tables():
    n = np.arange(Q)
    turn = 2.0 * np.pi * ((n[:, None] * n[None, :]) % Q) / Q
    cos, sin = np.cos(turn) / 16.0, np.sin(turn) / 16.0
    forward = np.block([[cos, -sin], [sin, cos]])
    inverse = np.block([[cos, sin], [-sin, cos]])
    tables = {"forward": bf16(forward)}
    for name, order in ORDERS.items():
        tables[name] = bf16(inverse[:, np.concatenate([order(n), Q + order(n)])])
    return tables


def spot_table():
    turn = 2.0 * np.pi * ((np.arange(SPOT)[:, None] * np.arange(SUB)[None, :]) % SPOT) / SPOT
    wave = (np.cos(turn) - 1j * np.sin(turn)) / math.sqrt(SUB)
    kron = wave[:, None, None, :] * wave[None, :, :, None]
    kron = kron.reshape(SPOT * SPOT, SUB * SUB)
    return bf16(np.block([[kron.real, -kron.imag], [kron.imag, kron.real]]).T)


def sincos(x):
    y = 0.5 * x
    z = y * y
    s = 2.6048728614114225e-06
    for a in (-0.0001980891975108534, 0.008333048783242702, -0.16666658222675323, 1.0):
        s = s * z + a
    s = s * y
    c = 2.3149976186687127e-05
    for a in (-0.0013853529235348105, 0.04166356101632118, -0.4999990463256836, 0.9999999403953552):
        c = c * z + a
    t = s + s
    return 1.0 - t * s, t * c


def coded(phase):
    return jnp.exp(CODE * phase).astype(BF)


def decoded(code):
    return jnp.log(code.astype(F32)) * (1.0 / CODE)


def twiddles(out):
    k1 = lax.broadcasted_iota(jnp.int32, (4, Q), 0)
    at = lax.broadcasted_iota(jnp.int32, (4, Q), 1)
    for i, order in enumerate(ORDERS.values()):
        turns = (k1 * order(at)).astype(F32) * (1.0 / N)
        turns = jnp.where(turns > 0.5, turns - 1.0, turns)
        out[8 * i : 8 * i + 4, :], out[8 * i + 4 : 8 * i + 8, :] = sincos(turns * (2.0 * math.pi))


def spectra(shared, out):
    d = []
    for layer in range(4):
        tail = shared[layer, 0:16, N : N + 128].astype(F32)
        d.append((tail[0:1] + tail[1:2]) + tail[2:3])
    d = jnp.concatenate([jnp.concatenate(d, axis=0)] * (N // 128), axis=1)
    place = lax.broadcasted_iota(jnp.int32, (4, N), 1)
    k = 4 * (place % Q) + place // Q
    m = jnp.where(k < N // 2, k, k - N).astype(F32)
    turns = d * (m * m * (0.5 / (N * N)))
    frac = turns - jnp.floor(turns + 0.5)
    cos, sin = sincos(frac * (2.0 * math.pi))
    out[0:4, :], out[4:8, :] = 0.25 * cos, -0.25 * sin


def twisted(twiddle, order, k1):
    row = 8 * list(ORDERS).index(order) + k1
    return twiddle[row : row + 1, :], twiddle[row + 4 : row + 5, :]


def granules(parts, width):
    parts = list(parts)
    lane = lax.broadcasted_iota(jnp.int32, parts[0].shape, 1) // width
    bit = 1
    while bit < len(parts):
        high = (lane & bit) != 0
        for i in range(len(parts)):
            if i & bit:
                continue
            a, b = parts[i], parts[i | bit]
            parts[i] = jnp.where(high, pltpu.roll(b, width * bit, 1), a)
            parts[i | bit] = jnp.where(high, b, pltpu.roll(a, 128 - width * bit, 1))
        bit *= 2
    return parts


def gathered(block, base, first):
    columns = []
    for start in range(base, base + 32, 4):
        parts = [block[start + t, first : first + 16, :] for t in range(4)]
        columns.append(granules(parts, 32))
    return [jnp.concatenate([c[g] for c in columns], axis=1).astype(F32) for g in range(4)]


def field_of(block, base=0):
    groups = gathered(block, base, 0)
    return (
        jnp.concatenate([groups[0], groups[2]], axis=0),
        jnp.concatenate([groups[1], groups[3]], axis=0),
    )


def quarters(x):
    return [x[:, Q * n : Q * n + Q] for n in range(4)]


def forward(re, im, layer, spectrum_rows, twiddle, table):
    ar, ai = re[0] + re[2], im[0] + im[2]
    br, bi = re[0] - re[2], im[0] - im[2]
    cr, ci = re[1] + re[3], im[1] + im[3]
    dr, di = re[1] - re[3], im[1] - im[3]
    outs = [
        (ar + cr, ai + ci),
        (br + di, bi - dr),
        (ar - cr, ai - ci),
        (br - di, bi + dr),
    ]
    rows = []
    for k1, (r, m) in enumerate(outs):
        if k1:
            c, s = twisted(twiddle, "plain", k1)
            r, m = r * c + m * s, m * c - r * s
        rows.append(jnp.concatenate([r, m], axis=1).astype(BF))
    z = jnp.dot(jnp.concatenate(rows, axis=0), table[...], preferred_element_type=F32)
    spectrum = []
    size = re[0].shape[0]
    for k1 in range(4):
        zr, zi = z[size * k1 : size * k1 + size, :Q], z[size * k1 : size * k1 + size, Q:]
        hr = spectrum_rows[layer : layer + 1, Q * k1 : Q * k1 + Q]
        hi = spectrum_rows[layer + 4 : layer + 5, Q * k1 : Q * k1 + Q]
        spectrum.append(((zr * hr - zi * hi).astype(BF), (zr * hi + zi * hr).astype(BF)))
    return spectrum


def inverse(spectrum, order, twiddle, table):
    stacked = jnp.concatenate([jnp.concatenate(s, axis=1) for s in spectrum], axis=0)
    y = jnp.dot(stacked, table[...], preferred_element_type=F32)
    outs = []
    size = spectrum[0][0].shape[0]
    for k1 in range(4):
        r, m = y[size * k1 : size * k1 + size, :Q], y[size * k1 : size * k1 + size, Q:]
        if k1:
            c, s = twisted(twiddle, order, k1)
            r, m = r * c - m * s, m * c + r * s
        outs.append((r, m))
    (r0, i0), (r1, i1), (r2, i2), (r3, i3) = outs
    ar, ai, br, bi = r0 + r2, i0 + i2, r0 - r2, i0 - i2
    cr, ci, dr, di = r1 + r3, i1 + i3, r1 - r3, i1 - i3
    re = [ar + cr, br - di, ar - cr, br + di]
    im = [ai + ci, bi + dr, ai - ci, bi - dr]
    return re, im


def sent(spectrum, twiddle, table, out, turned=F32):
    for n1, (r, m) in enumerate(zip(*inverse(spectrum, "send", twiddle, table))):
        x = jnp.concatenate([r[:, :128], m[:, :128], r[:, 128:], m[:, 128:]], axis=0)
        x = x.astype(turned).T.astype(BF).reshape(8, 16, 128)
        for base in range(0, out.shape[0], 32):
            out[base + 8 * n1 : base + 8 * n1 + 8, 0:16, :] = x


def through_screen(re, im, phase):
    cos, sin = sincos(phase)
    out_re, out_im = [], []
    for r, m, c, s in zip(re, im, quarters(cos), quarters(sin)):
        out_re.append(r * c - m * s)
        out_im.append(r * s + m * c)
    return out_re, out_im


def payload_kernel(
    distance, far_screens, launch, far_targets, far_counts,
    shared, held, twiddle,
    screens, targets, counts, sems,
):
    group = lax.axis_index("layer")
    copies = [
        pltpu.make_async_copy(source, target, sems.at[i])
        for i, (source, target) in enumerate([
            (far_screens, screens), (far_targets, targets), (far_counts, counts),
            (launch.at[group % 2], held),
        ])
    ]
    for copy in copies:
        copy.start()
    d = jnp.full((32, 128), distance[0], F32)
    high = d.astype(BF).astype(F32)
    middle = (d - high).astype(BF).astype(F32)
    low = (d - high) - middle
    row = lax.broadcasted_iota(jnp.int32, (32, 128), 0)
    twiddles(twiddle)
    for copy in copies[:3]:
        copy.wait()
    picks = jnp.where(group < counts[...], targets[...], -1).astype(F32)
    picks = jnp.concatenate([picks, jnp.full((1, 96), -1.0, F32)], axis=1)
    tail = jnp.zeros((32, 128), F32)
    for i, value in enumerate((high, middle, low, picks)):
        tail = jnp.where(row == i, value, tail)
    tail = tail.astype(BF)
    phase = coded(screens[0])
    for other in range(4):
        shared[other, :, 0:N] = phase
        shared[other, :, N : N + 128] = tail
    for copy in copies[3:]:
        copy.wait()


def first_kernel(held, shared, twiddle, table, send, out, h):
    spectra(shared, h)
    re, im = quarters(held[0].astype(F32)), quarters(held[1].astype(F32))
    re, im = through_screen(re, im, decoded(shared[0, :, 0:N]))
    sent(forward(re, im, 0, h, twiddle, table), twiddle, send, out)
    both = jnp.concatenate([shared[1, :, 0:N], shared[3, :, 0:N]], axis=0).astype(F32)
    for block in range(8):
        piece = both[:, 128 * block : 128 * block + 128].T.reshape(4, 2, 16, 64)
        out[4 * block : 4 * block + 4, 16:32, :] = jnp.concatenate(
            [piece[:, 0], piece[:, 1]], axis=2
        ).astype(BF)


def middle(layer, came, phase, h, twiddle, table, back, send, out):
    re, im = field_of(came)
    spectrum = forward(quarters(re), quarters(im), layer, h, twiddle, table)
    re, im = inverse(spectrum, "plain", twiddle, back)
    re, im = through_screen(re, im, phase)
    sent(forward(re, im, layer + 1, h, twiddle, table), twiddle, send, out, BF)


def column_kernel(layer, came, carried, *rest):
    groups = gathered(carried, 0, 16)
    which = layer // 2
    phase = decoded(jnp.concatenate([groups[which], groups[2 + which]], axis=0))
    middle(layer, came, phase, *rest)


def row_kernel(layer, came, shared, *rest):
    middle(layer, came, decoded(shared[layer + 1, :, 0:N]), *rest)


def last_kernel(
    came, shared, h, twiddle, table, back, back_sub, spots, templates, mine, result, cells
):
    re, im = field_of(came)
    spectrum = forward(quarters(re), quarters(im), 3, h, twiddle, table)
    for part, x in enumerate(inverse(spectrum, "sub", twiddle, back_sub)):
        for upper in range(2):
            parts = [
                x[n1][16 * a : 16 * a + 16, 128 * upper : 128 * upper + 128].astype(BF)
                for a in range(2)
                for n1 in range(4)
            ]
            for k, piece in enumerate(granules(parts, 16)):
                row = part * 256 + (upper * 8 + k) * 16
                cells[row : row + 16, :] = piece
    for part, x in enumerate(inverse(spectrum, "plain", twiddle, back)):
        for n in range(4):
            mine[part, :, Q * n : Q * n + Q] = x[n].astype(BF)
    first = lax.axis_index("layer") // 2 * 2
    picks = [shared[first + i, 0:16, N : N + 128].astype(F32)[3:4, :32] for i in range(2)]
    picks = jnp.concatenate(picks, axis=1)
    place = lax.broadcasted_iota(jnp.int32, (128, 64), 0).astype(F32)
    chosen = jnp.where(place == picks, 1.0, 0.0).astype(F32).T.astype(BF)
    slots = lax.dot_general(
        chosen, cells[...], (((1,), (1,)), ((), ())), preferred_element_type=F32
    ).astype(BF)
    spot = jnp.dot(slots, spots[...], preferred_element_type=F32)
    intensity = (spot[:, :1024] * spot[:, :1024] + spot[:, 1024:] * spot[:, 1024:]).astype(BF)
    result[...] = lax.dot_general(
        intensity, templates[...], (((1,), (1,)), ((), ())), preferred_element_type=F32
    )


def outputs_kernel(mine, other, result, pupil, correlation, turned, sems):
    own = lax.axis_index("layer") % 2
    copies = [
        pltpu.make_async_copy(mine, pupil.at[own], sems.at[0]),
        pltpu.make_async_copy(other, pupil.at[1 - own], sems.at[1]),
    ]
    for copy in copies:
        copy.start()
    for field in range(2):
        turned[field] = result[32 * field : 32 * field + 32, :].T
    copies.append(pltpu.make_async_copy(turned, correlation, sems.at[2]))
    copies[2].start()
    for copy in copies:
        copy.wait()


VMEM = pl.BlockSpec(memory_space=pltpu.VMEM)
SMEM = pl.BlockSpec(memory_space=pltpu.SMEM)
FAR = pl.BlockSpec(memory_space=pltpu.HBM)


def call(kernel, shapes, *operands, name=None, **specs):
    return pl.pallas_call(
        kernel,
        out_shape=shapes,
        compiler_params=pltpu.CompilerParams(vmem_limit_bytes=24 * 1024 * 1024),
        name=name,
        **specs,
    )(*operands)


def exchanged(block, axis="strip", groups=None):
    return lax.all_to_all(
        block, axis, split_axis=0, concat_axis=0, tiled=True, axis_index_groups=groups
    )


def per_device(launch, screens, distance, templates, send_table, send_counts):
    tables = {name: jnp.asarray(value) for name, value in angle_tables().items()}
    table, back, send = tables["forward"], tables["plain"], tables["send"]

    payload, held, twiddle = call(
        payload_kernel,
        (
            jax.ShapeDtypeStruct((4, 32, N + 128), BF),
            jax.ShapeDtypeStruct(launch.shape[1:], BF),
            jax.ShapeDtypeStruct((24, Q), F32),
        ),
        distance,
        *[
            pltpu.with_memory_space_constraint(x, pltpu.HBM)
            for x in (
                screens, launch, send_table.reshape(1, 32), send_counts
            )
        ],
        in_specs=[SMEM] + [FAR] * 4,
        out_specs=(VMEM,) * 3,
        scratch_shapes=[
            pltpu.VMEM(screens.shape, F32),
            pltpu.VMEM((1, 32), jnp.int32),
            pltpu.VMEM((1, 32), jnp.int32),
            pltpu.SemaphoreType.DMA((4,)),
        ],
        cost_estimate=pl.CostEstimate(flops=1500000000, bytes_accessed=4000000, transcendentals=0),
        name="payload",
    )
    shared = exchanged(payload, "layer")

    wide = jax.ShapeDtypeStruct((32, 32, 128), BF)
    plain = jax.ShapeDtypeStruct((32, 16, 128), BF)
    pairs = [[32 * group + strip for group in pair for strip in range(32)] for pair in ((0, 1), (2, 3))]
    leaving, h = call(
        first_kernel, (wide, jax.ShapeDtypeStruct((8, N), F32)),
        held, shared, twiddle, table, send, name="rows0",
    )
    carried = exchanged(leaving)

    def columns(layer, came, name):
        def kernel(*refs):
            column_kernel(layer, *refs)

        return call(kernel, plain, came, carried, h, twiddle, table, back, send, name=name)

    def rows(layer, came, name):
        def kernel(*refs):
            row_kernel(layer, *refs)

        return call(kernel, plain, came, shared, h, twiddle, table, back, send, name=name)

    came = exchanged(columns(0, carried, "columns01"))
    came = exchanged(rows(1, came, "rows12"))
    came = exchanged(columns(2, came, "columns23"))

    spots = jnp.asarray(spot_table())
    mine, result = call(
        last_kernel,
        (jax.ShapeDtypeStruct(launch.shape[1:], BF), jax.ShapeDtypeStruct((64, 16), F32)),
        came, shared, h, twiddle, table, back, tables["sub"], spots, templates.T,
        scratch_shapes=[pltpu.VMEM((512, 128), BF)],
        name="rows3",
    )
    other = lax.ppermute(mine, "layer", [(0, 1), (1, 0), (2, 3), (3, 2)])
    result = exchanged(result, ("layer", "strip"), pairs)
    pupil, correlation = call(
        outputs_kernel,
        (jax.ShapeDtypeStruct(launch.shape, BF), jax.ShapeDtypeStruct((2, 16, 32), F32)),
        mine, other, result,
        in_specs=[VMEM] * 3,
        out_specs=(FAR, FAR),
        scratch_shapes=[pltpu.VMEM((2, 16, 32), F32), pltpu.SemaphoreType.DMA((3,))],
        name="outputs",
    )
    return (pupil, correlation.transpose(2, 0, 1)[None, :, None])


def solution(mesh):
    placed = (
        P(None, None, "strip", None),
        P("layer", "strip", None),
        P("layer"),
        P(),
        P("strip", None, "layer"),
        P("strip", None),
    )
    return jax.shard_map(
        per_device,
        mesh=mesh,
        in_specs=placed,
        out_specs=(P(None, None, "strip", None), P("strip", None, "layer", None, None)),
        check_vma=False,
    )
```

```python
import math

import jax
import jax.numpy as jnp
import numpy as np
from jax import lax
from jax.experimental import pallas as pl
from jax.experimental.pallas import tpu as pltpu
from jax.sharding import PartitionSpec as P

N = 1024
Q = 256
SUB = 16
SPOT = 2 * SUB
BF = jnp.bfloat16
F32 = jnp.float32
CODE = 25.0


def bf16(table):
    return np.asarray(table, np.float32).astype(jnp.bfloat16)


ORDERS = {
    "plain": lambda at: at,
    "send": lambda at: (at % 128) // 16 * 32 + at // 128 * 16 + at % 16,
    "sub": lambda at: at % SUB * SUB + at // SUB,
}


def angle_tables():
    n = np.arange(Q)
    turn = 2.0 * np.pi * ((n[:, None] * n[None, :]) % Q) / Q
    cos, sin = np.cos(turn) / 16.0, np.sin(turn) / 16.0
    forward = np.block([[cos, -sin], [sin, cos]])
    inverse = np.block([[cos, sin], [-sin, cos]])
    tables = {"forward": bf16(forward)}
    for name, order in ORDERS.items():
        tables[name] = bf16(inverse[:, np.concatenate([order(n), Q + order(n)])])
    return tables


def spot_table():
    turn = 2.0 * np.pi * ((np.arange(SPOT)[:, None] * np.arange(SUB)[None, :]) % SPOT) / SPOT
    wave = (np.cos(turn) - 1j * np.sin(turn)) / math.sqrt(SUB)
    kron = wave[:, None, None, :] * wave[None, :, :, None]
    kron = kron.reshape(SPOT * SPOT, SUB * SUB)
    return bf16(np.block([[kron.real, -kron.imag], [kron.imag, kron.real]]).T)


def sincos(x):
    y = 0.5 * x
    z = y * y
    s = 2.6048728614114225e-06
    for a in (-0.0001980891975108534, 0.008333048783242702, -0.16666658222675323, 1.0):
        s = s * z + a
    s = s * y
    c = 2.3149976186687127e-05
    for a in (-0.0013853529235348105, 0.04166356101632118, -0.4999990463256836, 0.9999999403953552):
        c = c * z + a
    t = s + s
    return 1.0 - t * s, t * c


def coded(phase):
    return jnp.exp(CODE * phase).astype(BF)


def decoded(code):
    return jnp.log(code.astype(F32)) * (1.0 / CODE)


def twiddles(out):
    k1 = lax.broadcasted_iota(jnp.int32, (4, Q), 0)
    at = lax.broadcasted_iota(jnp.int32, (4, Q), 1)
    for i, order in enumerate(ORDERS.values()):
        turns = (k1 * order(at)).astype(F32) * (1.0 / N)
        turns = jnp.where(turns > 0.5, turns - 1.0, turns)
        out[8 * i : 8 * i + 4, :], out[8 * i + 4 : 8 * i + 8, :] = sincos(turns * (2.0 * math.pi))


def spectra(shared, out):
    d = []
    for layer in range(4):
        tail = shared[layer, 0:16, N : N + 128].astype(F32)
        d.append((tail[0:1] + tail[1:2]) + tail[2:3])
    d = jnp.concatenate([jnp.concatenate(d, axis=0)] * (N // 128), axis=1)
    place = lax.broadcasted_iota(jnp.int32, (4, N), 1)
    k = 4 * (place % Q) + place // Q
    m = jnp.where(k < N // 2, k, k - N).astype(F32)
    turns = d * (m * m * (0.5 / (N * N)))
    frac = turns - jnp.floor(turns + 0.5)
    cos, sin = sincos(frac * (2.0 * math.pi))
    out[0:4, :], out[4:8, :] = 0.25 * cos, -0.25 * sin


def twisted(twiddle, order, k1):
    row = 8 * list(ORDERS).index(order) + k1
    return twiddle[row : row + 1, :], twiddle[row + 4 : row + 5, :]


def granules(parts, width):
    parts = list(parts)
    lane = lax.broadcasted_iota(jnp.int32, parts[0].shape, 1) // width
    bit = 1
    while bit < len(parts):
        high = (lane & bit) != 0
        for i in range(len(parts)):
            if i & bit:
                continue
            a, b = parts[i], parts[i | bit]
            parts[i] = jnp.where(high, pltpu.roll(b, width * bit, 1), a)
            parts[i | bit] = jnp.where(high, b, pltpu.roll(a, 128 - width * bit, 1))
        bit *= 2
    return parts


def gathered(block, base, first):
    columns = []
    for start in range(base, base + 32, 4):
        parts = [block[start + t, first : first + 16, :] for t in range(4)]
        columns.append(granules(parts, 32))
    return [jnp.concatenate([c[g] for c in columns], axis=1).astype(F32) for g in range(4)]


def field_of(block, base=0):
    groups = gathered(block, base, 0)
    return (
        jnp.concatenate([groups[0], groups[2]], axis=0),
        jnp.concatenate([groups[1], groups[3]], axis=0),
    )


def quarters(x):
    return [x[:, Q * n : Q * n + Q] for n in range(4)]


def forward(re, im, layer, spectrum_rows, twiddle, table):
    ar, ai = re[0] + re[2], im[0] + im[2]
    br, bi = re[0] - re[2], im[0] - im[2]
    cr, ci = re[1] + re[3], im[1] + im[3]
    dr, di = re[1] - re[3], im[1] - im[3]
    outs = [
        (ar + cr, ai + ci),
        (br + di, bi - dr),
        (ar - cr, ai - ci),
        (br - di, bi + dr),
    ]
    rows = []
    for k1, (r, m) in enumerate(outs):
        if k1:
            c, s = twisted(twiddle, "plain", k1)
            r, m = r * c + m * s, m * c - r * s
        rows.append(jnp.concatenate([r, m], axis=1).astype(BF))
    z = jnp.dot(jnp.concatenate(rows, axis=0), table[...], preferred_element_type=F32)
    spectrum = []
    size = re[0].shape[0]
    for k1 in range(4):
        zr, zi = z[size * k1 : size * k1 + size, :Q], z[size * k1 : size * k1 + size, Q:]
        hr = spectrum_rows[layer : layer + 1, Q * k1 : Q * k1 + Q]
        hi = spectrum_rows[layer + 4 : layer + 5, Q * k1 : Q * k1 + Q]
        spectrum.append(((zr * hr - zi * hi).astype(BF), (zr * hi + zi * hr).astype(BF)))
    return spectrum


def inverse(spectrum, order, twiddle, table):
    stacked = jnp.concatenate([jnp.concatenate(s, axis=1) for s in spectrum], axis=0)
    y = jnp.dot(stacked, table[...], preferred_element_type=F32)
    outs = []
    size = spectrum[0][0].shape[0]
    for k1 in range(4):
        r, m = y[size * k1 : size * k1 + size, :Q], y[size * k1 : size * k1 + size, Q:]
        if k1:
            c, s = twisted(twiddle, order, k1)
            r, m = r * c - m * s, m * c + r * s
        outs.append((r, m))
    (r0, i0), (r1, i1), (r2, i2), (r3, i3) = outs
    ar, ai, br, bi = r0 + r2, i0 + i2, r0 - r2, i0 - i2
    cr, ci, dr, di = r1 + r3, i1 + i3, r1 - r3, i1 - i3
    re = [ar + cr, br - di, ar - cr, br + di]
    im = [ai + ci, bi + dr, ai - ci, bi - dr]
    return re, im


def sent(spectrum, twiddle, table, out, turned=F32):
    for n1, (r, m) in enumerate(zip(*inverse(spectrum, "send", twiddle, table))):
        x = jnp.concatenate([r[:, :128], m[:, :128], r[:, 128:], m[:, 128:]], axis=0)
        x = x.astype(turned).T.astype(BF).reshape(8, 16, 128)
        for base in range(0, out.shape[0], 32):
            out[base + 8 * n1 : base + 8 * n1 + 8, 0:16, :] = x


def through_screen(re, im, phase):
    cos, sin = sincos(phase)
    out_re, out_im = [], []
    for r, m, c, s in zip(re, im, quarters(cos), quarters(sin)):
        out_re.append(r * c - m * s)
        out_im.append(r * s + m * c)
    return out_re, out_im


def payload_kernel(
    distance, far_screens, far_targets, far_counts,
    shared, picks, twiddle,
    screens, targets, counts, sems,
):
    group = lax.axis_index("layer")
    copies = [
        pltpu.make_async_copy(source, target, sems.at[i])
        for i, (source, target) in enumerate([
            (far_screens, screens), (far_targets, targets), (far_counts, counts),
        ])
    ]
    for copy in copies:
        copy.start()
    d = jnp.full((32, 128), distance[0], F32)
    high = d.astype(BF).astype(F32)
    middle = (d - high).astype(BF).astype(F32)
    low = (d - high) - middle
    row = lax.broadcasted_iota(jnp.int32, (32, 128), 0)
    tail = jnp.where(row == 0, high, jnp.where(row == 1, middle, jnp.where(row == 2, low, 0.0)))
    tail = tail.astype(BF)
    twiddles(twiddle)
    for copy in copies:
        copy.wait()
    phase = coded(screens[0])
    for other in range(4):
        shared[other, :, 0:N] = phase
        shared[other, :, N : N + 128] = tail
    picks[...] = jnp.where(group < counts[...], targets[...], -1)


def first_kernel(launch, shared, twiddle, table, send, out, h):
    spectra(shared, h)
    field = lax.axis_index("layer") % 2
    re, im = quarters(launch[field, 0].astype(F32)), quarters(launch[field, 1].astype(F32))
    re, im = through_screen(re, im, decoded(shared[0, :, 0:N]))
    sent(forward(re, im, 0, h, twiddle, table), twiddle, send, out)
    both = jnp.concatenate([shared[1, :, 0:N], shared[3, :, 0:N]], axis=0).astype(F32)
    for block in range(8):
        piece = both[:, 128 * block : 128 * block + 128].T.reshape(4, 2, 16, 64)
        out[4 * block : 4 * block + 4, 16:32, :] = jnp.concatenate(
            [piece[:, 0], piece[:, 1]], axis=2
        ).astype(BF)


def middle(layer, came, phase, h, twiddle, table, back, send, out):
    re, im = field_of(came)
    spectrum = forward(quarters(re), quarters(im), layer, h, twiddle, table)
    re, im = inverse(spectrum, "plain", twiddle, back)
    re, im = through_screen(re, im, phase)
    sent(forward(re, im, layer + 1, h, twiddle, table), twiddle, send, out, BF)


def column_kernel(layer, came, carried, *rest):
    groups = gathered(carried, 0, 16)
    which = layer // 2
    phase = decoded(jnp.concatenate([groups[which], groups[2 + which]], axis=0))
    middle(layer, came, phase, *rest)


def row_kernel(layer, came, shared, *rest):
    middle(layer, came, decoded(shared[layer + 1, :, 0:N]), *rest)


def last_kernel(
    came, h, twiddle, table, back, back_sub, spots, templates, picks,
    far_pupil, result,
    cells, pupil, sem,
):
    fields = [field_of(came, 0), field_of(came, 32)]
    re, im = [quarters(jnp.concatenate(x, axis=0)) for x in zip(*fields)]
    spectrum = forward(re, im, 3, h, twiddle, table)
    for part, x in enumerate(inverse(spectrum, "sub", twiddle, back_sub)):
        for field in range(2):
            for upper in range(2):
                parts = [
                    x[n1][32 * field + 16 * a : 32 * field + 16 * a + 16,
                          128 * upper : 128 * upper + 128].astype(BF)
                    for a in range(2)
                    for n1 in range(4)
                ]
                for k, piece in enumerate(granules(parts, 16)):
                    row = part * 256 + (upper * 8 + k) * 16
                    cells[row : row + 16, 128 * field : 128 * field + 128] = piece
    re, im = inverse(spectrum, "plain", twiddle, back)
    for n in range(4):
        for field in range(2):
            rows = slice(32 * field, 32 * field + 32)
            pupil[field, 0, :, Q * n : Q * n + Q] = re[n][rows].astype(BF)
            pupil[field, 1, :, Q * n : Q * n + Q] = im[n][rows].astype(BF)
    written = pltpu.make_async_copy(pupil, far_pupil, sem)
    written.start()
    place = lax.broadcasted_iota(jnp.int32, (128, 32), 0)
    chosen = jnp.where(place == picks[...], 1.0, 0.0).astype(F32).T.astype(BF)
    slots = [
        lax.dot_general(
            chosen,
            cells[:, 128 * field : 128 * field + 128],
            (((1,), (1,)), ((), ())),
            preferred_element_type=F32,
        ).astype(BF)
        for field in range(2)
    ]
    spot = jnp.dot(jnp.concatenate(slots, axis=0), spots[...], preferred_element_type=F32)
    intensity = (spot[:, :1024] * spot[:, :1024] + spot[:, 1024:] * spot[:, 1024:]).astype(BF)
    total = lax.dot_general(
        intensity, templates[...], (((1,), (1,)), ((), ())), preferred_element_type=F32
    )
    for field in range(2):
        result[:, 16 * field : 16 * field + 16] = total[32 * field : 32 * field + 32]
    written.wait()


VMEM = pl.BlockSpec(memory_space=pltpu.VMEM)
SMEM = pl.BlockSpec(memory_space=pltpu.SMEM)
FAR = pl.BlockSpec(memory_space=pltpu.HBM)


def call(kernel, shapes, *operands, name=None, **specs):
    return pl.pallas_call(
        kernel,
        out_shape=shapes,
        compiler_params=pltpu.CompilerParams(vmem_limit_bytes=24 * 1024 * 1024),
        name=name,
        **specs,
    )(*operands)


def exchanged(block, axis="strip", groups=None):
    return lax.all_to_all(
        block, axis, split_axis=0, concat_axis=0, tiled=True, axis_index_groups=groups
    )


def per_device(launch, screens, distance, templates, send_table, send_counts):
    tables = {name: jnp.asarray(value) for name, value in angle_tables().items()}
    table, back, send = tables["forward"], tables["plain"], tables["send"]

    payload, picks, twiddle = call(
        payload_kernel,
        (
            jax.ShapeDtypeStruct((4, 32, N + 128), BF),
            jax.ShapeDtypeStruct((1, 32), jnp.int32),
            jax.ShapeDtypeStruct((24, Q), F32),
        ),
        distance,
        *[
            pltpu.with_memory_space_constraint(x, pltpu.HBM)
            for x in (
                screens, send_table.reshape(1, 32), send_counts
            )
        ],
        in_specs=[SMEM] + [FAR] * 3,
        out_specs=(VMEM,) * 3,
        scratch_shapes=[
            pltpu.VMEM(screens.shape, F32),
            pltpu.VMEM((1, 32), jnp.int32),
            pltpu.VMEM((1, 32), jnp.int32),
            pltpu.SemaphoreType.DMA((3,)),
        ],
        cost_estimate=pl.CostEstimate(flops=1500000000, bytes_accessed=4000000, transcendentals=0),
        name="payload",
    )
    shared = exchanged(payload, "layer")

    wide = jax.ShapeDtypeStruct((32, 32, 128), BF)
    plain = jax.ShapeDtypeStruct((32, 16, 128), BF)
    twice = jax.ShapeDtypeStruct((64, 16, 128), BF)
    pairs = [[32 * group + strip for group in pair for strip in range(32)] for pair in ((0, 1), (2, 3))]
    leaving, h = call(
        first_kernel, (wide, jax.ShapeDtypeStruct((8, N), F32)),
        launch, shared, twiddle, table, send, name="rows0",
    )
    carried = exchanged(leaving)

    def columns(layer, came, shape, name):
        def kernel(*refs):
            column_kernel(layer, *refs)

        return call(kernel, shape, came, carried, h, twiddle, table, back, send, name=name)

    def rows(layer, came, name):
        def kernel(*refs):
            row_kernel(layer, *refs)

        return call(kernel, plain, came, shared, h, twiddle, table, back, send, name=name)

    came = exchanged(columns(0, carried, plain, "columns01"))
    came = exchanged(rows(1, came, "rows12"))
    came = exchanged(columns(2, came, twice, "columns23"), ("layer", "strip"), pairs)

    spots = jnp.asarray(spot_table())
    pupil, result = call(
        last_kernel,
        (jax.ShapeDtypeStruct(launch.shape, BF), jax.ShapeDtypeStruct((32, 32), F32)),
        came, h, twiddle, table, back, tables["sub"], spots, templates.T, picks,
        in_specs=[VMEM] * 9,
        out_specs=(FAR, VMEM),
        scratch_shapes=[
            pltpu.VMEM((512, 256), BF),
            pltpu.VMEM(launch.shape, BF),
            pltpu.SemaphoreType.DMA,
        ],
        name="rows3",
    )
    return (pupil, exchanged(result).reshape(1, 32, 1, 2, 16))


def solution(mesh):
    placed = (
        P(None, None, "strip", None),
        P("layer", "strip", None),
        P("layer"),
        P(),
        P("strip", None, "layer"),
        P("strip", None),
    )
    return jax.shard_map(
        per_device,
        mesh=mesh,
        in_specs=placed,
        out_specs=(P(None, None, "strip", None), P("strip", None, "layer", None, None)),
        check_vma=False,
    )
```

```python
import math

import jax
import jax.numpy as jnp
import numpy as np
from jax import lax
from jax.experimental import pallas as pl
from jax.experimental.pallas import tpu as pltpu
from jax.sharding import PartitionSpec as P

N = 1024
Q = 256
SUB = 16
SPOT = 2 * SUB
BF = jnp.bfloat16
F32 = jnp.float32
CODE = 25.0


def bf16(table):
    return np.asarray(table, np.float32).astype(jnp.bfloat16)


ORDERS = {
    "plain": lambda at: at,
    "send": lambda at: (at % 128) // 16 * 32 + at // 128 * 16 + at % 16,
    "sub": lambda at: at % SUB * SUB + at // SUB,
}


def angle_tables():
    n = np.arange(Q)
    turn = 2.0 * np.pi * ((n[:, None] * n[None, :]) % Q) / Q
    cos, sin = np.cos(turn) / 16.0, np.sin(turn) / 16.0
    forward = np.block([[cos, -sin], [sin, cos]])
    inverse = np.block([[cos, sin], [-sin, cos]])
    tables = {"forward": bf16(forward)}
    for name, order in ORDERS.items():
        tables[name] = bf16(inverse[:, np.concatenate([order(n), Q + order(n)])])
    return tables


def spot_table():
    turn = 2.0 * np.pi * ((np.arange(SPOT)[:, None] * np.arange(SUB)[None, :]) % SPOT) / SPOT
    wave = (np.cos(turn) - 1j * np.sin(turn)) / math.sqrt(SUB)
    kron = wave[:, None, None, :] * wave[None, :, :, None]
    kron = kron.reshape(SPOT * SPOT, SUB * SUB)
    return bf16(np.block([[kron.real, -kron.imag], [kron.imag, kron.real]]).T)


def sincos(x):
    y = 0.5 * x
    z = y * y
    s = 2.6048728614114225e-06
    for a in (-0.0001980891975108534, 0.008333048783242702, -0.16666658222675323, 1.0):
        s = s * z + a
    s = s * y
    c = 2.3149976186687127e-05
    for a in (-0.0013853529235348105, 0.04166356101632118, -0.4999990463256836, 0.9999999403953552):
        c = c * z + a
    t = s + s
    return 1.0 - t * s, t * c


def coded(phase):
    return jnp.exp(CODE * phase).astype(BF)


def decoded(code):
    return jnp.log(code.astype(F32)) * (1.0 / CODE)


def twiddles(out):
    k1 = lax.broadcasted_iota(jnp.int32, (4, Q), 0)
    at = lax.broadcasted_iota(jnp.int32, (4, Q), 1)
    for i, order in enumerate(ORDERS.values()):
        turns = (k1 * order(at)).astype(F32) * (1.0 / N)
        turns = jnp.where(turns > 0.5, turns - 1.0, turns)
        out[8 * i : 8 * i + 4, :], out[8 * i + 4 : 8 * i + 8, :] = sincos(turns * (2.0 * math.pi))


def spectra(shared, out):
    d = []
    for layer in range(4):
        tail = shared[layer, 0:16, N : N + 128].astype(F32)
        d.append((tail[0:1] + tail[1:2]) + tail[2:3])
    d = jnp.concatenate([jnp.concatenate(d, axis=0)] * (N // 128), axis=1)
    place = lax.broadcasted_iota(jnp.int32, (4, N), 1)
    k = 4 * (place % Q) + place // Q
    m = jnp.where(k < N // 2, k, k - N).astype(F32)
    turns = d * (m * m * (0.5 / (N * N)))
    frac = turns - jnp.floor(turns + 0.5)
    cos, sin = sincos(frac * (2.0 * math.pi))
    out[0:4, :], out[4:8, :] = 0.25 * cos, -0.25 * sin


def twisted(twiddle, order, k1):
    row = 8 * list(ORDERS).index(order) + k1
    return twiddle[row : row + 1, :], twiddle[row + 4 : row + 5, :]


def granules(parts, width):
    parts = list(parts)
    lane = lax.broadcasted_iota(jnp.int32, parts[0].shape, 1) // width
    bit = 1
    while bit < len(parts):
        high = (lane & bit) != 0
        for i in range(len(parts)):
            if i & bit:
                continue
            a, b = parts[i], parts[i | bit]
            parts[i] = jnp.where(high, pltpu.roll(b, width * bit, 1), a)
            parts[i | bit] = jnp.where(high, b, pltpu.roll(a, 128 - width * bit, 1))
        bit *= 2
    return parts


def gathered(block, base, first):
    columns = []
    for start in range(base, base + 32, 4):
        parts = [block[start + t, first : first + 16, :] for t in range(4)]
        columns.append(granules(parts, 32))
    return [jnp.concatenate([c[g] for c in columns], axis=1).astype(F32) for g in range(4)]


def field_of(block, base=0):
    groups = gathered(block, base, 0)
    return (
        jnp.concatenate([groups[0], groups[2]], axis=0),
        jnp.concatenate([groups[1], groups[3]], axis=0),
    )


def quarters(x):
    return [x[:, Q * n : Q * n + Q] for n in range(4)]


def forward(re, im, layer, spectrum_rows, twiddle, table):
    ar, ai = re[0] + re[2], im[0] + im[2]
    br, bi = re[0] - re[2], im[0] - im[2]
    cr, ci = re[1] + re[3], im[1] + im[3]
    dr, di = re[1] - re[3], im[1] - im[3]
    outs = [
        (ar + cr, ai + ci),
        (br + di, bi - dr),
        (ar - cr, ai - ci),
        (br - di, bi + dr),
    ]
    rows = []
    for k1, (r, m) in enumerate(outs):
        if k1:
            c, s = twisted(twiddle, "plain", k1)
            r, m = r * c + m * s, m * c - r * s
        rows.append(jnp.concatenate([r, m], axis=1).astype(BF))
    z = jnp.dot(jnp.concatenate(rows, axis=0), table[...], preferred_element_type=F32)
    spectrum = []
    size = re[0].shape[0]
    for k1 in range(4):
        zr, zi = z[size * k1 : size * k1 + size, :Q], z[size * k1 : size * k1 + size, Q:]
        hr = spectrum_rows[layer : layer + 1, Q * k1 : Q * k1 + Q]
        hi = spectrum_rows[layer + 4 : layer + 5, Q * k1 : Q * k1 + Q]
        spectrum.append(((zr * hr - zi * hi).astype(BF), (zr * hi + zi * hr).astype(BF)))
    return spectrum


def inverse(spectrum, order, twiddle, table):
    stacked = jnp.concatenate([jnp.concatenate(s, axis=1) for s in spectrum], axis=0)
    y = jnp.dot(stacked, table[...], preferred_element_type=F32)
    outs = []
    size = spectrum[0][0].shape[0]
    for k1 in range(4):
        r, m = y[size * k1 : size * k1 + size, :Q], y[size * k1 : size * k1 + size, Q:]
        if k1:
            c, s = twisted(twiddle, order, k1)
            r, m = r * c - m * s, m * c + r * s
        outs.append((r, m))
    (r0, i0), (r1, i1), (r2, i2), (r3, i3) = outs
    ar, ai, br, bi = r0 + r2, i0 + i2, r0 - r2, i0 - i2
    cr, ci, dr, di = r1 + r3, i1 + i3, r1 - r3, i1 - i3
    re = [ar + cr, br - di, ar - cr, br + di]
    im = [ai + ci, bi + dr, ai - ci, bi - dr]
    return re, im


def sent(spectrum, twiddle, table, out, turned=F32):
    for n1, (r, m) in enumerate(zip(*inverse(spectrum, "send", twiddle, table))):
        x = jnp.concatenate([r[:, :128], m[:, :128], r[:, 128:], m[:, 128:]], axis=0)
        x = x.astype(turned).T.astype(BF).reshape(8, 16, 128)
        for base in range(0, out.shape[0], 32):
            out[base + 8 * n1 : base + 8 * n1 + 8, 0:16, :] = x


def through_screen(re, im, phase):
    cos, sin = sincos(phase)
    out_re, out_im = [], []
    for r, m, c, s in zip(re, im, quarters(cos), quarters(sin)):
        out_re.append(r * c - m * s)
        out_im.append(r * s + m * c)
    return out_re, out_im


def payload_kernel(
    distance, far_screens, far_targets, far_counts,
    shared, picks, twiddle,
    screens, targets, counts, sems,
):
    group = lax.axis_index("layer")
    copies = [
        pltpu.make_async_copy(source, target, sems.at[i])
        for i, (source, target) in enumerate([
            (far_screens, screens), (far_targets, targets), (far_counts, counts),
        ])
    ]
    for copy in copies:
        copy.start()
    d = jnp.full((32, 128), distance[0], F32)
    high = d.astype(BF).astype(F32)
    middle = (d - high).astype(BF).astype(F32)
    low = (d - high) - middle
    row = lax.broadcasted_iota(jnp.int32, (32, 128), 0)
    tail = jnp.where(row == 0, high, jnp.where(row == 1, middle, jnp.where(row == 2, low, 0.0)))
    tail = tail.astype(BF)
    twiddles(twiddle)
    for copy in copies:
        copy.wait()
    phase = coded(screens[0])
    for other in range(4):
        shared[other, :, 0:N] = phase
        shared[other, :, N : N + 128] = tail
    picks[...] = jnp.where(group < counts[...], targets[...], -1)


def first_kernel(launch, shared, twiddle, table, send, out, h):
    both = jnp.concatenate([shared[1, :, 0:N], shared[3, :, 0:N]], axis=0).astype(F32)
    for block in range(8):
        piece = both[:, 128 * block : 128 * block + 128].T.reshape(4, 2, 16, 64)
        out[4 * block : 4 * block + 4, 16:32, :] = jnp.concatenate(
            [piece[:, 0], piece[:, 1]], axis=2
        ).astype(BF)
    spectra(shared, h)
    field = lax.axis_index("layer") % 2
    re, im = quarters(launch[field, 0].astype(F32)), quarters(launch[field, 1].astype(F32))
    re, im = through_screen(re, im, decoded(shared[0, :, 0:N]))
    sent(forward(re, im, 0, h, twiddle, table), twiddle, send, out)


def middle(layer, came, phase, h, twiddle, table, back, send, out):
    re, im = field_of(came)
    spectrum = forward(quarters(re), quarters(im), layer, h, twiddle, table)
    re, im = inverse(spectrum, "plain", twiddle, back)
    re, im = through_screen(re, im, phase)
    sent(forward(re, im, layer + 1, h, twiddle, table), twiddle, send, out, BF)


def column_kernel(layer, came, carried, *rest):
    groups = gathered(carried, 0, 16)
    which = layer // 2
    phase = decoded(jnp.concatenate([groups[which], groups[2 + which]], axis=0))
    middle(layer, came, phase, *rest)


def row_kernel(layer, came, shared, *rest):
    middle(layer, came, decoded(shared[layer + 1, :, 0:N]), *rest)


def last_kernel(
    came, h, twiddle, table, back, back_sub, spots, templates, picks,
    far_pupil, result,
    cells, pupil, sem,
):
    fields = [field_of(came, 0), field_of(came, 32)]
    re, im = [quarters(jnp.concatenate(x, axis=0)) for x in zip(*fields)]
    spectrum = forward(re, im, 3, h, twiddle, table)
    for part, x in enumerate(inverse(spectrum, "sub", twiddle, back_sub)):
        for field in range(2):
            for upper in range(2):
                parts = [
                    x[n1][32 * field + 16 * a : 32 * field + 16 * a + 16,
                          128 * upper : 128 * upper + 128].astype(BF)
                    for a in range(2)
                    for n1 in range(4)
                ]
                for k, piece in enumerate(granules(parts, 16)):
                    row = part * 256 + (upper * 8 + k) * 16
                    cells[row : row + 16, 128 * field : 128 * field + 128] = piece
    re, im = inverse(spectrum, "plain", twiddle, back)
    for n in range(4):
        for field in range(2):
            rows = slice(32 * field, 32 * field + 32)
            pupil[field, 0, :, Q * n : Q * n + Q] = re[n][rows].astype(BF)
            pupil[field, 1, :, Q * n : Q * n + Q] = im[n][rows].astype(BF)
    written = pltpu.make_async_copy(pupil, far_pupil, sem)
    written.start()
    place = lax.broadcasted_iota(jnp.int32, (128, 32), 0)
    chosen = jnp.where(place == picks[...], 1.0, 0.0).astype(F32).T.astype(BF)
    slots = [
        lax.dot_general(
            chosen,
            cells[:, 128 * field : 128 * field + 128],
            (((1,), (1,)), ((), ())),
            preferred_element_type=F32,
        ).astype(BF)
        for field in range(2)
    ]
    picked = jnp.concatenate(slots, axis=0)
    intensity = []
    for at in range(0, 1024, 256):
        re = jnp.dot(picked, spots[:, at : at + 256], preferred_element_type=F32)
        im = jnp.dot(picked, spots[:, 1024 + at : 1024 + at + 256], preferred_element_type=F32)
        intensity.append((re * re + im * im).astype(BF))
    total = lax.dot_general(
        jnp.concatenate(intensity, axis=1),
        templates[...],
        (((1,), (1,)), ((), ())),
        preferred_element_type=F32,
    )
    for field in range(2):
        result[:, 16 * field : 16 * field + 16] = total[32 * field : 32 * field + 32]
    written.wait()


VMEM = pl.BlockSpec(memory_space=pltpu.VMEM)
SMEM = pl.BlockSpec(memory_space=pltpu.SMEM)
FAR = pl.BlockSpec(memory_space=pltpu.HBM)


def call(kernel, shapes, *operands, name=None, **specs):
    return pl.pallas_call(
        kernel,
        out_shape=shapes,
        compiler_params=pltpu.CompilerParams(vmem_limit_bytes=24 * 1024 * 1024),
        name=name,
        **specs,
    )(*operands)


def exchanged(block, axis="strip", groups=None):
    return lax.all_to_all(
        block, axis, split_axis=0, concat_axis=0, tiled=True, axis_index_groups=groups
    )


def per_device(launch, screens, distance, templates, send_table, send_counts):
    tables = {name: jnp.asarray(value) for name, value in angle_tables().items()}
    table, back, send = tables["forward"], tables["plain"], tables["send"]

    payload, picks, twiddle = call(
        payload_kernel,
        (
            jax.ShapeDtypeStruct((4, 32, N + 128), BF),
            jax.ShapeDtypeStruct((1, 32), jnp.int32),
            jax.ShapeDtypeStruct((24, Q), F32),
        ),
        distance,
        *[
            pltpu.with_memory_space_constraint(x, pltpu.HBM)
            for x in (
                screens, send_table.reshape(1, 32), send_counts
            )
        ],
        in_specs=[SMEM] + [FAR] * 3,
        out_specs=(VMEM,) * 3,
        scratch_shapes=[
            pltpu.VMEM(screens.shape, F32),
            pltpu.VMEM((1, 32), jnp.int32),
            pltpu.VMEM((1, 32), jnp.int32),
            pltpu.SemaphoreType.DMA((3,)),
        ],
        cost_estimate=pl.CostEstimate(flops=1500000000, bytes_accessed=4000000, transcendentals=0),
        name="payload",
    )
    shared = exchanged(payload, "layer")

    wide = jax.ShapeDtypeStruct((32, 32, 128), BF)
    plain = jax.ShapeDtypeStruct((32, 16, 128), BF)
    twice = jax.ShapeDtypeStruct((64, 16, 128), BF)
    pairs = [[32 * group + strip for group in pair for strip in range(32)] for pair in ((0, 1), (2, 3))]
    leaving, h = call(
        first_kernel, (wide, jax.ShapeDtypeStruct((8, N), F32)),
        launch, shared, twiddle, table, send, name="rows0",
    )
    carried = exchanged(leaving)

    def columns(layer, came, shape, name):
        def kernel(*refs):
            column_kernel(layer, *refs)

        return call(kernel, shape, came, carried, h, twiddle, table, back, send, name=name)

    def rows(layer, came, name):
        def kernel(*refs):
            row_kernel(layer, *refs)

        return call(kernel, plain, came, shared, h, twiddle, table, back, send, name=name)

    came = exchanged(columns(0, carried, plain, "columns01"))
    came = exchanged(rows(1, came, "rows12"))
    came = exchanged(columns(2, came, twice, "columns23"), ("layer", "strip"), pairs)

    spots = jnp.asarray(spot_table())
    pupil, result = call(
        last_kernel,
        (jax.ShapeDtypeStruct(launch.shape, BF), jax.ShapeDtypeStruct((32, 32), F32)),
        came, h, twiddle, table, back, tables["sub"], spots, templates.T, picks,
        in_specs=[VMEM] * 9,
        out_specs=(FAR, VMEM),
        scratch_shapes=[
            pltpu.VMEM((512, 256), BF),
            pltpu.VMEM(launch.shape, BF),
            pltpu.SemaphoreType.DMA,
        ],
        name="rows3",
    )
    return (pupil, exchanged(result).reshape(1, 32, 1, 2, 16))


def solution(mesh):
    placed = (
        P(None, None, "strip", None),
        P("layer", "strip", None),
        P("layer"),
        P(),
        P("strip", None, "layer"),
        P("strip", None),
    )
    return jax.shard_map(
        per_device,
        mesh=mesh,
        in_specs=placed,
        out_specs=(P(None, None, "strip", None), P("strip", None, "layer", None, None)),
        check_vma=False,
    )
```

```python
import math

import jax
import jax.numpy as jnp
import numpy as np
from jax import lax
from jax.experimental import pallas as pl
from jax.experimental.pallas import tpu as pltpu
from jax.sharding import PartitionSpec as P

N = 1024
Q = 256
SUB = 16
SPOT = 2 * SUB
BF = jnp.bfloat16
F32 = jnp.float32
CODE = 25.0


def bf16(table):
    return np.asarray(table, np.float32).astype(jnp.bfloat16)


ORDERS = {
    "plain": lambda at: at,
    "send": lambda at: (at % 128) // 16 * 32 + at // 128 * 16 + at % 16,
    "sub": lambda at: at % SUB * SUB + at // SUB,
}


def angle_tables():
    n = np.arange(Q)
    turn = 2.0 * np.pi * ((n[:, None] * n[None, :]) % Q) / Q
    cos, sin = np.cos(turn) / 16.0, np.sin(turn) / 16.0
    forward = np.block([[cos, -sin], [sin, cos]])
    inverse = np.block([[cos, sin], [-sin, cos]])
    tables = {"forward": bf16(forward)}
    for name, order in ORDERS.items():
        tables[name] = bf16(inverse[:, np.concatenate([order(n), Q + order(n)])])
    return tables


def spot_table():
    turn = 2.0 * np.pi * ((np.arange(SPOT)[:, None] * np.arange(SUB)[None, :]) % SPOT) / SPOT
    wave = (np.cos(turn) - 1j * np.sin(turn)) / math.sqrt(SUB)
    kron = wave[:, None, None, :] * wave[None, :, :, None]
    kron = kron.reshape(SPOT * SPOT, SUB * SUB)
    return bf16(np.block([[kron.real, -kron.imag], [kron.imag, kron.real]]).T)


def sincos(x):
    y = 0.5 * x
    z = y * y
    s = 2.6048728614114225e-06
    for a in (-0.0001980891975108534, 0.008333048783242702, -0.16666658222675323, 1.0):
        s = s * z + a
    s = s * y
    c = 2.3149976186687127e-05
    for a in (-0.0013853529235348105, 0.04166356101632118, -0.4999990463256836, 0.9999999403953552):
        c = c * z + a
    t = s + s
    return 1.0 - t * s, t * c


def coded(phase):
    return jnp.exp(CODE * phase).astype(BF)


def decoded(code):
    return jnp.log(code.astype(F32)) * (1.0 / CODE)


def twiddles(out):
    k1 = lax.broadcasted_iota(jnp.int32, (4, Q), 0)
    at = lax.broadcasted_iota(jnp.int32, (4, Q), 1)
    for i, order in enumerate(ORDERS.values()):
        turns = (k1 * order(at)).astype(F32) * (1.0 / N)
        turns = jnp.where(turns > 0.5, turns - 1.0, turns)
        out[8 * i : 8 * i + 4, :], out[8 * i + 4 : 8 * i + 8, :] = sincos(turns * (2.0 * math.pi))


def spectra(shared, out):
    d = []
    for layer in range(4):
        tail = shared[layer, 0:16, N : N + 128].astype(F32)
        d.append((tail[0:1] + tail[1:2]) + tail[2:3])
    d = jnp.concatenate([jnp.concatenate(d, axis=0)] * (N // 128), axis=1)
    place = lax.broadcasted_iota(jnp.int32, (4, N), 1)
    k = 4 * (place % Q) + place // Q
    m = jnp.where(k < N // 2, k, k - N).astype(F32)
    turns = d * (m * m * (0.5 / (N * N)))
    frac = turns - jnp.floor(turns + 0.5)
    cos, sin = sincos(frac * (2.0 * math.pi))
    out[0:4, :], out[4:8, :] = 0.25 * cos, -0.25 * sin


def twisted(twiddle, order, k1):
    row = 8 * list(ORDERS).index(order) + k1
    return twiddle[row : row + 1, :], twiddle[row + 4 : row + 5, :]


def granules(parts, width):
    parts = list(parts)
    lane = lax.broadcasted_iota(jnp.int32, parts[0].shape, 1) // width
    bit = 1
    while bit < len(parts):
        high = (lane & bit) != 0
        for i in range(len(parts)):
            if i & bit:
                continue
            a, b = parts[i], parts[i | bit]
            parts[i] = jnp.where(high, pltpu.roll(b, width * bit, 1), a)
            parts[i | bit] = jnp.where(high, b, pltpu.roll(a, 128 - width * bit, 1))
        bit *= 2
    return parts


def gathered(block, base, first):
    columns = []
    for start in range(base, base + 32, 4):
        parts = [block[start + t, first : first + 16, :] for t in range(4)]
        columns.append(granules(parts, 32))
    return [jnp.concatenate([c[g] for c in columns], axis=1).astype(F32) for g in range(4)]


def field_of(block, base=0):
    groups = gathered(block, base, 0)
    return (
        jnp.concatenate([groups[0], groups[2]], axis=0),
        jnp.concatenate([groups[1], groups[3]], axis=0),
    )


def quarters(x):
    return [x[:, Q * n : Q * n + Q] for n in range(4)]


def forward(re, im, layer, spectrum_rows, twiddle, table):
    ar, ai = re[0] + re[2], im[0] + im[2]
    br, bi = re[0] - re[2], im[0] - im[2]
    cr, ci = re[1] + re[3], im[1] + im[3]
    dr, di = re[1] - re[3], im[1] - im[3]
    outs = [
        (ar + cr, ai + ci),
        (br + di, bi - dr),
        (ar - cr, ai - ci),
        (br - di, bi + dr),
    ]
    rows = []
    for k1, (r, m) in enumerate(outs):
        if k1:
            c, s = twisted(twiddle, "plain", k1)
            r, m = r * c + m * s, m * c - r * s
        rows.append(jnp.concatenate([r, m], axis=1).astype(BF))
    z = jnp.dot(jnp.concatenate(rows, axis=0), table[...], preferred_element_type=F32)
    spectrum = []
    size = re[0].shape[0]
    for k1 in range(4):
        zr, zi = z[size * k1 : size * k1 + size, :Q], z[size * k1 : size * k1 + size, Q:]
        hr = spectrum_rows[layer : layer + 1, Q * k1 : Q * k1 + Q]
        hi = spectrum_rows[layer + 4 : layer + 5, Q * k1 : Q * k1 + Q]
        spectrum.append(((zr * hr - zi * hi).astype(BF), (zr * hi + zi * hr).astype(BF)))
    return spectrum


def inverse(spectrum, order, twiddle, table):
    stacked = jnp.concatenate([jnp.concatenate(s, axis=1) for s in spectrum], axis=0)
    y = jnp.dot(stacked, table[...], preferred_element_type=F32)
    outs = []
    size = spectrum[0][0].shape[0]
    for k1 in range(4):
        r, m = y[size * k1 : size * k1 + size, :Q], y[size * k1 : size * k1 + size, Q:]
        if k1:
            c, s = twisted(twiddle, order, k1)
            r, m = r * c - m * s, m * c + r * s
        outs.append((r, m))
    (r0, i0), (r1, i1), (r2, i2), (r3, i3) = outs
    ar, ai, br, bi = r0 + r2, i0 + i2, r0 - r2, i0 - i2
    cr, ci, dr, di = r1 + r3, i1 + i3, r1 - r3, i1 - i3
    re = [ar + cr, br - di, ar - cr, br + di]
    im = [ai + ci, bi + dr, ai - ci, bi - dr]
    return re, im


def sent(spectrum, twiddle, table, out, turned=F32):
    for n1, (r, m) in enumerate(zip(*inverse(spectrum, "send", twiddle, table))):
        x = jnp.concatenate([r[:, :128], m[:, :128], r[:, 128:], m[:, 128:]], axis=0)
        x = x.astype(turned).T.astype(BF).reshape(8, 16, 128)
        for base in range(0, out.shape[0], 32):
            out[base + 8 * n1 : base + 8 * n1 + 8, 0:16, :] = x


def through_screen(re, im, phase):
    cos, sin = sincos(phase)
    out_re, out_im = [], []
    for r, m, c, s in zip(re, im, quarters(cos), quarters(sin)):
        out_re.append(r * c - m * s)
        out_im.append(r * s + m * c)
    return out_re, out_im


def payload_kernel(
    distance, far_screens, far_targets, far_counts,
    shared, picks, twiddle,
    screens, targets, counts, sems,
):
    group = lax.axis_index("layer")
    copies = [
        pltpu.make_async_copy(source, target, sems.at[i])
        for i, (source, target) in enumerate([
            (far_screens, screens), (far_targets, targets), (far_counts, counts),
        ])
    ]
    for copy in copies:
        copy.start()
    d = jnp.full((32, 128), distance[0], F32)
    high = d.astype(BF).astype(F32)
    middle = (d - high).astype(BF).astype(F32)
    low = (d - high) - middle
    row = lax.broadcasted_iota(jnp.int32, (32, 128), 0)
    tail = jnp.where(row == 0, high, jnp.where(row == 1, middle, jnp.where(row == 2, low, 0.0)))
    tail = tail.astype(BF)
    twiddles(twiddle)
    for copy in copies:
        copy.wait()
    phase = coded(screens[0])
    for other in range(4):
        shared[other, :, 0:N] = phase
        shared[other, :, N : N + 128] = tail
    picks[...] = jnp.where(group < counts[...], targets[...], -1)


def first_kernel(launch, shared, twiddle, table, send, out, h):
    both = jnp.concatenate([shared[1, :, 0:N], shared[3, :, 0:N]], axis=0).astype(F32)
    for block in range(8):
        piece = both[:, 128 * block : 128 * block + 128].T.reshape(4, 2, 16, 64)
        out[4 * block : 4 * block + 4, 16:32, :] = jnp.concatenate(
            [piece[:, 0], piece[:, 1]], axis=2
        ).astype(BF)
    spectra(shared, h)
    field = lax.axis_index("layer") % 2
    re, im = quarters(launch[field, 0].astype(F32)), quarters(launch[field, 1].astype(F32))
    re, im = through_screen(re, im, decoded(shared[0, :, 0:N]))
    sent(forward(re, im, 0, h, twiddle, table), twiddle, send, out)


def middle(layer, came, phase, h, twiddle, table, back, send, out):
    re, im = field_of(came)
    spectrum = forward(quarters(re), quarters(im), layer, h, twiddle, table)
    re, im = inverse(spectrum, "plain", twiddle, back)
    re, im = through_screen(re, im, phase())
    sent(forward(re, im, layer + 1, h, twiddle, table), twiddle, send, out, BF)


def column_kernel(layer, came, carried, *rest):
    def phase():
        groups = gathered(carried, 0, 16)
        which = layer // 2
        return decoded(jnp.concatenate([groups[which], groups[2 + which]], axis=0))

    middle(layer, came, phase, *rest)


def row_kernel(layer, came, shared, *rest):
    middle(layer, came, lambda: decoded(shared[layer + 1, :, 0:N]), *rest)


def last_kernel(
    came, h, twiddle, table, back, back_sub, spots, templates, picks,
    far_pupil, result,
    cells, pupil, sem,
):
    fields = [field_of(came, 0), field_of(came, 32)]
    re, im = [quarters(jnp.concatenate(x, axis=0)) for x in zip(*fields)]
    spectrum = forward(re, im, 3, h, twiddle, table)
    for part, x in enumerate(inverse(spectrum, "sub", twiddle, back_sub)):
        for field in range(2):
            for upper in range(2):
                parts = [
                    x[n1][32 * field + 16 * a : 32 * field + 16 * a + 16,
                          128 * upper : 128 * upper + 128].astype(BF)
                    for a in range(2)
                    for n1 in range(4)
                ]
                for k, piece in enumerate(granules(parts, 16)):
                    row = part * 256 + (upper * 8 + k) * 16
                    cells[row : row + 16, 128 * field : 128 * field + 128] = piece
    re, im = inverse(spectrum, "plain", twiddle, back)
    for n in range(4):
        for field in range(2):
            rows = slice(32 * field, 32 * field + 32)
            pupil[field, 0, :, Q * n : Q * n + Q] = re[n][rows].astype(BF)
            pupil[field, 1, :, Q * n : Q * n + Q] = im[n][rows].astype(BF)
    written = pltpu.make_async_copy(pupil, far_pupil, sem)
    written.start()
    place = lax.broadcasted_iota(jnp.int32, (128, 32), 0)
    chosen = jnp.where(place == picks[...], 1.0, 0.0).astype(F32).T.astype(BF)
    slots = [
        lax.dot_general(
            chosen,
            cells[:, 128 * field : 128 * field + 128],
            (((1,), (1,)), ((), ())),
            preferred_element_type=F32,
        ).astype(BF)
        for field in range(2)
    ]
    picked = jnp.concatenate(slots, axis=0)
    intensity = []
    for at in range(0, 1024, 256):
        re = jnp.dot(picked, spots[:, at : at + 256], preferred_element_type=F32)
        im = jnp.dot(picked, spots[:, 1024 + at : 1024 + at + 256], preferred_element_type=F32)
        intensity.append((re * re + im * im).astype(BF))
    total = lax.dot_general(
        jnp.concatenate(intensity, axis=1),
        templates[...],
        (((1,), (1,)), ((), ())),
        preferred_element_type=F32,
    )
    for field in range(2):
        result[:, 16 * field : 16 * field + 16] = total[32 * field : 32 * field + 32]
    written.wait()


VMEM = pl.BlockSpec(memory_space=pltpu.VMEM)
SMEM = pl.BlockSpec(memory_space=pltpu.SMEM)
FAR = pl.BlockSpec(memory_space=pltpu.HBM)


def call(kernel, shapes, *operands, name=None, **specs):
    return pl.pallas_call(
        kernel,
        out_shape=shapes,
        compiler_params=pltpu.CompilerParams(vmem_limit_bytes=24 * 1024 * 1024),
        name=name,
        **specs,
    )(*operands)


def exchanged(block, axis="strip", groups=None):
    return lax.all_to_all(
        block, axis, split_axis=0, concat_axis=0, tiled=True, axis_index_groups=groups
    )


def per_device(launch, screens, distance, templates, send_table, send_counts):
    tables = {name: jnp.asarray(value) for name, value in angle_tables().items()}
    table, back, send = tables["forward"], tables["plain"], tables["send"]

    payload, picks, twiddle = call(
        payload_kernel,
        (
            jax.ShapeDtypeStruct((4, 32, N + 128), BF),
            jax.ShapeDtypeStruct((1, 32), jnp.int32),
            jax.ShapeDtypeStruct((24, Q), F32),
        ),
        distance,
        *[
            pltpu.with_memory_space_constraint(x, pltpu.HBM)
            for x in (
                screens, send_table.reshape(1, 32), send_counts
            )
        ],
        in_specs=[SMEM] + [FAR] * 3,
        out_specs=(VMEM,) * 3,
        scratch_shapes=[
            pltpu.VMEM(screens.shape, F32),
            pltpu.VMEM((1, 32), jnp.int32),
            pltpu.VMEM((1, 32), jnp.int32),
            pltpu.SemaphoreType.DMA((3,)),
        ],
        cost_estimate=pl.CostEstimate(flops=1500000000, bytes_accessed=4000000, transcendentals=0),
        name="payload",
    )
    shared = exchanged(payload, "layer")

    wide = jax.ShapeDtypeStruct((32, 32, 128), BF)
    plain = jax.ShapeDtypeStruct((32, 16, 128), BF)
    twice = jax.ShapeDtypeStruct((64, 16, 128), BF)
    pairs = [[32 * group + strip for group in pair for strip in range(32)] for pair in ((0, 1), (2, 3))]
    leaving, h = call(
        first_kernel, (wide, jax.ShapeDtypeStruct((8, N), F32)),
        launch, shared, twiddle, table, send, name="rows0",
    )
    carried = exchanged(leaving)

    def columns(layer, came, shape, name):
        def kernel(*refs):
            column_kernel(layer, *refs)

        return call(kernel, shape, came, carried, h, twiddle, table, back, send, name=name)

    def rows(layer, came, name):
        def kernel(*refs):
            row_kernel(layer, *refs)

        return call(kernel, plain, came, shared, h, twiddle, table, back, send, name=name)

    came = exchanged(columns(0, carried, plain, "columns01"))
    came = exchanged(rows(1, came, "rows12"))
    came = exchanged(columns(2, came, twice, "columns23"), ("layer", "strip"), pairs)

    spots = jnp.asarray(spot_table())
    pupil, result = call(
        last_kernel,
        (jax.ShapeDtypeStruct(launch.shape, BF), jax.ShapeDtypeStruct((32, 32), F32)),
        came, h, twiddle, table, back, tables["sub"], spots, templates.T, picks,
        in_specs=[VMEM] * 9,
        out_specs=(FAR, VMEM),
        scratch_shapes=[
            pltpu.VMEM((512, 256), BF),
            pltpu.VMEM(launch.shape, BF),
            pltpu.SemaphoreType.DMA,
        ],
        name="rows3",
    )
    return (pupil, exchanged(result).reshape(1, 32, 1, 2, 16))


def solution(mesh):
    placed = (
        P(None, None, "strip", None),
        P("layer", "strip", None),
        P("layer"),
        P(),
        P("strip", None, "layer"),
        P("strip", None),
    )
    return jax.shard_map(
        per_device,
        mesh=mesh,
        in_specs=placed,
        out_specs=(P(None, None, "strip", None), P("strip", None, "layer", None, None)),
        check_vma=False,
    )
```
